256 devices in a mesh: row: 64 (over y, x, z_hi, core), grp: 4 (over z_lo).
Axes of the slice: x: 4, y: 4, z: 8 (z_hi: 2, z_lo: 4; z = z_hi * 4 + z_lo), core: 2. Of those that a mesh axis runs over, the one named last changes fastest.
Arguments:
- positions: float32 [3, 8192], replicated, may hold values from -0.05 to 9.35, as said below
- detuning: float32 [8192], replicated, may hold values from -1 to 1
- populations: float32 [8192], P('row'), may hold values from 0 to 1
- base: float32 [2, 64, 8192], P(None, 'grp', 'row'), may hold values from -6 to 6
- section: float32 [2, 64, 8192], P(None, 'grp', 'row'), may hold values from -6 to 6
- accum: float32 [2, 64, 8192], P(None, 'grp', 'row'), may hold values from -3 to 3
Outputs:
- next_input: float32 [2, 64, 8192], P(None, 'grp', 'row')
- accum_out: float32 [2, 64, 8192], P(None, 'grp', 'row')
The draws below stay inside these ranges and needn't reach their ends.
Inputs may be any that keep to these rules, and one draw needn't show every extreme that they name: `positions`: emitter n sits near the lattice point 0.3 * (n % 32, (n // 32) % 32, n // 1024), displaced by at most 0.05 in each coordinate.
All inputs are finite; a program needn't handle non-finite values.
Results may differ from the reference program's by a relative error of at most 0.0003.
Values sent between devices are 32-bit elements; how exact they have to be, the bound alone decides.
No kernel may reach another device: no remote copies, remote signals or barrier semaphores. Data moves between devices by JAX's collectives and lax.ppermute only.
A program may use at most 64 MiB of HBM per device.

```python
import math
import jax
import jax.numpy as jnp
from jax import lax

S = 64
N = 8192


def draw_positions(key, part):
    index = jnp.arange(N, dtype=jnp.int32)
    lattice = jnp.stack([index % 32, index // 32 % 32, index // 1024]).astype(jnp.float32) * 0.3
    jitter = jax.random.uniform(key, (3, N), jnp.float32, -0.05, 0.05)
    return lattice + jitter


def levels(own_key, extent, shards, low, high):
    def one(dim, shards_of):
        steps = jax.random.uniform(jax.random.fold_in(jax.random.fold_in(own_key, 6), dim), (shards_of,), jnp.float32, low / len(shards), high / len(shards))
        return jnp.repeat(jnp.exp(steps), extent[dim] // shards_of).reshape((-1,) + (1,) * (len(extent) - dim - 1))

    loudness = one(*shards[0])
    for cut in shards[1:]:
        loudness = loudness * one(*cut)
    return loudness


def centred(own_key, shape, spread, bound, cuts=(), held_as=jnp.bfloat16):
    array = jax.random.normal(own_key, shape, jnp.float32) * spread
    if len(cuts) > 0:
        array = levels(own_key, shape, cuts, -0.22, 0.18) * array
    return jnp.clip(array, min=-bound, max=bound).astype(held_as)


def setup_inputs(seed: int = 0) -> dict:
    seeds = jax.random.split(jax.random.key(seed), 7)
    positions = draw_positions(jax.random.fold_in(seeds[6], 71), 0)
    detuning = jnp.clip(jax.random.uniform(seeds[1], (N,), jnp.float32, -1.0, 1.0), -1.0, 1.0)
    populations = jnp.clip(1.0 * jax.random.uniform(seeds[2], (N,), jnp.float32) ** levels(seeds[2], (N,), ((0, 64),), -0.2, 0.2), 0.0, 1.0)
    base = centred(seeds[3], (2, S, N), 1.0, 6.0, ((1, 4), (2, 64)), jnp.float32)
    section = centred(seeds[4], (2, S, N), 1.0, 6.0, ((1, 4), (2, 64)), jnp.float32)
    accum = centred(seeds[5], (2, S, N), 0.5, 3.0, ((1, 4), (2, 64)), jnp.float32)
    return {"positions": positions, "detuning": detuning, "populations": populations, "base": base, "section": section, "accum": accum}


WAVE_NUMBER = 2.0 * math.pi
TIME_STEP = 0.2

def coupling(pos_rows, pos_cols, row_ids, col_ids):
    offsets = pos_rows[:, :, None] - pos_cols[:, None, :]
    dist_sq = lax.optimization_barrier(jnp.sum(offsets * offsets, axis=0))
    on_diag = row_ids[:, None] == col_ids[None, :]
    safe_sq = jnp.where(on_diag, 1.0, dist_sq)
    phase = WAVE_NUMBER * jnp.sqrt(safe_sq)
    inverse = 1.0 / phase
    inverse_sq = inverse * inverse
    aligned = offsets[2] * offsets[2] / safe_sq
    quad_real = 1.0 - inverse_sq - aligned * (1.0 - 3.0 * inverse_sq)
    quad_imag = inverse - 3.0 * aligned * inverse
    cosine = jnp.cos(phase)
    sine = jnp.sin(phase)
    h_real = -0.75 * inverse * (cosine * quad_real - sine * quad_imag)
    h_imag = -0.75 * inverse * (sine * quad_real + cosine * quad_imag)
    return (jnp.where(on_diag, 0.0, h_real), jnp.where(on_diag, 0.0, h_imag))

def cross_rows(slab_part, tile):
    return lax.dot_general(slab_part, tile, (((1,), (1,)), ((), ())), precision=lax.Precision.HIGHEST, preferred_element_type=jnp.float32)

def lead_rows(tile, slab_part):
    return lax.dot_general(tile, slab_part, (((0,), (0,)), ((), ())), precision=lax.Precision.HIGHEST, preferred_element_type=jnp.float32)

def slab_rate(z_real, z_imag, shift, local_slab, full_slab, local_det, slab_pos, slab_det, col_start, col_count):
    slab_ids = lax.iota(jnp.int32, slab_pos.shape[1])
    w_real, w_imag = coupling(slab_pos, slab_pos, slab_ids, slab_ids)
    eye_mask = slab_ids[:, None] == slab_ids[None, :]
    w_real = w_real + jnp.where(eye_mask, slab_det[:, None], 0.0)
    w_imag = w_imag + jnp.where(eye_mask, -0.5, 0.0)
    w_real = lax.dynamic_slice_in_dim(w_real, col_start, col_count, 1)
    w_imag = lax.dynamic_slice_in_dim(w_imag, col_start, col_count, 1)
    v_real = lead_rows(w_real, full_slab[0]) + lead_rows(w_imag, full_slab[1])
    v_imag = lead_rows(w_real, full_slab[1]) - lead_rows(w_imag, full_slab[0])
    y_real = local_slab[0]
    y_imag = local_slab[1]
    z_real = z_real + local_det * y_real + 0.5 * y_imag
    z_imag = z_imag + local_det * y_imag - 0.5 * y_real
    f_real = z_imag + shift * y_imag - v_imag
    f_imag = -z_real - shift * y_real + v_real
    return jnp.stack([f_real, f_imag])

def reference(positions, detuning, populations, base, section, accum):
    block_len = math.gcd(N, 512)
    block_total = N // block_len
    signed_pops = 2.0 * populations - 1.0
    all_ids = lax.iota(jnp.int32, N)

    def one_block(row_start):
        pos_rows = lax.dynamic_slice_in_dim(positions, row_start, block_len, 1)
        row_ids = row_start + lax.iota(jnp.int32, block_len)
        h_real, h_imag = coupling(pos_rows, positions, row_ids, all_ids)
        z_real = cross_rows(section[0], h_real) - cross_rows(section[1], h_imag)
        z_imag = cross_rows(section[0], h_imag) + cross_rows(section[1], h_real)
        shift = jnp.dot(h_real, signed_pops, precision=lax.Precision.HIGHEST)
        return (z_real, z_imag, shift)
    starts = (jnp.arange(block_total) * block_len).astype(jnp.int32)
    z_real, z_imag, shift = lax.map(one_block, starts)
    z_real = jnp.transpose(z_real, (1, 0, 2)).reshape(S, N)
    z_imag = jnp.transpose(z_imag, (1, 0, 2)).reshape(S, N)
    shift = shift.reshape(N)
    rate = slab_rate(z_real, z_imag, shift, section, section, detuning, positions[:, :S], detuning[:S], 0, S)
    return (base + 0.5 * TIME_STEP * rate, accum + TIME_STEP / 3.0 * rate)
```

```python
import math

import jax
import jax.numpy as jnp
from jax import lax
from jax.experimental import pallas as pl
from jax.experimental.pallas import tpu as pltpu
from jax.sharding import Mesh
from jax.sharding import PartitionSpec as P

TIME_STEP = 0.2
LANES = 128
COS = (0.9999999892, -19.73920453, 64.93911891, -85.45016433, 60.16782231, -25.96827976, 6.529565646)
SIN = (6.283182817, -41.3414213, 81.59618177, -76.58008122, 41.20531753, -12.27114973)
SCALE = -0.75 / (2.0 * math.pi)
INV_WAVE = 1.0 / (2.0 * math.pi)
ROUNDER = 12582912.0
PART = 40
WIDE = 48


def horner(coefs, scale, arg):
    total = jnp.float32(coefs[-1] * scale)
    for c in coefs[-2::-1]:
        total = total * arg + jnp.float32(c * scale)
    return total


def coupling(dx, dy, dz):
    dz_sq = dz * dz
    dist_sq = dx * dx + dy * dy + dz_sq
    inv = lax.rsqrt(dist_sq)
    dist = dist_sq * inv
    turn = dist - ((dist + ROUNDER) - ROUNDER)
    turn_sq = turn * turn
    cosine = horner(COS, SCALE, turn_sq) * inv
    sine = horner(SIN, SCALE, turn_sq) * turn * inv
    aligned = dz_sq * (inv * inv)
    quad_imag = inv * (INV_WAVE - (3.0 * INV_WAVE) * aligned)
    quad_real = (1.0 - aligned) - (INV_WAVE * inv) * quad_imag
    return cosine * quad_real - sine * quad_imag, sine * quad_real + cosine * quad_imag


def split(value):
    high = value.astype(jnp.bfloat16)
    low = (value - high.astype(jnp.float32)).astype(jnp.bfloat16)
    return high, low


def own_quad():
    return lax.axis_index("zh") * 2 + lax.axis_index("c")


def lanes_at(index):
    return pl.ds(pl.multiple_of(index * LANES, LANES), LANES)


def coupling_kernel(pos_ref, det_ref, high_ref, low_ref, w_ref, row_ref):
    quad = own_quad()
    place = lax.axis_index("yx")
    tiles = pos_ref.shape[1] // (4 * LANES)

    def turned(k, index):
        line = pos_ref[k : k + 1, lanes_at(index)]
        return jnp.broadcast_to(line, (LANES, LANES)).T

    for b in range(4):
        for k in range(3):
            row_ref[k, b * LANES : (b + 1) * LANES, :] = turned(k, place * 4 + b)

    def tile(step, carry):
        at = lanes_at(step * 4 + quad)
        cols = [pos_ref[k : k + 1, at] for k in range(3)]

        def strip(n, carry):
            rows = pl.ds(pl.multiple_of(n * 32, 32), 32)
            dx, dy, dz = [row_ref[k, rows, :] - cols[k] for k in range(3)]
            for part, value in enumerate(coupling(dx, dy, dz)):
                high, low = split(value)
                lanes = lanes_at(step + part * tiles)
                high_ref[rows, lanes] = high
                low_ref[rows, lanes] = low
            return carry

        return lax.fori_loop(0, 16, strip, carry, unroll=2)

    lax.fori_loop(0, tiles, tile, 0)
    rows = pl.ds(pl.multiple_of(quad * LANES, LANES), LANES)
    eye = lax.broadcasted_iota(jnp.int32, (LANES, LANES), 0) == lax.broadcasted_iota(jnp.int32, (LANES, LANES), 1)
    for part in range(2):
        lanes = lanes_at(place + part * tiles)
        for ref in (high_ref, low_ref):
            ref[rows, lanes] = jnp.where(eye, 0.0, ref[rows, lanes].astype(jnp.float32)).astype(jnp.bfloat16)

    start = pl.multiple_of(lax.axis_index("zl") * 16, 16)
    offsets = []
    for k in range(3):
        row_ref[k, 0:LANES, :] = turned(k, 0)
        offsets.append(row_ref[k, pl.ds(start, 16), :] - pos_ref[k : k + 1, 0:LANES])
    w_real, w_imag = coupling(*offsets)
    eye = (lax.broadcasted_iota(jnp.int32, (16, LANES), 0) + start) == lax.broadcasted_iota(jnp.int32, (16, LANES), 1)
    w_ref[0:16, :] = jnp.where(eye, det_ref[:, 0:LANES], w_real)
    w_ref[16:32, :] = jnp.where(eye, -0.5, w_imag)


def product_kernel(high_ref, low_ref, block_ref, out_ref, y_ref):
    tiles = block_ref.shape[0]
    zeros = jnp.zeros((16, LANES), jnp.float32)

    def fill(step, carry):
        block = block_ref[step]
        pops = jnp.concatenate([block[32:40], zeros[0:8]], axis=0)
        first, second = block[0:16], block[16:32]
        for n, value in enumerate((first, second, pops)):
            high, low = split(value)
            y_ref[n * 16 : n * 16 + 16, lanes_at(step)] = high
            y_ref[WIDE + n * 16 : WIDE + n * 16 + 16, lanes_at(step)] = low
        for n, value in enumerate((-second, first, zeros)):
            high, low = split(value)
            y_ref[n * 16 : n * 16 + 16, lanes_at(step + tiles)] = high
            y_ref[WIDE + n * 16 : WIDE + n * 16 + 16, lanes_at(step + tiles)] = low
        y_ref[2 * WIDE :, lanes_at(step)] = jnp.zeros((LANES - 2 * WIDE, LANES), jnp.bfloat16)
        y_ref[2 * WIDE :, lanes_at(step + tiles)] = jnp.zeros((LANES - 2 * WIDE, LANES), jnp.bfloat16)
        return carry

    lax.fori_loop(0, tiles, fill, 0)
    dims = (((1,), (1,)), ((), ()))
    total = lax.dot_general(high_ref[...], y_ref[...], dims, preferred_element_type=jnp.float32)
    total += lax.dot_general(low_ref[...], y_ref[...], dims, preferred_element_type=jnp.float32)
    for b in range(4):
        flat = total[b * LANES : (b + 1) * LANES, :].T
        out_ref[b] = flat[0:PART] + flat[WIDE : WIDE + PART]


def finish_kernel(z_ref, add_ref, w_ref, slab0, slab1, slab2, slab3, base_ref, accum_ref, det_ref, next_ref, acc_ref, y_ref):
    own = lax.axis_index("zl")
    for n, ref in enumerate((slab0, slab1, slab2, slab3)):
        start = pl.multiple_of(lax.rem(own + 4 - n, 4) * 16, 16)
        y_ref[0, pl.ds(start, 16), :] = ref[0]
        y_ref[1, pl.ds(start, 16), :] = ref[1]

    def mul(a, b):
        return jnp.dot(a, b, precision=lax.Precision.HIGHEST, preferred_element_type=jnp.float32)

    w_real, w_imag = w_ref[0:16, 0:64], w_ref[16:32, 0:64]
    v_real = mul(w_real, y_ref[0]) + mul(w_imag, y_ref[1])
    v_imag = mul(w_real, y_ref[1]) - mul(w_imag, y_ref[0])
    z_real = z_ref[0:16] + add_ref[0:16]
    z_imag = z_ref[16:32] + add_ref[16:32]
    shift = z_ref[32:33] + add_ref[32:33]
    y_real, y_imag = slab0[0], slab0[1]
    line = det_ref[:, lanes_at(lax.axis_index("yx") * 4 + own_quad())]
    z_real = z_real + line * y_real + 0.5 * y_imag
    z_imag = z_imag + line * y_imag - 0.5 * y_real
    rate_real = z_imag + shift * y_imag - v_imag
    rate_imag = v_real - z_real - shift * y_real
    for n, rate in enumerate((rate_real, rate_imag)):
        next_ref[n] = base_ref[n] + (0.5 * TIME_STEP) * rate
        acc_ref[n] = accum_ref[n] + (TIME_STEP / 3.0) * rate


def params(mib):
    return pltpu.CompilerParams(vmem_limit_bytes=mib << 20)


def local(positions, detuning, populations, base, section, accum):
    bf16, f32 = jnp.bfloat16, jnp.float32
    count = positions.shape[1]
    tiles = count // (4 * LANES)
    det = detuning.reshape(1, count)
    pops = (2.0 * populations - 1.0).reshape(1, LANES)
    block = jnp.concatenate([section.reshape(32, LANES), pops, jnp.zeros((PART - 33, LANES), f32)], axis=0)
    copies = jnp.broadcast_to(block[None], (tiles, PART, LANES))
    blocks = lax.all_to_all(copies, "yx", 0, 0, tiled=True)
    slabs = [section] + [lax.ppermute(section, "zl", [(i, (i + d) % 4) for i in range(4)]) for d in (1, 2, 3)]

    high, low, w = pl.pallas_call(
        coupling_kernel,
        out_shape=(
            jax.ShapeDtypeStruct((4 * LANES, 2 * tiles * LANES), bf16),
            jax.ShapeDtypeStruct((4 * LANES, 2 * tiles * LANES), bf16),
            jax.ShapeDtypeStruct((32, LANES), f32),
        ),
        in_specs=[pl.BlockSpec(memory_space=pltpu.VMEM), pl.BlockSpec(memory_space=pltpu.VMEM)],
        out_specs=[pl.BlockSpec(memory_space=pltpu.VMEM)] * 3,
        scratch_shapes=[pltpu.VMEM((3, 4 * LANES, LANES), f32)],
        compiler_params=params(24),
        cost_estimate=pl.CostEstimate(flops=60 << 20, bytes_accessed=8 << 20, transcendentals=1 << 20),
        name="coupling_tiles",
    )(positions, det)

    partial = pl.pallas_call(
        product_kernel,
        out_shape=jax.ShapeDtypeStruct((4, PART, LANES), f32),
        scratch_shapes=[pltpu.VMEM((LANES, 2 * tiles * LANES), bf16)],
        compiler_params=params(24),
        cost_estimate=pl.CostEstimate(flops=1 << 30, bytes_accessed=8 << 20, transcendentals=0),
        name="tile_products",
    )(high, low, blocks)

    mine = lax.axis_index("zh")
    other_half = lax.dynamic_slice_in_dim(partial, (1 - mine) * 2, 2, 0)
    own_half = lax.dynamic_slice_in_dim(partial, mine * 2, 2, 0)
    own_half = own_half + lax.ppermute(other_half, "zh", [(0, 1), (1, 0)])
    core = lax.axis_index("c")
    other = lax.dynamic_slice_in_dim(own_half, 1 - core, 1, 0)[0]
    own = lax.dynamic_slice_in_dim(own_half, core, 1, 0)[0]
    added = lax.ppermute(other, "c", [(0, 1), (1, 0)])

    return pl.pallas_call(
        finish_kernel,
        out_shape=(jax.ShapeDtypeStruct(base.shape, f32),) * 2,
        scratch_shapes=[pltpu.VMEM((2, 64, LANES), f32)],
        compiler_params=params(8),
        cost_estimate=pl.CostEstimate(flops=4 << 20, bytes_accessed=1 << 18, transcendentals=0),
        name="finish_rate",
    )(own, added, w, *slabs, base, accum, det)


def solution(mesh):
    fine = Mesh(mesh.devices.reshape(16, 2, 2, 4), ("yx", "zh", "c", "zl"))
    rows = ("yx", "zh", "c")
    slab = P(None, "zl", rows)
    return jax.shard_map(
        local,
        mesh=fine,
        in_specs=(P(), P(), P(rows), slab, slab, slab),
        out_specs=(slab, slab),
        check_vma=False,
    )
```

```python
import math

import jax
import jax.numpy as jnp
from jax import lax
from jax.experimental import pallas as pl
from jax.experimental.pallas import tpu as pltpu
from jax.sharding import Mesh
from jax.sharding import PartitionSpec as P

TIME_STEP = 0.2
LANES = 128
COS = (0.9999999892, -19.73920453, 64.93911891, -85.45016433, 60.16782231, -25.96827976, 6.529565646)
SIN = (6.283182817, -41.3414213, 81.59618177, -76.58008122, 41.20531753, -12.27114973)
SCALE = -0.75 / (2.0 * math.pi)
INV_WAVE = 1.0 / (2.0 * math.pi)
ROUNDER = 12582912.0
PART = 40
WIDE = 48


def horner(coefs, scale, arg):
    total = jnp.float32(coefs[-1] * scale)
    for c in coefs[-2::-1]:
        total = total * arg + jnp.float32(c * scale)
    return total


def coupling(dx, dy, dz):
    dz_sq = dz * dz
    dist_sq = dx * dx + dy * dy + dz_sq
    inv = lax.rsqrt(dist_sq)
    dist = dist_sq * inv
    turn = dist - ((dist + ROUNDER) - ROUNDER)
    turn_sq = turn * turn
    cosine = horner(COS, SCALE, turn_sq) * inv
    sine = horner(SIN, SCALE, turn_sq) * turn * inv
    aligned = dz_sq * (inv * inv)
    quad_imag = inv * (INV_WAVE - (3.0 * INV_WAVE) * aligned)
    quad_real = (1.0 - aligned) - (INV_WAVE * inv) * quad_imag
    return cosine * quad_real - sine * quad_imag, sine * quad_real + cosine * quad_imag


def split(value):
    high = value.astype(jnp.bfloat16)
    low = (value - high.astype(jnp.float32)).astype(jnp.bfloat16)
    return high, low


def lanes_at(index):
    return pl.ds(pl.multiple_of(index * LANES, LANES), LANES)


def pack_kernel(section_ref, pops_ref, pos_ref, det_ref, copies_ref, pos_out, det_out, block_ref, sems):
    own = lax.axis_index("yx") * 4 + lax.axis_index("zh") * 2 + lax.axis_index("c")
    moves = [
        pltpu.make_async_copy(section_ref.at[0], block_ref.at[pl.ds(0, 16)], sems.at[0]),
        pltpu.make_async_copy(section_ref.at[1], block_ref.at[pl.ds(16, 16)], sems.at[1]),
        pltpu.make_async_copy(pops_ref, block_ref.at[pl.ds(32, 1)], sems.at[2]),
        pltpu.make_async_copy(pos_ref, pos_out, sems.at[3]),
        pltpu.make_async_copy(det_ref.at[:, lanes_at(own)], det_out.at[pl.ds(0, 1)], sems.at[4]),
        pltpu.make_async_copy(det_ref.at[:, pl.ds(0, LANES)], det_out.at[pl.ds(1, 1)], sems.at[5]),
    ]
    for move in moves:
        move.start()
    for move in moves[:3]:
        move.wait()
    block = block_ref[0:32, :]
    top = lax.broadcasted_iota(jnp.int32, (8, LANES), 0) == 0
    pops = jnp.where(top, 2.0 * block_ref[32:40, :] - 1.0, 0.0)
    for n in range(copies_ref.shape[0]):
        copies_ref[n, 0:32, :] = block
        copies_ref[n, 32:40, :] = pops
    for move in moves[3:]:
        move.wait()


def turned(pos_ref, k, index):
    line = pos_ref[k : k + 1, lanes_at(index)]
    return jnp.broadcast_to(line, (LANES, LANES)).T


def fill_tiles(pos_ref, row_ref, high_ref, low_ref, quads, unroll, after=None):
    quad = lax.axis_index("zh") * 2 + lax.axis_index("c")
    place = lax.axis_index("yx")
    for n, other in enumerate(quads):
        for k in range(3):
            row_ref[k, n * LANES : (n + 1) * LANES, :] = turned(pos_ref, k, place * 4 + other)

    def tile(step, carry):
        at = lanes_at(step * 4 + quad)
        cols = [pos_ref[k : k + 1, at] for k in range(3)]

        def strip(n, carry):
            rows = pl.ds(pl.multiple_of(n * 32, 32), 32)
            dx, dy, dz = [row_ref[k, rows, :] - cols[k] for k in range(3)]
            for part, value in enumerate(coupling(dx, dy, dz)):
                high, low = split(value)
                lanes = lanes_at(step * 2 + part)
                high_ref[rows, lanes] = high
                low_ref[rows, lanes] = low
            return carry

        lax.fori_loop(0, 4 * len(quads), strip, carry, unroll=unroll)
        if after is not None:
            after(step)
        return carry

    lax.fori_loop(0, pos_ref.shape[1] // (4 * LANES), tile, 0)


def far_kernel(pos_ref, near_ref, low_ref, last_ref, row_ref, high_all, low_all, sems):
    half, core = lax.axis_index("zh"), lax.axis_index("c")
    quads = ((1 - half) * 2 + 1 - core, (1 - half) * 2 + core, half * 2 + 1 - core)
    send = 2 * LANES

    def moves(step):
        lanes = pl.ds(pl.multiple_of(step * 2 * LANES, 2 * LANES), 2 * LANES)
        return (
            pltpu.make_async_copy(high_all.at[pl.ds(0, send), lanes], near_ref.at[:, lanes], sems.at[step, 0]),
            pltpu.make_async_copy(low_all.at[pl.ds(0, send), lanes], low_ref.at[:, lanes], sems.at[step, 1]),
            pltpu.make_async_copy(high_all.at[pl.ds(send, LANES), lanes], last_ref.at[0, :, lanes], sems.at[step, 2]),
            pltpu.make_async_copy(low_all.at[pl.ds(send, LANES), lanes], last_ref.at[1, :, lanes], sems.at[step, 3]),
        )

    def start(step):
        for move in moves(step):
            move.start()

    fill_tiles(pos_ref, row_ref, high_all, low_all, quads, 6, start)

    def finish(step, carry):
        for move in moves(step):
            move.wait()
        return carry

    lax.fori_loop(0, pos_ref.shape[1] // (4 * LANES), finish, 0)


def fill_slab(block_ref, y_ref):
    tiles = block_ref.shape[0]
    zeros = jnp.zeros((16, LANES), jnp.float32)

    def fill(step, carry):
        block = block_ref[step]
        pops = jnp.concatenate([block[32:40], zeros[0:8]], axis=0)
        first, second = block[0:16], block[16:32]
        for part, rows in enumerate(((first, second, pops), (-second, first, zeros))):
            lanes = lanes_at(step * 2 + part)
            for n, value in enumerate(rows):
                high, low = split(value)
                y_ref[n * 16 : n * 16 + 16, lanes] = high
                y_ref[WIDE + n * 16 : WIDE + n * 16 + 16, lanes] = low
            y_ref[2 * WIDE :, lanes] = jnp.zeros((LANES - 2 * WIDE, LANES), jnp.bfloat16)
        return carry

    lax.fori_loop(0, tiles, fill, 0, unroll=4)


def store_products(total, out_ref, at):
    for n in range(total.shape[0] // LANES):
        flat = total[n * LANES : (n + 1) * LANES, :].T
        out_ref[at + n] = flat[0:PART] + flat[WIDE : WIDE + PART]


def send_kernel(near_ref, low_ref, block_ref, out_ref, y_ref, low, sem):
    move = pltpu.make_async_copy(low_ref, low, sem)
    move.start()
    fill_slab(block_ref, y_ref)
    dims = (((1,), (1,)), ((), ()))
    total = lax.dot_general(near_ref[...], y_ref[...], dims, preferred_element_type=jnp.float32)
    move.wait()
    total += lax.dot_general(low[...], y_ref[...], dims, preferred_element_type=jnp.float32)
    store_products(total, out_ref, 0)


def keep_kernel(pos_ref, last_ref, y_ref, slab0, slab1, slab2, slab3, det_ref, out_ref, rest_ref, row_ref, high_ref, low_ref, full_ref, last, sem):
    move = pltpu.make_async_copy(last_ref, last, sem)
    move.start()
    own, place = lax.axis_index("zl"), lax.axis_index("yx")
    quad = lax.axis_index("zh") * 2 + lax.axis_index("c")
    fill_tiles(pos_ref, row_ref, high_ref, low_ref, (quad,), 4)
    eye = lax.broadcasted_iota(jnp.int32, (LANES, LANES), 0) == lax.broadcasted_iota(jnp.int32, (LANES, LANES), 1)
    for part in range(2):
        lanes = lanes_at(place * 2 + part)
        for ref in (high_ref, low_ref):
            ref[:, lanes] = jnp.where(eye, 0.0, ref[:, lanes].astype(jnp.float32)).astype(jnp.bfloat16)
    move.wait()
    dims = (((1,), (1,)), ((), ()))
    for n, (high, low) in enumerate(((last[0], last[1]), (high_ref[...], low_ref[...]))):
        total = lax.dot_general(high, y_ref[...], dims, preferred_element_type=jnp.float32)
        total += lax.dot_general(low, y_ref[...], dims, preferred_element_type=jnp.float32)
        store_products(total, out_ref, n)

    start = pl.multiple_of(own * 16, 16)
    offsets = []
    for k in range(3):
        row_ref[k] = turned(pos_ref, k, 0)
        offsets.append(row_ref[k, pl.ds(start, 16), :] - pos_ref[k : k + 1, 0:LANES])
    w_real, w_imag = coupling(*offsets)
    eye = (lax.broadcasted_iota(jnp.int32, (16, LANES), 0) + start) == lax.broadcasted_iota(jnp.int32, (16, LANES), 1)
    w_real = jnp.where(eye, det_ref[1:2, :], w_real)[:, 0:64]
    w_imag = jnp.where(eye, -0.5, w_imag)[:, 0:64]
    for n, ref in enumerate((slab0, slab1, slab2, slab3)):
        there = pl.ds(pl.multiple_of(lax.rem(own + 4 - n, 4) * 16, 16), 16)
        full_ref[0, there, :] = ref[0]
        full_ref[1, there, :] = ref[1]

    def mul(a, b):
        return jnp.dot(a, b, precision=lax.Precision.HIGHEST, preferred_element_type=jnp.float32)

    v_real = mul(w_real, full_ref[0]) + mul(w_imag, full_ref[1])
    v_imag = mul(w_real, full_ref[1]) - mul(w_imag, full_ref[0])
    y_real, y_imag = slab0[0], slab0[1]
    line = det_ref[0:1, :]
    rest_ref[0] = line * y_imag - 0.5 * y_real - v_imag
    rest_ref[1] = v_real - line * y_real - 0.5 * y_imag


def finish_kernel(keep_ref, half_ref, core_ref, rest_ref, slab_ref, base_ref, accum_ref, next_ref, acc_ref):
    z = keep_ref[1] + half_ref[1] + core_ref[...]
    shift = z[32:33]
    rate_real = z[16:32] + shift * slab_ref[1] + rest_ref[0]
    rate_imag = rest_ref[1] - z[0:16] - shift * slab_ref[0]
    for n, rate in enumerate((rate_real, rate_imag)):
        next_ref[n] = base_ref[n] + (0.5 * TIME_STEP) * rate
        acc_ref[n] = accum_ref[n] + (TIME_STEP / 3.0) * rate


def params(mib):
    return pltpu.CompilerParams(vmem_limit_bytes=mib << 20)


def in_hbm(array):
    return pltpu.with_memory_space_constraint(array, pltpu.HBM)


def local(positions, detuning, populations, base, section, accum):
    bf16, f32 = jnp.bfloat16, jnp.float32
    count = positions.shape[1]
    tiles = count // (4 * LANES)
    deep = 2 * tiles * LANES
    hbm, vmem = pl.BlockSpec(memory_space=pltpu.HBM), pl.BlockSpec(memory_space=pltpu.VMEM)

    copies, pos, det = pl.pallas_call(
        pack_kernel,
        out_shape=(
            jax.ShapeDtypeStruct((tiles, PART, LANES), f32),
            pltpu.VMEM(positions.shape, f32),
            pltpu.VMEM((8, LANES), f32),
        ),
        in_specs=[hbm] * 4,
        out_specs=[vmem] * 3,
        scratch_shapes=[pltpu.VMEM((PART, LANES), f32), pltpu.SemaphoreType.DMA((6,))],
        compiler_params=params(4),
        cost_estimate=pl.CostEstimate(flops=1 << 16, bytes_accessed=1 << 19, transcendentals=0),
        name="pack_block",
    )(in_hbm(section), in_hbm(populations.reshape(1, LANES)), in_hbm(positions), in_hbm(detuning.reshape(1, count)))
    blocks = lax.all_to_all(copies, "yx", 0, 0, tiled=True)
    slabs = [section] + [lax.ppermute(section, "zl", [(i, (i + d) % 4) for i in range(4)]) for d in (1, 2, 3)]

    near, low, last = pl.pallas_call(
        far_kernel,
        out_shape=(
            pltpu.VMEM((2 * LANES, deep), bf16),
            pltpu.HBM((2 * LANES, deep), bf16),
            pltpu.HBM((2, LANES, deep), bf16),
        ),
        in_specs=[vmem],
        out_specs=[vmem, hbm, hbm],
        scratch_shapes=[
            pltpu.VMEM((3, 3 * LANES, LANES), f32),
            pltpu.VMEM((3 * LANES, deep), bf16),
            pltpu.VMEM((3 * LANES, deep), bf16),
            pltpu.SemaphoreType.DMA((tiles, 4)),
        ],
        compiler_params=params(12),
        cost_estimate=pl.CostEstimate(flops=45 << 20, bytes_accessed=6 << 20, transcendentals=1 << 20),
        name="far_tiles",
    )(pos)

    sent, y = pl.pallas_call(
        send_kernel,
        out_shape=(pltpu.VMEM((2, PART, LANES), f32), pltpu.VMEM((LANES, deep), bf16)),
        in_specs=[vmem, hbm, vmem],
        out_specs=[vmem] * 2,
        scratch_shapes=[pltpu.VMEM((2 * LANES, deep), bf16), pltpu.SemaphoreType.DMA],
        compiler_params=params(8),
        cost_estimate=pl.CostEstimate(flops=1 << 29, bytes_accessed=4 << 20, transcendentals=0),
        name="send_products",
    )(near, in_hbm(low), blocks)
    half = lax.ppermute(sent, "zh", [(0, 1), (1, 0)])

    keep, rest = pl.pallas_call(
        keep_kernel,
        out_shape=(pltpu.VMEM((2, PART, LANES), f32), pltpu.VMEM((2, 16, LANES), f32)),
        in_specs=[vmem, hbm] + [vmem] * 6,
        out_specs=[vmem] * 2,
        scratch_shapes=[
            pltpu.VMEM((3, LANES, LANES), f32),
            pltpu.VMEM((LANES, deep), bf16),
            pltpu.VMEM((LANES, deep), bf16),
            pltpu.VMEM((2, 64, LANES), f32),
            pltpu.VMEM((2, LANES, deep), bf16),
            pltpu.SemaphoreType.DMA,
        ],
        compiler_params=params(8),
        cost_estimate=pl.CostEstimate(flops=1 << 29, bytes_accessed=4 << 20, transcendentals=1 << 20),
        name="keep_products",
    )(pos, in_hbm(last), y, *slabs, det)
    core = lax.ppermute(keep[0] + half[0], "c", [(0, 1), (1, 0)])

    return pl.pallas_call(
        finish_kernel,
        out_shape=(jax.ShapeDtypeStruct(base.shape, f32),) * 2,
        compiler_params=params(4),
        cost_estimate=pl.CostEstimate(flops=1 << 16, bytes_accessed=1 << 18, transcendentals=0),
        name="finish_rate",
    )(keep, half, core, rest, section, base, accum)


def solution(mesh):
    fine = Mesh(mesh.devices.reshape(16, 2, 2, 4), ("yx", "zh", "c", "zl"))
    rows = ("yx", "zh", "c")
    slab = P(None, "zl", rows)
    return jax.shard_map(
        local,
        mesh=fine,
        in_specs=(P(), P(), P(rows), slab, slab, slab),
        out_specs=(slab, slab),
        check_vma=False,
    )
```

```python
import math

import jax
import jax.numpy as jnp
from jax import lax
from jax.experimental import pallas as pl
from jax.experimental.pallas import tpu as pltpu
from jax.sharding import Mesh
from jax.sharding import PartitionSpec as P

TIME_STEP = 0.2
LANES = 128
COS = (0.9999999892, -19.73920453, 64.93911891, -85.45016433, 60.16782231, -25.96827976, 6.529565646)
SIN = (6.283182817, -41.3414213, 81.59618177, -76.58008122, 41.20531753, -12.27114973)
SCALE = -0.75 / (2.0 * math.pi)
INV_WAVE = 1.0 / (2.0 * math.pi)
ROUNDER = 12582912.0
PART = 40
WIDE = 48
GROUPS = 2


def horner(coefs, scale, arg):
    total = jnp.float32(coefs[-1] * scale)
    for c in coefs[-2::-1]:
        total = total * arg + jnp.float32(c * scale)
    return total


def coupling(dx, dy, dz):
    dz_sq = dz * dz
    dist_sq = dx * dx + dy * dy + dz_sq
    inv = lax.rsqrt(dist_sq)
    dist = dist_sq * inv
    turn = dist - ((dist + ROUNDER) - ROUNDER)
    turn_sq = turn * turn
    cosine = horner(COS, SCALE, turn_sq) * inv
    sine = horner(SIN, SCALE, turn_sq) * turn * inv
    aligned = dz_sq * (inv * inv)
    quad_imag = inv * (INV_WAVE - (3.0 * INV_WAVE) * aligned)
    quad_real = (1.0 - aligned) - (INV_WAVE * inv) * quad_imag
    return cosine * quad_real - sine * quad_imag, sine * quad_real + cosine * quad_imag


def split(value):
    high = value.astype(jnp.bfloat16)
    low = (value - high.astype(jnp.float32)).astype(jnp.bfloat16)
    return high, low


def lanes_at(index):
    return pl.ds(pl.multiple_of(index * LANES, LANES), LANES)


def pack_kernel(section_ref, pops_ref, pos_ref, det_ref, copies_ref, pos_out, det_out, block_ref, sems):
    own = lax.axis_index("yx") * 4 + lax.axis_index("zh") * 2 + lax.axis_index("c")
    moves = [
        pltpu.make_async_copy(section_ref.at[0], block_ref.at[pl.ds(0, 16)], sems.at[0]),
        pltpu.make_async_copy(section_ref.at[1], block_ref.at[pl.ds(16, 16)], sems.at[1]),
        pltpu.make_async_copy(pops_ref, block_ref.at[pl.ds(32, 1)], sems.at[2]),
        pltpu.make_async_copy(pos_ref, pos_out, sems.at[3]),
        pltpu.make_async_copy(det_ref.at[:, lanes_at(own)], det_out.at[pl.ds(0, 1)], sems.at[4]),
        pltpu.make_async_copy(det_ref.at[:, pl.ds(0, LANES)], det_out.at[pl.ds(1, 1)], sems.at[5]),
    ]
    for move in moves:
        move.start()
    for move in moves[:3]:
        move.wait()
    block = block_ref[0:32, :]
    top = lax.broadcasted_iota(jnp.int32, (8, LANES), 0) == 0
    pops = jnp.where(top, 2.0 * block_ref[32:40, :] - 1.0, 0.0)
    for n in range(copies_ref.shape[0]):
        copies_ref[n, 0:32, :] = block
        copies_ref[n, 32:40, :] = pops
    for move in moves[3:]:
        move.wait()


def turned(pos_ref, k, index):
    line = pos_ref[k : k + 1, lanes_at(index)]
    return jnp.broadcast_to(line, (LANES, LANES)).T


def fill_tiles(pos_ref, row_ref, high_ref, low_ref, quads, after=None):
    quad = lax.axis_index("zh") * 2 + lax.axis_index("c")
    place = lax.axis_index("yx")
    tiles = pos_ref.shape[1] // (4 * LANES)
    strips = 4 * len(quads)
    for n, other in enumerate(quads):
        for k in range(3):
            row_ref[k, n * LANES : (n + 1) * LANES, :] = turned(pos_ref, k, place * 4 + other)

    def tile(step, carry):
        at = lanes_at(step * 4 + quad)
        cols = [pos_ref[k : k + 1, at] for k in range(3)]

        def strip(n, carry):
            rows = pl.ds(pl.multiple_of(n * 32, 32), 32)
            dx, dy, dz = [row_ref[k, rows, :] - cols[k] for k in range(3)]
            for part, value in enumerate(coupling(dx, dy, dz)):
                high, low = split(value)
                lanes = lanes_at(step + part * tiles)
                high_ref[rows, lanes] = high
                low_ref[rows, lanes] = low
            return carry

        return lax.fori_loop(0, strips, strip, carry, unroll=strips)

    group = tiles // GROUPS
    for g in range(GROUPS):
        lax.fori_loop(g * group, (g + 1) * group, tile, 0)
        if after is not None:
            after(g)


def far_kernel(pos_ref, near_ref, low_ref, last_ref, row_ref, low_all, last_all, low_sems, last_sems):
    half, core = lax.axis_index("zh"), lax.axis_index("c")
    quad = half * 2 + core
    deep = near_ref.shape[1]
    wide = deep // 2 // GROUPS

    def moves(source, target, sems, g):
        for part in range(2):
            lanes = pl.ds(part * (deep // 2) + g * wide, wide)
            yield pltpu.make_async_copy(source.at[..., lanes], target.at[..., lanes], sems.at[g, part])

    def start_low(g):
        for move in moves(low_all, low_ref, low_sems, g):
            move.start()

    def start_last(g):
        for move in moves(last_all, last_ref, last_sems, g):
            move.start()

    fill_tiles(pos_ref, row_ref, near_ref, low_all, ((1 - half) * 2 + 1 - core, (1 - half) * 2 + core), start_low)
    fill_tiles(pos_ref, row_ref, last_all.at[0], last_all.at[1], (half * 2 + 1 - core,), start_last)
    for g in range(GROUPS):
        for move in moves(low_all, low_ref, low_sems, g):
            move.wait()
        for move in moves(last_all, last_ref, last_sems, g):
            move.wait()


def fill_slab(block_ref, y_ref):
    zeros = jnp.zeros((16, LANES), jnp.float32)

    def fill(step, carry):
        block = block_ref[step]
        pops = jnp.concatenate([block[32:40], zeros[0:8]], axis=0)
        lanes = lanes_at(step)
        for n, value in enumerate((block[0:16], block[16:32], pops)):
            high, low = split(value)
            y_ref[n * 16 : n * 16 + 16, lanes] = high
            y_ref[WIDE + n * 16 : WIDE + n * 16 + 16, lanes] = low
        y_ref[2 * WIDE :, lanes] = jnp.zeros((LANES - 2 * WIDE, LANES), jnp.bfloat16)
        return carry

    lax.fori_loop(0, block_ref.shape[0], fill, 0, unroll=4)


def dot_slab(tiles, y):
    return lax.dot_general(tiles, y, (((1,), (1,)), ((), ())), preferred_element_type=jnp.float32)


def store_products(by_real, by_imag, out_ref, at):
    for n in range(by_real.shape[0] // LANES):
        rows = slice(n * LANES, (n + 1) * LANES)
        real, imag = by_real[rows, :].T, by_imag[rows, :].T
        real = real[0:PART] + real[WIDE : WIDE + PART]
        imag = imag[0:32] + imag[WIDE : WIDE + 32]
        out_ref[at + n, 0:16, :] = real[0:16] - imag[16:32]
        out_ref[at + n, 16:32, :] = real[16:32] + imag[0:16]
        out_ref[at + n, 32:PART, :] = real[32:PART]


def send_kernel(near_ref, low_ref, block_ref, out_ref, y_ref, low, sem):
    move = pltpu.make_async_copy(low_ref, low, sem)
    move.start()
    fill_slab(block_ref, y_ref)
    half = near_ref.shape[1] // 2
    y = y_ref[...]
    by_real = dot_slab(near_ref[:, 0:half], y)
    by_imag = dot_slab(near_ref[:, half:], y)
    move.wait()
    by_real += dot_slab(low[:, 0:half], y)
    by_imag += dot_slab(low[:, half:], y)
    store_products(by_real, by_imag, out_ref, 0)


def keep_kernel(pos_ref, last_ref, y_ref, slab0, slab1, slab2, slab3, det_ref, out_ref, rest_ref, row_ref, high_ref, low_ref, full_ref, last, sem):
    move = pltpu.make_async_copy(last_ref, last, sem)
    move.start()
    own, place = lax.axis_index("zl"), lax.axis_index("yx")
    quad = lax.axis_index("zh") * 2 + lax.axis_index("c")
    tiles = pos_ref.shape[1] // (4 * LANES)
    half = tiles * LANES
    fill_tiles(pos_ref, row_ref, high_ref, low_ref, (quad,))
    eye = lax.broadcasted_iota(jnp.int32, (LANES, LANES), 0) == lax.broadcasted_iota(jnp.int32, (LANES, LANES), 1)
    for part in range(2):
        lanes = lanes_at(place + part * tiles)
        for ref in (high_ref, low_ref):
            ref[:, lanes] = jnp.where(eye, 0.0, ref[:, lanes].astype(jnp.float32)).astype(jnp.bfloat16)
    move.wait()
    y = y_ref[...]
    for n, (high, low) in enumerate(((last.at[0], last.at[1]), (high_ref, low_ref))):
        by_real = dot_slab(high[:, 0:half], y) + dot_slab(low[:, 0:half], y)
        by_imag = dot_slab(high[:, half:], y) + dot_slab(low[:, half:], y)
        store_products(by_real, by_imag, out_ref, n)

    start = pl.multiple_of(own * 16, 16)
    offsets = []
    for k in range(3):
        row_ref[k] = turned(pos_ref, k, 0)
        offsets.append(row_ref[k, pl.ds(start, 16), :] - pos_ref[k : k + 1, 0:LANES])
    w_real, w_imag = coupling(*offsets)
    eye = (lax.broadcasted_iota(jnp.int32, (16, LANES), 0) + start) == lax.broadcasted_iota(jnp.int32, (16, LANES), 1)
    w_real = jnp.where(eye, det_ref[1:2, :], w_real)[:, 0:64]
    w_imag = jnp.where(eye, -0.5, w_imag)[:, 0:64]
    for n, ref in enumerate((slab0, slab1, slab2, slab3)):
        there = pl.ds(pl.multiple_of(lax.rem(own + 4 - n, 4) * 16, 16), 16)
        full_ref[0, there, :] = ref[0]
        full_ref[1, there, :] = ref[1]

    def mul(a, b):
        return jnp.dot(a, b, precision=lax.Precision.HIGHEST, preferred_element_type=jnp.float32)

    v_real = mul(w_real, full_ref[0]) + mul(w_imag, full_ref[1])
    v_imag = mul(w_real, full_ref[1]) - mul(w_imag, full_ref[0])
    y_real, y_imag = slab0[0], slab0[1]
    line = det_ref[0:1, :]
    rest_ref[0] = line * y_imag - 0.5 * y_real - v_imag
    rest_ref[1] = v_real - line * y_real - 0.5 * y_imag


def finish_kernel(keep_ref, half_ref, core_ref, rest_ref, slab_ref, base_ref, accum_ref, next_ref, acc_ref):
    z = keep_ref[1] + half_ref[1] + core_ref[...]
    shift = z[32:33]
    rate_real = z[16:32] + shift * slab_ref[1] + rest_ref[0]
    rate_imag = rest_ref[1] - z[0:16] - shift * slab_ref[0]
    for n, rate in enumerate((rate_real, rate_imag)):
        next_ref[n] = base_ref[n] + (0.5 * TIME_STEP) * rate
        acc_ref[n] = accum_ref[n] + (TIME_STEP / 3.0) * rate


def params(mib):
    return pltpu.CompilerParams(vmem_limit_bytes=mib << 20)


def in_hbm(array):
    return pltpu.with_memory_space_constraint(array, pltpu.HBM)


def local(positions, detuning, populations, base, section, accum):
    bf16, f32 = jnp.bfloat16, jnp.float32
    count = positions.shape[1]
    tiles = count // (4 * LANES)
    deep = 2 * tiles * LANES
    hbm, vmem = pl.BlockSpec(memory_space=pltpu.HBM), pl.BlockSpec(memory_space=pltpu.VMEM)

    copies, pos, det = pl.pallas_call(
        pack_kernel,
        out_shape=(
            jax.ShapeDtypeStruct((tiles, PART, LANES), f32),
            pltpu.VMEM(positions.shape, f32),
            pltpu.VMEM((8, LANES), f32),
        ),
        in_specs=[hbm] * 4,
        out_specs=[vmem] * 3,
        scratch_shapes=[pltpu.VMEM((PART, LANES), f32), pltpu.SemaphoreType.DMA((6,))],
        compiler_params=params(4),
        cost_estimate=pl.CostEstimate(flops=1 << 16, bytes_accessed=1 << 19, transcendentals=0),
        name="pack_block",
    )(in_hbm(section), in_hbm(populations.reshape(1, LANES)), in_hbm(positions), in_hbm(detuning.reshape(1, count)))
    slabs = [section] + [lax.ppermute(section, "zl", [(i, (i + d) % 4) for i in range(4)]) for d in (1, 2, 3)]
    blocks = lax.all_to_all(copies, "yx", 0, 0, tiled=True)

    near, low, last = pl.pallas_call(
        far_kernel,
        out_shape=(
            pltpu.VMEM((2 * LANES, deep), bf16),
            pltpu.HBM((2 * LANES, deep), bf16),
            pltpu.HBM((2, LANES, deep), bf16),
        ),
        in_specs=[vmem],
        out_specs=[vmem, hbm, hbm],
        scratch_shapes=[
            pltpu.VMEM((3, 2 * LANES, LANES), f32),
            pltpu.VMEM((2 * LANES, deep), bf16),
            pltpu.VMEM((2, LANES, deep), bf16),
            pltpu.SemaphoreType.DMA((GROUPS, 2)),
            pltpu.SemaphoreType.DMA((GROUPS, 2)),
        ],
        compiler_params=params(12),
        cost_estimate=pl.CostEstimate(flops=45 << 20, bytes_accessed=6 << 20, transcendentals=1 << 20),
        name="far_tiles",
    )(pos)

    sent, y = pl.pallas_call(
        send_kernel,
        out_shape=(pltpu.VMEM((2, PART, LANES), f32), pltpu.VMEM((LANES, deep // 2), bf16)),
        in_specs=[vmem, hbm, vmem],
        out_specs=[vmem] * 2,
        scratch_shapes=[pltpu.VMEM((2 * LANES, deep), bf16), pltpu.SemaphoreType.DMA],
        compiler_params=params(8),
        cost_estimate=pl.CostEstimate(flops=1 << 29, bytes_accessed=4 << 20, transcendentals=0),
        name="send_products",
    )(near, in_hbm(low), blocks)
    half = lax.ppermute(sent, "zh", [(0, 1), (1, 0)])

    keep, rest = pl.pallas_call(
        keep_kernel,
        out_shape=(pltpu.VMEM((2, PART, LANES), f32), pltpu.VMEM((2, 16, LANES), f32)),
        in_specs=[vmem, hbm] + [vmem] * 6,
        out_specs=[vmem] * 2,
        scratch_shapes=[
            pltpu.VMEM((3, LANES, LANES), f32),
            pltpu.VMEM((LANES, deep), bf16),
            pltpu.VMEM((LANES, deep), bf16),
            pltpu.VMEM((2, 64, LANES), f32),
            pltpu.VMEM((2, LANES, deep), bf16),
            pltpu.SemaphoreType.DMA,
        ],
        compiler_params=params(8),
        cost_estimate=pl.CostEstimate(flops=1 << 29, bytes_accessed=4 << 20, transcendentals=1 << 20),
        name="keep_products",
    )(pos, in_hbm(last), y, *slabs, det)
    core = lax.ppermute(keep[0] + half[0], "c", [(0, 1), (1, 0)])

    return pl.pallas_call(
        finish_kernel,
        out_shape=(jax.ShapeDtypeStruct(base.shape, f32),) * 2,
        compiler_params=params(4),
        cost_estimate=pl.CostEstimate(flops=1 << 16, bytes_accessed=1 << 18, transcendentals=0),
        name="finish_rate",
    )(keep, half, core, rest, section, base, accum)


def solution(mesh):
    fine = Mesh(mesh.devices.reshape(16, 2, 2, 4), ("yx", "zh", "c", "zl"))
    rows = ("yx", "zh", "c")
    slab = P(None, "zl", rows)
    return jax.shard_map(
        local,
        mesh=fine,
        in_specs=(P(), P(), P(rows), slab, slab, slab),
        out_specs=(slab, slab),
        check_vma=False,
    )
```

```python
import math

import jax
import jax.numpy as jnp
from jax import lax
from jax.experimental import pallas as pl
from jax.experimental.pallas import tpu as pltpu
from jax.sharding import Mesh
from jax.sharding import PartitionSpec as P

TIME_STEP = 0.2
LANES = 128
COS = (0.9999999892, -19.73920453, 64.93911891, -85.45016433, 60.16782231, -25.96827976, 6.529565646)
SIN = (6.283182817, -41.3414213, 81.59618177, -76.58008122, 41.20531753, -12.27114973)
SCALE = -0.75 / (2.0 * math.pi)
INV_WAVE = 1.0 / (2.0 * math.pi)
ROUNDER = 12582912.0
PART = 40
WIDE = 48
EARLY = 160


def horner(coefs, scale, arg):
    total = jnp.float32(coefs[-1] * scale)
    for c in coefs[-2::-1]:
        total = total * arg + jnp.float32(c * scale)
    return total


def coupling(dx, dy, dz):
    dz_sq = dz * dz
    dist_sq = dx * dx + dy * dy + dz_sq
    inv = lax.rsqrt(dist_sq)
    dist = dist_sq * inv
    turn = dist - ((dist + ROUNDER) - ROUNDER)
    turn_sq = turn * turn
    cosine = horner(COS, SCALE, turn_sq) * inv
    sine = horner(SIN, SCALE, turn_sq) * turn * inv
    aligned = dz_sq * (inv * inv)
    quad_imag = inv * (INV_WAVE - (3.0 * INV_WAVE) * aligned)
    quad_real = (1.0 - aligned) - (INV_WAVE * inv) * quad_imag
    return cosine * quad_real - sine * quad_imag, sine * quad_real + cosine * quad_imag


def split(value):
    high = value.astype(jnp.bfloat16)
    low = (value - high.astype(jnp.float32)).astype(jnp.bfloat16)
    return high, low


def lanes_at(index):
    return pl.ds(pl.multiple_of(index * LANES, LANES), LANES)


def pack_kernel(section_ref, pops_ref, pos_ref, det_ref, copies_ref, pos_out, det_out, block_ref, sems):
    own = lax.axis_index("yx") * 4 + lax.axis_index("zh") * 2 + lax.axis_index("c")
    moves = [
        pltpu.make_async_copy(section_ref.at[0], block_ref.at[pl.ds(0, 16)], sems.at[0]),
        pltpu.make_async_copy(section_ref.at[1], block_ref.at[pl.ds(16, 16)], sems.at[1]),
        pltpu.make_async_copy(pops_ref, block_ref.at[pl.ds(32, 1)], sems.at[2]),
        pltpu.make_async_copy(pos_ref, pos_out, sems.at[3]),
        pltpu.make_async_copy(det_ref.at[:, lanes_at(own)], det_out.at[pl.ds(0, 1)], sems.at[4]),
        pltpu.make_async_copy(det_ref.at[:, pl.ds(0, LANES)], det_out.at[pl.ds(1, 1)], sems.at[5]),
    ]
    for move in moves:
        move.start()
    for move in moves[:3]:
        move.wait()
    block = block_ref[0:32, :]
    top = lax.broadcasted_iota(jnp.int32, (8, LANES), 0) == 0
    pops = jnp.where(top, 2.0 * block_ref[32:40, :] - 1.0, 0.0)
    for n in range(copies_ref.shape[0]):
        copies_ref[n, 0:32, :] = block
        copies_ref[n, 32:40, :] = pops
    for move in moves[3:]:
        move.wait()


def turned(pos_ref, k, index):
    line = pos_ref[k : k + 1, lanes_at(index)]
    return jnp.broadcast_to(line, (LANES, LANES)).T


def fill_tiles(pos_ref, row_ref, high_ref, low_ref, quads, first, count):
    quad = lax.axis_index("zh") * 2 + lax.axis_index("c")
    place = lax.axis_index("yx")
    tiles = pos_ref.shape[1] // (4 * LANES)
    for n, other in enumerate(quads):
        for k in range(3):
            row_ref[k, n * LANES : (n + 1) * LANES, :] = turned(pos_ref, k, place * 4 + other)

    def tile(step, carry):
        at = lanes_at(step * 4 + quad)
        cols = [pos_ref[k : k + 1, at] for k in range(3)]
        for n in range(0, count, 32):
            dx, dy, dz = [row_ref[k, first + n : first + n + 32, :] - cols[k] for k in range(3)]
            for part, value in enumerate(coupling(dx, dy, dz)):
                high, low = split(value)
                lanes = lanes_at(step + part * tiles)
                high_ref[n : n + 32, lanes] = high
                low_ref[n : n + 32, lanes] = low
        return carry

    lax.fori_loop(0, tiles, tile, 0)


def slab_term(pos_ref, slabs, det_ref, rest_ref, row_ref, full_ref):
    own = lax.axis_index("zl")
    start = pl.multiple_of(own * 16, 16)
    offsets = []
    for k in range(3):
        row_ref[k, 0:LANES, :] = turned(pos_ref, k, 0)
        offsets.append(row_ref[k, pl.ds(start, 16), :] - pos_ref[k : k + 1, 0:LANES])
    w_real, w_imag = coupling(*offsets)
    eye = (lax.broadcasted_iota(jnp.int32, (16, LANES), 0) + start) == lax.broadcasted_iota(jnp.int32, (16, LANES), 1)
    w_real = jnp.where(eye, det_ref[1:2, :], w_real)[:, 0:64]
    w_imag = jnp.where(eye, -0.5, w_imag)[:, 0:64]
    for n, ref in enumerate(slabs):
        there = pl.ds(pl.multiple_of(lax.rem(own + 4 - n, 4) * 16, 16), 16)
        full_ref[0, there, :] = ref[0]
        full_ref[1, there, :] = ref[1]

    def mul(a, b):
        return jnp.dot(a, b, precision=lax.Precision.HIGHEST, preferred_element_type=jnp.float32)

    v_real = mul(w_real, full_ref[0]) + mul(w_imag, full_ref[1])
    v_imag = mul(w_real, full_ref[1]) - mul(w_imag, full_ref[0])
    y_real, y_imag = slabs[0][0], slabs[0][1]
    line = det_ref[0:1, :]
    rest_ref[0] = line * y_imag - 0.5 * y_real - v_imag
    rest_ref[1] = v_real - line * y_real - 0.5 * y_imag


def far_quads():
    half, core = lax.axis_index("zh"), lax.axis_index("c")
    return (1 - half) * 2 + 1 - core, (1 - half) * 2 + core


def far_kernel(pos_ref, slab0, slab1, slab2, slab3, det_ref, high_ref, low_ref, rest_ref, row_ref, full_ref):
    slab_term(pos_ref, (slab0, slab1, slab2, slab3), det_ref, rest_ref, row_ref, full_ref)
    fill_tiles(pos_ref, row_ref, high_ref, low_ref, far_quads(), 0, EARLY)


def fill_slab(block_ref, y_ref):
    zeros = jnp.zeros((16, LANES), jnp.float32)

    def fill(step, carry):
        block = block_ref[step]
        pops = jnp.concatenate([block[32:40], zeros[0:8]], axis=0)
        lanes = lanes_at(step)
        for n, value in enumerate((block[0:16], block[16:32], pops)):
            high, low = split(value)
            y_ref[n * 16 : n * 16 + 16, lanes] = high
            y_ref[WIDE + n * 16 : WIDE + n * 16 + 16, lanes] = low
        y_ref[2 * WIDE :, lanes] = jnp.zeros((LANES - 2 * WIDE, LANES), jnp.bfloat16)
        return carry

    lax.fori_loop(0, block_ref.shape[0], fill, 0, unroll=4)


def dot_slab(tiles, y):
    return lax.dot_general(tiles, y, (((1,), (1,)), ((), ())), preferred_element_type=jnp.float32)


def store_products(by_real, by_imag, out_ref, at):
    for n in range(by_real.shape[0] // LANES):
        rows = slice(n * LANES, (n + 1) * LANES)
        real, imag = by_real[rows, :].T, by_imag[rows, :].T
        real = real[0:PART] + real[WIDE : WIDE + PART]
        imag = imag[0:32] + imag[WIDE : WIDE + 32]
        out_ref[at + n, 0:16, :] = real[0:16] - imag[16:32]
        out_ref[at + n, 16:32, :] = real[16:32] + imag[0:16]
        out_ref[at + n, 32:PART, :] = real[32:PART]


def products(high_ref, low_ref, y):
    half = high_ref.shape[1] // 2
    by_real = dot_slab(high_ref[:, 0:half], y) + dot_slab(low_ref[:, 0:half], y)
    by_imag = dot_slab(high_ref[:, half:], y) + dot_slab(low_ref[:, half:], y)
    return by_real, by_imag


def send_kernel(pos_ref, high_ref, low_ref, block_ref, out_ref, y_ref, row_ref, more_high, more_low):
    fill_slab(block_ref, y_ref)
    fill_tiles(pos_ref, row_ref, more_high, more_low, far_quads()[1:], EARLY - LANES, 2 * LANES - EARLY)
    y = y_ref[...]
    pairs = zip(products(high_ref, low_ref, y), products(more_high, more_low, y))
    by_real, by_imag = [jnp.concatenate(pair, axis=0) for pair in pairs]
    store_products(by_real, by_imag, out_ref, 0)


def keep_kernel(pos_ref, y_ref, out_ref, row_ref, high_ref, low_ref):
    place = lax.axis_index("yx")
    half, core = lax.axis_index("zh"), lax.axis_index("c")
    tiles = pos_ref.shape[1] // (4 * LANES)
    fill_tiles(pos_ref, row_ref, high_ref, low_ref, (half * 2 + 1 - core, half * 2 + core), 0, 2 * LANES)
    eye = lax.broadcasted_iota(jnp.int32, (LANES, LANES), 0) == lax.broadcasted_iota(jnp.int32, (LANES, LANES), 1)
    for part in range(2):
        lanes = lanes_at(place + part * tiles)
        for ref in (high_ref, low_ref):
            own = ref[LANES:, lanes].astype(jnp.float32)
            ref[LANES:, lanes] = jnp.where(eye, 0.0, own).astype(jnp.bfloat16)
    by_real, by_imag = products(high_ref, low_ref, y_ref[...])
    store_products(by_real, by_imag, out_ref, 0)


def finish_kernel(keep_ref, half_ref, core_ref, rest_ref, slab_ref, base_ref, accum_ref, next_ref, acc_ref):
    z = keep_ref[1] + half_ref[1] + core_ref[...]
    shift = z[32:33]
    rate_real = z[16:32] + shift * slab_ref[1] + rest_ref[0]
    rate_imag = rest_ref[1] - z[0:16] - shift * slab_ref[0]
    for n, rate in enumerate((rate_real, rate_imag)):
        next_ref[n] = base_ref[n] + (0.5 * TIME_STEP) * rate
        acc_ref[n] = accum_ref[n] + (TIME_STEP / 3.0) * rate


def params(mib):
    return pltpu.CompilerParams(vmem_limit_bytes=mib << 20)


def in_hbm(array):
    return pltpu.with_memory_space_constraint(array, pltpu.HBM)


def local(positions, detuning, populations, base, section, accum):
    bf16, f32 = jnp.bfloat16, jnp.float32
    count = positions.shape[1]
    tiles = count // (4 * LANES)
    deep = 2 * tiles * LANES
    hbm, vmem = pl.BlockSpec(memory_space=pltpu.HBM), pl.BlockSpec(memory_space=pltpu.VMEM)

    copies, pos, det = pl.pallas_call(
        pack_kernel,
        out_shape=(
            jax.ShapeDtypeStruct((tiles, PART, LANES), f32),
            pltpu.VMEM(positions.shape, f32),
            pltpu.VMEM((8, LANES), f32),
        ),
        in_specs=[hbm] * 4,
        out_specs=[vmem] * 3,
        scratch_shapes=[pltpu.VMEM((PART, LANES), f32), pltpu.SemaphoreType.DMA((6,))],
        compiler_params=params(4),
        cost_estimate=pl.CostEstimate(flops=1 << 16, bytes_accessed=1 << 19, transcendentals=0),
        name="pack_block",
    )(in_hbm(section), in_hbm(populations.reshape(1, LANES)), in_hbm(positions), in_hbm(detuning.reshape(1, count)))
    slabs = [section] + [lax.ppermute(section, "zl", [(i, (i + d) % 4) for i in range(4)]) for d in (1, 2, 3)]
    copies, *slabs = lax.optimization_barrier((copies, *slabs))
    blocks = lax.all_to_all(copies, "yx", 0, 0, tiled=True)

    high, low, rest = pl.pallas_call(
        far_kernel,
        out_shape=(
            pltpu.VMEM((EARLY, deep), bf16),
            pltpu.VMEM((EARLY, deep), bf16),
            pltpu.VMEM((2, 16, LANES), f32),
        ),
        in_specs=[vmem] * 6,
        out_specs=[vmem] * 3,
        scratch_shapes=[pltpu.VMEM((3, 2 * LANES, LANES), f32), pltpu.VMEM((2, 64, LANES), f32)],
        compiler_params=params(4),
        cost_estimate=pl.CostEstimate(flops=45 << 20, bytes_accessed=6 << 20, transcendentals=1 << 20),
        name="far_tiles",
    )(pos, *slabs, det)

    sent, y = pl.pallas_call(
        send_kernel,
        out_shape=(pltpu.VMEM((2, PART, LANES), f32), pltpu.VMEM((LANES, deep // 2), bf16)),
        in_specs=[vmem] * 4,
        out_specs=[vmem] * 2,
        scratch_shapes=[
            pltpu.VMEM((3, LANES, LANES), f32),
            pltpu.VMEM((2 * LANES - EARLY, deep), bf16),
            pltpu.VMEM((2 * LANES - EARLY, deep), bf16),
        ],
        compiler_params=params(8),
        cost_estimate=pl.CostEstimate(flops=1 << 29, bytes_accessed=4 << 20, transcendentals=0),
        name="send_products",
    )(pos, high, low, blocks)
    half = lax.ppermute(sent, "zh", [(0, 1), (1, 0)])

    keep = pl.pallas_call(
        keep_kernel,
        out_shape=pltpu.VMEM((2, PART, LANES), f32),
        in_specs=[vmem] * 2,
        out_specs=vmem,
        scratch_shapes=[
            pltpu.VMEM((3, 2 * LANES, LANES), f32),
            pltpu.VMEM((2 * LANES, deep), bf16),
            pltpu.VMEM((2 * LANES, deep), bf16),
        ],
        compiler_params=params(8),
        cost_estimate=pl.CostEstimate(flops=1 << 29, bytes_accessed=4 << 20, transcendentals=1 << 20),
        name="keep_products",
    )(pos, y)
    core = lax.ppermute(keep[0] + half[0], "c", [(0, 1), (1, 0)])

    return pl.pallas_call(
        finish_kernel,
        out_shape=(jax.ShapeDtypeStruct(base.shape, f32),) * 2,
        compiler_params=params(4),
        cost_estimate=pl.CostEstimate(flops=1 << 16, bytes_accessed=1 << 18, transcendentals=0),
        name="finish_rate",
    )(keep, half, core, rest, section, base, accum)


def solution(mesh):
    fine = Mesh(mesh.devices.reshape(16, 2, 2, 4), ("yx", "zh", "c", "zl"))
    rows = ("yx", "zh", "c")
    slab = P(None, "zl", rows)
    return jax.shard_map(
        local,
        mesh=fine,
        in_specs=(P(), P(), P(rows), slab, slab, slab),
        out_specs=(slab, slab),
        check_vma=False,
    )
```

```python
import math

import jax
import jax.numpy as jnp
from jax import lax
from jax.experimental import pallas as pl
from jax.experimental.pallas import tpu as pltpu
from jax.sharding import Mesh
from jax.sharding import PartitionSpec as P

TIME_STEP = 0.2
LANES = 128
COS = (0.9999992211, -19.73898242, 64.92872338, -85.27236068, 58.79387231, -21.07651549)
SIN = (6.283182817, -41.3414213, 81.59618177, -76.58008122, 41.20531753, -12.27114973)
SCALE = -0.75 / (2.0 * math.pi)
INV_WAVE = 1.0 / (2.0 * math.pi)
ROUNDER = 12582912.0
PART = 40
WIDE = 48
EARLY = 160


def horner(coefs, scale, arg):
    total = jnp.float32(coefs[-1] * scale)
    for c in coefs[-2::-1]:
        total = total * arg + jnp.float32(c * scale)
    return total


def coupling(dx, dy, dz):
    dz_sq = dz * dz
    dist_sq = dx * dx + dy * dy + dz_sq
    inv = lax.rsqrt(dist_sq)
    dist = dist_sq * inv
    turn = dist - ((dist + ROUNDER) - ROUNDER)
    turn_sq = turn * turn
    cosine = horner(COS, SCALE, turn_sq)
    sine = horner(SIN, SCALE, turn_sq) * turn
    inv_sq = inv * inv
    aligned = dz_sq * inv_sq
    quad_imag = inv_sq * (INV_WAVE - (3.0 * INV_WAVE) * aligned)
    quad_real = inv * ((1.0 - aligned) - INV_WAVE * quad_imag)
    return cosine * quad_real - sine * quad_imag, sine * quad_real + cosine * quad_imag


def split(value):
    high = value.astype(jnp.bfloat16)
    low = (value - high.astype(jnp.float32)).astype(jnp.bfloat16)
    return high, low


def lanes_at(index):
    return pl.ds(pl.multiple_of(index * LANES, LANES), LANES)


def pack_kernel(section_ref, pops_ref, pos_ref, det_ref, copies_ref, pos_out, det_out, block_ref, sems):
    own = lax.axis_index("yx") * 4 + lax.axis_index("zh") * 2 + lax.axis_index("c")
    moves = [
        pltpu.make_async_copy(section_ref.at[0], block_ref.at[pl.ds(0, 16)], sems.at[0]),
        pltpu.make_async_copy(section_ref.at[1], block_ref.at[pl.ds(16, 16)], sems.at[1]),
        pltpu.make_async_copy(pops_ref, block_ref.at[pl.ds(32, 1)], sems.at[2]),
        pltpu.make_async_copy(pos_ref, pos_out, sems.at[3]),
        pltpu.make_async_copy(det_ref.at[:, lanes_at(own)], det_out.at[pl.ds(0, 1)], sems.at[4]),
        pltpu.make_async_copy(det_ref.at[:, pl.ds(0, LANES)], det_out.at[pl.ds(1, 1)], sems.at[5]),
    ]
    for move in moves:
        move.start()
    for move in moves[:3]:
        move.wait()
    block = block_ref[0:32, :]
    top = lax.broadcasted_iota(jnp.int32, (8, LANES), 0) == 0
    pops = jnp.where(top, 2.0 * block_ref[32:40, :] - 1.0, 0.0)
    for n in range(copies_ref.shape[0]):
        copies_ref[n, 0:32, :] = block
        copies_ref[n, 32:40, :] = pops
    for move in moves[3:]:
        move.wait()


def turned(pos_ref, k, index):
    line = pos_ref[k : k + 1, lanes_at(index)]
    return jnp.broadcast_to(line, (LANES, LANES)).T


def fill_tiles(pos_ref, row_ref, high_ref, low_ref, quads, first, count):
    quad = lax.axis_index("zh") * 2 + lax.axis_index("c")
    place = lax.axis_index("yx")
    tiles = pos_ref.shape[1] // (4 * LANES)
    for n, other in enumerate(quads):
        for k in range(3):
            row_ref[k, n * LANES : (n + 1) * LANES, :] = turned(pos_ref, k, place * 4 + other)

    def tile(step, carry):
        at = lanes_at(step * 4 + quad)
        cols = [pos_ref[k : k + 1, at] for k in range(3)]
        for n in range(0, count, 32):
            dx, dy, dz = [row_ref[k, first + n : first + n + 32, :] - cols[k] for k in range(3)]
            for part, value in enumerate(coupling(dx, dy, dz)):
                high, low = split(value)
                lanes = lanes_at(step + part * tiles)
                high_ref[n : n + 32, lanes] = high
                low_ref[n : n + 32, lanes] = low
        return carry

    lax.fori_loop(0, tiles, tile, 0)


def term_kernel(pos_ref, slab_ref, near_ref, pair_ref, det_ref, rest_ref, row_ref, full_ref):
    own = lax.axis_index("zl")
    start = pl.multiple_of(own * 16, 16)
    offsets = []
    for k in range(3):
        row_ref[k] = turned(pos_ref, k, 0)
        offsets.append(row_ref[k, pl.ds(start, 16), :] - pos_ref[k : k + 1, 0:LANES])
    w_real, w_imag = coupling(*offsets)
    eye = (lax.broadcasted_iota(jnp.int32, (16, LANES), 0) + start) == lax.broadcasted_iota(jnp.int32, (16, LANES), 1)
    w_real = jnp.where(eye, det_ref[1:2, :], w_real)[:, 0:64]
    w_imag = jnp.where(eye, -0.5, w_imag)[:, 0:64]
    for n, ref in enumerate((slab_ref, near_ref, pair_ref.at[0], pair_ref.at[1])):
        place = own + (n % 2) * (1 - 2 * (own % 2))
        place = place + (n // 2) * (2 - 4 * (own // 2))
        there = pl.ds(pl.multiple_of(place * 16, 16), 16)
        full_ref[0, there, :] = ref[0]
        full_ref[1, there, :] = ref[1]

    def mul(a, b):
        return jnp.dot(a, b, precision=lax.Precision.HIGHEST, preferred_element_type=jnp.float32)

    v_real = mul(w_real, full_ref[0]) + mul(w_imag, full_ref[1])
    v_imag = mul(w_real, full_ref[1]) - mul(w_imag, full_ref[0])
    y_real, y_imag = slab_ref[0], slab_ref[1]
    line = det_ref[0:1, :]
    rest_ref[0] = line * y_imag - 0.5 * y_real - v_imag
    rest_ref[1] = v_real - line * y_real - 0.5 * y_imag


def pair_kernel(slab_ref, near_ref, pair_ref):
    pair_ref[0] = slab_ref[...]
    pair_ref[1] = near_ref[...]


def far_quads():
    half, core = lax.axis_index("zh"), lax.axis_index("c")
    return (1 - half) * 2 + 1 - core, (1 - half) * 2 + core


def far_kernel(pos_ref, high_ref, low_ref, row_ref):
    fill_tiles(pos_ref, row_ref, high_ref, low_ref, far_quads(), 0, EARLY)


def fill_slab(block_ref, y_ref):
    zeros = jnp.zeros((16, LANES), jnp.float32)

    def fill(step, carry):
        block = block_ref[step]
        pops = jnp.concatenate([block[32:40], zeros[0:8]], axis=0)
        lanes = lanes_at(step)
        for n, value in enumerate((block[0:16], block[16:32], pops)):
            high, low = split(value)
            y_ref[n * 16 : n * 16 + 16, lanes] = high
            y_ref[WIDE + n * 16 : WIDE + n * 16 + 16, lanes] = low
        y_ref[2 * WIDE :, lanes] = jnp.zeros((LANES - 2 * WIDE, LANES), jnp.bfloat16)
        return carry

    lax.fori_loop(0, block_ref.shape[0], fill, 0, unroll=4)


def dot_slab(tiles, y):
    return lax.dot_general(tiles, y, (((1,), (1,)), ((), ())), preferred_element_type=jnp.float32)


def store_products(by_real, by_imag, out_ref, at):
    for n in range(by_real.shape[0] // LANES):
        rows = slice(n * LANES, (n + 1) * LANES)
        real, imag = by_real[rows, :].T, by_imag[rows, :].T
        real = real[0:PART] + real[WIDE : WIDE + PART]
        imag = imag[0:32] + imag[WIDE : WIDE + 32]
        out_ref[at + n, 0:16, :] = real[0:16] - imag[16:32]
        out_ref[at + n, 16:32, :] = real[16:32] + imag[0:16]
        out_ref[at + n, 32:PART, :] = real[32:PART]


def products(high_ref, low_ref, y):
    half = high_ref.shape[1] // 2
    by_real = dot_slab(high_ref[:, 0:half], y) + dot_slab(low_ref[:, 0:half], y)
    by_imag = dot_slab(high_ref[:, half:], y) + dot_slab(low_ref[:, half:], y)
    return by_real, by_imag


def send_kernel(pos_ref, high_ref, low_ref, block_ref, out_ref, y_ref, row_ref, more_high, more_low):
    fill_slab(block_ref, y_ref)
    fill_tiles(pos_ref, row_ref, more_high, more_low, far_quads()[1:], EARLY - LANES, 2 * LANES - EARLY)
    y = y_ref[...]
    pairs = zip(products(high_ref, low_ref, y), products(more_high, more_low, y))
    by_real, by_imag = [jnp.concatenate(pair, axis=0) for pair in pairs]
    store_products(by_real, by_imag, out_ref, 0)


def keep_kernel(pos_ref, y_ref, out_ref, row_ref, high_ref, low_ref):
    place = lax.axis_index("yx")
    half, core = lax.axis_index("zh"), lax.axis_index("c")
    tiles = pos_ref.shape[1] // (4 * LANES)
    fill_tiles(pos_ref, row_ref, high_ref, low_ref, (half * 2 + 1 - core, half * 2 + core), 0, 2 * LANES)
    eye = lax.broadcasted_iota(jnp.int32, (LANES, LANES), 0) == lax.broadcasted_iota(jnp.int32, (LANES, LANES), 1)
    for part in range(2):
        lanes = lanes_at(place + part * tiles)
        for ref in (high_ref, low_ref):
            own = ref[LANES:, lanes].astype(jnp.float32)
            ref[LANES:, lanes] = jnp.where(eye, 0.0, own).astype(jnp.bfloat16)
    by_real, by_imag = products(high_ref, low_ref, y_ref[...])
    store_products(by_real, by_imag, out_ref, 0)


def finish_kernel(keep_ref, half_ref, core_ref, rest_ref, slab_ref, base_ref, accum_ref, next_ref, acc_ref):
    z = keep_ref[1] + half_ref[1] + core_ref[...]
    shift = z[32:33]
    rate_real = z[16:32] + shift * slab_ref[1] + rest_ref[0]
    rate_imag = rest_ref[1] - z[0:16] - shift * slab_ref[0]
    for n, rate in enumerate((rate_real, rate_imag)):
        next_ref[n] = base_ref[n] + (0.5 * TIME_STEP) * rate
        acc_ref[n] = accum_ref[n] + (TIME_STEP / 3.0) * rate


def params(mib):
    return pltpu.CompilerParams(vmem_limit_bytes=mib << 20)


def in_hbm(array):
    return pltpu.with_memory_space_constraint(array, pltpu.HBM)


def local(positions, detuning, populations, base, section, accum):
    bf16, f32 = jnp.bfloat16, jnp.float32
    count = positions.shape[1]
    tiles = count // (4 * LANES)
    deep = 2 * tiles * LANES
    hbm, vmem = pl.BlockSpec(memory_space=pltpu.HBM), pl.BlockSpec(memory_space=pltpu.VMEM)

    copies, pos, det = pl.pallas_call(
        pack_kernel,
        out_shape=(
            jax.ShapeDtypeStruct((tiles, PART, LANES), f32),
            pltpu.VMEM(positions.shape, f32),
            pltpu.VMEM((8, LANES), f32),
        ),
        in_specs=[hbm] * 4,
        out_specs=[vmem] * 3,
        scratch_shapes=[pltpu.VMEM((PART, LANES), f32), pltpu.SemaphoreType.DMA((6,))],
        compiler_params=params(4),
        cost_estimate=pl.CostEstimate(flops=1 << 16, bytes_accessed=1 << 19, transcendentals=0),
        name="pack_block",
    )(in_hbm(section), in_hbm(populations.reshape(1, LANES)), in_hbm(positions), in_hbm(detuning.reshape(1, count)))
    blocks = lax.all_to_all(copies, "yx", 0, 0, tiled=True)
    near = lax.ppermute(section, "zl", [(i, i ^ 1) for i in range(4)])

    pair = pl.pallas_call(
        pair_kernel,
        out_shape=pltpu.VMEM((2, 2, 16, LANES), f32),
        in_specs=[vmem] * 2,
        out_specs=vmem,
        compiler_params=params(1),
        cost_estimate=pl.CostEstimate(flops=1, bytes_accessed=1 << 16, transcendentals=0),
        name="pair_blocks",
    )(section, near)
    pair = lax.ppermute(pair, "zl", [(i, i ^ 2) for i in range(4)])

    high, low = pl.pallas_call(
        far_kernel,
        out_shape=(pltpu.VMEM((EARLY, deep), bf16),) * 2,
        in_specs=[vmem],
        out_specs=[vmem] * 2,
        scratch_shapes=[pltpu.VMEM((3, 2 * LANES, LANES), f32)],
        compiler_params=params(4),
        cost_estimate=pl.CostEstimate(flops=45 << 20, bytes_accessed=6 << 20, transcendentals=1 << 20),
        name="far_tiles",
    )(pos)

    sent, y = pl.pallas_call(
        send_kernel,
        out_shape=(
            pltpu.VMEM((2, PART, LANES), f32),
            pltpu.VMEM((LANES, deep // 2), bf16),
        ),
        in_specs=[vmem] * 4,
        out_specs=[vmem] * 2,
        scratch_shapes=[
            pltpu.VMEM((3, LANES, LANES), f32),
            pltpu.VMEM((2 * LANES - EARLY, deep), bf16),
            pltpu.VMEM((2 * LANES - EARLY, deep), bf16),
        ],
        compiler_params=params(8),
        cost_estimate=pl.CostEstimate(flops=1 << 29, bytes_accessed=4 << 20, transcendentals=0),
        name="send_products",
    )(pos, high, low, blocks)
    half = lax.ppermute(sent, "zh", [(0, 1), (1, 0)])

    keep = pl.pallas_call(
        keep_kernel,
        out_shape=pltpu.VMEM((2, PART, LANES), f32),
        in_specs=[vmem] * 2,
        out_specs=vmem,
        scratch_shapes=[
            pltpu.VMEM((3, 2 * LANES, LANES), f32),
            pltpu.VMEM((2 * LANES, deep), bf16),
            pltpu.VMEM((2 * LANES, deep), bf16),
        ],
        compiler_params=params(8),
        cost_estimate=pl.CostEstimate(flops=1 << 29, bytes_accessed=4 << 20, transcendentals=1 << 20),
        name="keep_products",
    )(pos, y)
    core = lax.ppermute(keep[0] + half[0], "c", [(0, 1), (1, 0)])
    rest = pl.pallas_call(
        term_kernel,
        out_shape=pltpu.VMEM((2, 16, LANES), f32),
        in_specs=[vmem] * 5,
        out_specs=vmem,
        scratch_shapes=[pltpu.VMEM((3, LANES, LANES), f32), pltpu.VMEM((2, 64, LANES), f32)],
        compiler_params=params(4),
        cost_estimate=pl.CostEstimate(flops=1 << 22, bytes_accessed=1 << 18, transcendentals=1 << 11),
        name="slab_term",
    )(pos, section, near, pair, det)

    return pl.pallas_call(
        finish_kernel,
        out_shape=(jax.ShapeDtypeStruct(base.shape, f32),) * 2,
        compiler_params=params(4),
        cost_estimate=pl.CostEstimate(flops=1 << 16, bytes_accessed=1 << 18, transcendentals=0),
        name="finish_rate",
    )(keep, half, core, rest, section, base, accum)


def solution(mesh):
    fine = Mesh(mesh.devices.reshape(16, 2, 2, 4), ("yx", "zh", "c", "zl"))
    rows = ("yx", "zh", "c")
    slab = P(None, "zl", rows)
    return jax.shard_map(
        local,
        mesh=fine,
        in_specs=(P(), P(), P(rows), slab, slab, slab),
        out_specs=(slab, slab),
        check_vma=False,
    )
```

```python
import math

import jax
import jax.numpy as jnp
from jax import lax
from jax.experimental import pallas as pl
from jax.experimental.pallas import tpu as pltpu
from jax.sharding import Mesh
from jax.sharding import PartitionSpec as P

TIME_STEP = 0.2
LANES = 128
COS = (0.9999992211, -19.73898242, 64.92872338, -85.27236068, 58.79387231, -21.07651549)
SIN = (6.283182817, -41.3414213, 81.59618177, -76.58008122, 41.20531753, -12.27114973)
SCALE = -0.75 / (2.0 * math.pi)
INV_WAVE = 1.0 / (2.0 * math.pi)
ROUNDER = 12582912.0
PART = 40
WIDE = 48
EARLY = 176


def horner(coefs, scale, arg):
    total = jnp.float32(coefs[-1] * scale)
    for c in coefs[-2::-1]:
        total = total * arg + jnp.float32(c * scale)
    return total


def coupling(dx, dy, dz):
    dz_sq = dz * dz
    dist_sq = dx * dx + dy * dy + dz_sq
    inv = lax.rsqrt(dist_sq)
    dist = dist_sq * inv
    turn = dist - ((dist + ROUNDER) - ROUNDER)
    turn_sq = turn * turn
    cosine = horner(COS, SCALE, turn_sq)
    sine = horner(SIN, SCALE, turn_sq) * turn
    inv_sq = inv * inv
    aligned = dz_sq * inv_sq
    quad_imag = inv_sq * (INV_WAVE - (3.0 * INV_WAVE) * aligned)
    quad_real = inv * ((1.0 - aligned) - INV_WAVE * quad_imag)
    return cosine * quad_real - sine * quad_imag, sine * quad_real + cosine * quad_imag


def split(value):
    high = value.astype(jnp.bfloat16)
    low = (value - high.astype(jnp.float32)).astype(jnp.bfloat16)
    return high, low


def lanes_at(index):
    return pl.ds(pl.multiple_of(index * LANES, LANES), LANES)


def pack_kernel(section_ref, pops_ref, pos_ref, det_ref, copies_ref, pos_out, det_out, block_ref, sems):
    own = lax.axis_index("yx") * 4 + lax.axis_index("zh") * 2 + lax.axis_index("c")
    moves = [
        pltpu.make_async_copy(section_ref.at[0], block_ref.at[pl.ds(0, 16)], sems.at[0]),
        pltpu.make_async_copy(section_ref.at[1], block_ref.at[pl.ds(16, 16)], sems.at[1]),
        pltpu.make_async_copy(pops_ref, block_ref.at[pl.ds(32, 1)], sems.at[2]),
        pltpu.make_async_copy(pos_ref, pos_out, sems.at[3]),
        pltpu.make_async_copy(det_ref.at[:, lanes_at(own)], det_out.at[pl.ds(0, 1)], sems.at[4]),
        pltpu.make_async_copy(det_ref.at[:, pl.ds(0, LANES)], det_out.at[pl.ds(1, 1)], sems.at[5]),
    ]
    for move in moves:
        move.start()
    for move in moves[:3]:
        move.wait()
    block = block_ref[0:32, :]
    top = lax.broadcasted_iota(jnp.int32, (8, LANES), 0) == 0
    pops = jnp.where(top, 2.0 * block_ref[32:40, :] - 1.0, 0.0)
    for n in range(copies_ref.shape[0]):
        copies_ref[n, 0:32, :] = block
        copies_ref[n, 32:40, :] = pops
    for move in moves[3:]:
        move.wait()


def turned(pos_ref, k, index):
    line = pos_ref[k : k + 1, lanes_at(index)]
    return jnp.broadcast_to(line, (LANES, LANES)).T


def fill_tiles(pos_ref, row_ref, high_ref, low_ref, quads, first, count):
    quad = lax.axis_index("zh") * 2 + lax.axis_index("c")
    place = lax.axis_index("yx")
    tiles = pos_ref.shape[1] // (4 * LANES)
    for n, other in enumerate(quads):
        for k in range(3):
            row_ref[k, n * LANES : (n + 1) * LANES, :] = turned(pos_ref, k, place * 4 + other)

    def tile(step, carry):
        at = lanes_at(step * 4 + quad)
        cols = [pos_ref[k : k + 1, at] for k in range(3)]
        for n in range(0, count, 32):
            size = min(32, count - n)
            dx, dy, dz = [row_ref[k, first + n : first + n + size, :] - cols[k] for k in range(3)]
            for part, value in enumerate(coupling(dx, dy, dz)):
                high, low = split(value)
                lanes = lanes_at(step + part * tiles)
                high_ref[n : n + size, lanes] = high
                low_ref[n : n + size, lanes] = low
        return carry

    lax.fori_loop(0, tiles, tile, 0)


def term_kernel(pos_ref, slab_ref, near_ref, pair_ref, det_ref, rest_ref, row_ref, full_ref):
    own = lax.axis_index("zl")
    start = pl.multiple_of(own * 16, 16)
    offsets = []
    for k in range(3):
        row_ref[k] = turned(pos_ref, k, 0)
        offsets.append(row_ref[k, pl.ds(start, 16), :] - pos_ref[k : k + 1, 0:LANES])
    w_real, w_imag = coupling(*offsets)
    eye = (lax.broadcasted_iota(jnp.int32, (16, LANES), 0) + start) == lax.broadcasted_iota(jnp.int32, (16, LANES), 1)
    w_real = jnp.where(eye, det_ref[1:2, :], w_real)[:, 0:64]
    w_imag = jnp.where(eye, -0.5, w_imag)[:, 0:64]
    for n, ref in enumerate((slab_ref, near_ref, pair_ref.at[0], pair_ref.at[1])):
        place = own + (n % 2) * (1 - 2 * (own % 2))
        place = place + (n // 2) * (2 - 4 * (own // 2))
        there = pl.ds(pl.multiple_of(place * 16, 16), 16)
        full_ref[0, there, :] = ref[0]
        full_ref[1, there, :] = ref[1]

    def mul(a, b):
        return jnp.dot(a, b, precision=lax.Precision.HIGHEST, preferred_element_type=jnp.float32)

    v_real = mul(w_real, full_ref[0]) + mul(w_imag, full_ref[1])
    v_imag = mul(w_real, full_ref[1]) - mul(w_imag, full_ref[0])
    y_real, y_imag = slab_ref[0], slab_ref[1]
    line = det_ref[0:1, :]
    rest_ref[0] = line * y_imag - 0.5 * y_real - v_imag
    rest_ref[1] = v_real - line * y_real - 0.5 * y_imag


def far_quads():
    half, core = lax.axis_index("zh"), lax.axis_index("c")
    return (1 - half) * 2 + 1 - core, (1 - half) * 2 + core


def fill_own(pos_ref, row_ref, high_ref, low_ref):
    place = lax.axis_index("yx")
    half, core = lax.axis_index("zh"), lax.axis_index("c")
    tiles = pos_ref.shape[1] // (4 * LANES)
    fill_tiles(pos_ref, row_ref, high_ref, low_ref, (half * 2 + 1 - core, half * 2 + core), 0, 2 * LANES)
    eye = lax.broadcasted_iota(jnp.int32, (LANES, LANES), 0) == lax.broadcasted_iota(jnp.int32, (LANES, LANES), 1)
    for part in range(2):
        lanes = lanes_at(place + part * tiles)
        for ref in (high_ref, low_ref):
            own = ref[LANES:, lanes].astype(jnp.float32)
            ref[LANES:, lanes] = jnp.where(eye, 0.0, own).astype(jnp.bfloat16)


def far_kernel(pos_ref, high_ref, low_ref, row_ref):
    fill_tiles(pos_ref, row_ref, high_ref, low_ref, far_quads(), 0, EARLY)


def fill_slab(block_ref, y_ref):
    zeros = jnp.zeros((16, LANES), jnp.float32)

    def fill(step, carry):
        block = block_ref[step]
        pops = jnp.concatenate([block[32:40], zeros[0:8]], axis=0)
        lanes = lanes_at(step)
        for n, value in enumerate((block[0:16], block[16:32], pops)):
            high, low = split(value)
            y_ref[n * 16 : n * 16 + 16, lanes] = high
            y_ref[WIDE + n * 16 : WIDE + n * 16 + 16, lanes] = low
        y_ref[2 * WIDE :, lanes] = jnp.zeros((LANES - 2 * WIDE, LANES), jnp.bfloat16)
        return carry

    lax.fori_loop(0, block_ref.shape[0], fill, 0, unroll=4)


def dot_slab(tiles, y):
    return lax.dot_general(tiles, y, (((1,), (1,)), ((), ())), preferred_element_type=jnp.float32)


def store_products(by_real, by_imag, out_ref, at):
    for n in range(by_real.shape[0] // LANES):
        rows = slice(n * LANES, (n + 1) * LANES)
        real, imag = by_real[rows, :].T, by_imag[rows, :].T
        real = real[0:PART] + real[WIDE : WIDE + PART]
        imag = imag[0:32] + imag[WIDE : WIDE + 32]
        out_ref[at + n, 0:16, :] = real[0:16] - imag[16:32]
        out_ref[at + n, 16:32, :] = real[16:32] + imag[0:16]
        out_ref[at + n, 32:PART, :] = real[32:PART]


def products(high_ref, low_ref, y):
    half = high_ref.shape[1] // 2
    by_real = dot_slab(high_ref[:, 0:half], y) + dot_slab(low_ref[:, 0:half], y)
    by_imag = dot_slab(high_ref[:, half:], y) + dot_slab(low_ref[:, half:], y)
    return by_real, by_imag


def send_kernel(pos_ref, high_ref, low_ref, block_ref, out_ref, y_ref, own_high, own_low, row_ref, more_high, more_low):
    fill_slab(block_ref, y_ref)
    fill_tiles(pos_ref, row_ref, more_high, more_low, far_quads()[1:], EARLY - LANES, 2 * LANES - EARLY)
    y = y_ref[...]
    pairs = zip(products(high_ref, low_ref, y), products(more_high, more_low, y))
    by_real, by_imag = [jnp.concatenate(pair, axis=0) for pair in pairs]
    store_products(by_real, by_imag, out_ref, 0)

    @pl.when(lax.axis_index("zh") == 0)
    def _():
        fill_own(pos_ref, row_ref, own_high, own_low)


def keep_kernel(pos_ref, y_ref, done_high, done_low, slab_ref, near_ref, out_ref, pair_ref, row_ref, high_ref, low_ref):
    pair_ref[0] = slab_ref[...]
    pair_ref[1] = near_ref[...]

    def finish(high, low):
        by_real, by_imag = products(high, low, y_ref[...])
        store_products(by_real, by_imag, out_ref, 0)

    @pl.when(lax.axis_index("zh") == 0)
    def _():
        finish(done_high, done_low)

    @pl.when(lax.axis_index("zh") == 1)
    def _():
        fill_own(pos_ref, row_ref, high_ref, low_ref)
        finish(high_ref, low_ref)


def finish_kernel(keep_ref, half_ref, core_ref, rest_ref, slab_ref, base_ref, accum_ref, next_ref, acc_ref):
    z = keep_ref[1] + half_ref[1] + core_ref[...]
    shift = z[32:33]
    rate_real = z[16:32] + shift * slab_ref[1] + rest_ref[0]
    rate_imag = rest_ref[1] - z[0:16] - shift * slab_ref[0]
    for n, rate in enumerate((rate_real, rate_imag)):
        next_ref[n] = base_ref[n] + (0.5 * TIME_STEP) * rate
        acc_ref[n] = accum_ref[n] + (TIME_STEP / 3.0) * rate


def params(mib):
    return pltpu.CompilerParams(vmem_limit_bytes=mib << 20)


def in_hbm(array):
    return pltpu.with_memory_space_constraint(array, pltpu.HBM)


def local(positions, detuning, populations, base, section, accum):
    bf16, f32 = jnp.bfloat16, jnp.float32
    count = positions.shape[1]
    tiles = count // (4 * LANES)
    deep = 2 * tiles * LANES
    hbm, vmem = pl.BlockSpec(memory_space=pltpu.HBM), pl.BlockSpec(memory_space=pltpu.VMEM)

    copies, pos, det = pl.pallas_call(
        pack_kernel,
        out_shape=(
            jax.ShapeDtypeStruct((tiles, PART, LANES), f32),
            pltpu.VMEM(positions.shape, f32),
            pltpu.VMEM((8, LANES), f32),
        ),
        in_specs=[hbm] * 4,
        out_specs=[vmem] * 3,
        scratch_shapes=[pltpu.VMEM((PART, LANES), f32), pltpu.SemaphoreType.DMA((6,))],
        compiler_params=params(4),
        cost_estimate=pl.CostEstimate(flops=1 << 16, bytes_accessed=1 << 19, transcendentals=0),
        name="pack_block",
    )(in_hbm(section), in_hbm(populations.reshape(1, LANES)), in_hbm(positions), in_hbm(detuning.reshape(1, count)))
    blocks = lax.all_to_all(copies, "yx", 0, 0, tiled=True)
    near = lax.ppermute(section, "zl", [(i, i ^ 1) for i in range(4)])

    high, low = pl.pallas_call(
        far_kernel,
        out_shape=(pltpu.VMEM((EARLY, deep), bf16),) * 2,
        in_specs=[vmem],
        out_specs=[vmem] * 2,
        scratch_shapes=[pltpu.VMEM((3, 2 * LANES, LANES), f32)],
        compiler_params=params(4),
        cost_estimate=pl.CostEstimate(flops=45 << 20, bytes_accessed=6 << 20, transcendentals=1 << 20),
        name="far_tiles",
    )(pos)

    sent, y, own_high, own_low = pl.pallas_call(
        send_kernel,
        out_shape=(
            pltpu.VMEM((2, PART, LANES), f32),
            pltpu.VMEM((LANES, deep // 2), bf16),
            pltpu.VMEM((2 * LANES, deep), bf16),
            pltpu.VMEM((2 * LANES, deep), bf16),
        ),
        in_specs=[vmem] * 4,
        out_specs=[vmem] * 4,
        scratch_shapes=[
            pltpu.VMEM((3, 2 * LANES, LANES), f32),
            pltpu.VMEM((2 * LANES - EARLY, deep), bf16),
            pltpu.VMEM((2 * LANES - EARLY, deep), bf16),
        ],
        compiler_params=params(8),
        cost_estimate=pl.CostEstimate(flops=1 << 29, bytes_accessed=4 << 20, transcendentals=0),
        name="send_products",
    )(pos, high, low, blocks)
    half = lax.ppermute(sent, "zh", [(0, 1), (1, 0)])

    keep, pair = pl.pallas_call(
        keep_kernel,
        out_shape=(pltpu.VMEM((2, PART, LANES), f32), pltpu.VMEM((2, 2, 16, LANES), f32)),
        in_specs=[vmem] * 6,
        out_specs=[vmem] * 2,
        scratch_shapes=[
            pltpu.VMEM((3, 2 * LANES, LANES), f32),
            pltpu.VMEM((2 * LANES, deep), bf16),
            pltpu.VMEM((2 * LANES, deep), bf16),
        ],
        compiler_params=params(8),
        cost_estimate=pl.CostEstimate(flops=1 << 29, bytes_accessed=4 << 20, transcendentals=1 << 20),
        name="keep_products",
    )(pos, y, own_high, own_low, section, near)
    pair = lax.ppermute(pair, "zl", [(i, i ^ 2) for i in range(4)])
    core = lax.ppermute(keep[0] + half[0], "c", [(0, 1), (1, 0)])
    rest = pl.pallas_call(
        term_kernel,
        out_shape=pltpu.VMEM((2, 16, LANES), f32),
        in_specs=[vmem] * 5,
        out_specs=vmem,
        scratch_shapes=[pltpu.VMEM((3, LANES, LANES), f32), pltpu.VMEM((2, 64, LANES), f32)],
        compiler_params=params(4),
        cost_estimate=pl.CostEstimate(flops=1 << 22, bytes_accessed=1 << 18, transcendentals=1 << 11),
        name="slab_term",
    )(pos, section, near, pair, det)

    return pl.pallas_call(
        finish_kernel,
        out_shape=(jax.ShapeDtypeStruct(base.shape, f32),) * 2,
        compiler_params=params(4),
        cost_estimate=pl.CostEstimate(flops=1 << 16, bytes_accessed=1 << 18, transcendentals=0),
        name="finish_rate",
    )(keep, half, core, rest, section, base, accum)


def solution(mesh):
    fine = Mesh(mesh.devices.reshape(16, 2, 2, 4), ("yx", "zh", "c", "zl"))
    rows = ("yx", "zh", "c")
    slab = P(None, "zl", rows)
    return jax.shard_map(
        local,
        mesh=fine,
        in_specs=(P(), P(), P(rows), slab, slab, slab),
        out_specs=(slab, slab),
        check_vma=False,
    )
```

```python
import math

import jax
import jax.numpy as jnp
from jax import lax
from jax.experimental import pallas as pl
from jax.experimental.pallas import tpu as pltpu
from jax.sharding import Mesh
from jax.sharding import PartitionSpec as P

TIME_STEP = 0.2
LANES = 128
COS = (0.9999992211, -19.73898242, 64.92872338, -85.27236068, 58.79387231, -21.07651549)
SIN = (6.283182817, -41.3414213, 81.59618177, -76.58008122, 41.20531753, -12.27114973)
SCALE = -0.75 / (2.0 * math.pi)
INV_WAVE = 1.0 / (2.0 * math.pi)
ROUNDER = 12582912.0
PART = 40
WIDE = 48
EARLY = 176


def horner(coefs, scale, arg):
    total = jnp.float32(coefs[-1] * scale)
    for c in coefs[-2::-1]:
        total = total * arg + jnp.float32(c * scale)
    return total


def coupling(dx, dy, dz):
    dz_sq = dz * dz
    dist_sq = dx * dx + dy * dy + dz_sq
    inv = lax.rsqrt(dist_sq)
    dist = dist_sq * inv
    turn = dist - ((dist + ROUNDER) - ROUNDER)
    turn_sq = turn * turn
    cosine = horner(COS, SCALE, turn_sq)
    sine = horner(SIN, SCALE, turn_sq) * turn
    inv_sq = inv * inv
    aligned = dz_sq * inv_sq
    quad_imag = inv_sq * (INV_WAVE - (3.0 * INV_WAVE) * aligned)
    quad_real = inv * ((1.0 - aligned) - INV_WAVE * quad_imag)
    return cosine * quad_real - sine * quad_imag, sine * quad_real + cosine * quad_imag


def split(value):
    high = value.astype(jnp.bfloat16)
    low = (value - high.astype(jnp.float32)).astype(jnp.bfloat16)
    return high, low


def lanes_at(index):
    return pl.ds(pl.multiple_of(index * LANES, LANES), LANES)


def pack_kernel(section_ref, pops_ref, pos_ref, det_ref, copies_ref, pos_out, det_out, block_ref, sems, out_sems):
    own = lax.axis_index("yx") * 4 + lax.axis_index("zh") * 2 + lax.axis_index("c")
    moves = [
        pltpu.make_async_copy(section_ref.at[0], block_ref.at[pl.ds(0, 16)], sems.at[0]),
        pltpu.make_async_copy(section_ref.at[1], block_ref.at[pl.ds(16, 16)], sems.at[1]),
        pltpu.make_async_copy(pops_ref, block_ref.at[pl.ds(32, 1)], sems.at[2]),
        pltpu.make_async_copy(pos_ref, pos_out, sems.at[3]),
        pltpu.make_async_copy(det_ref.at[:, lanes_at(own)], det_out.at[pl.ds(0, 1)], sems.at[4]),
        pltpu.make_async_copy(det_ref.at[:, pl.ds(0, LANES)], det_out.at[pl.ds(1, 1)], sems.at[5]),
    ]
    for move in moves:
        move.start()
    for move in moves[:3]:
        move.wait()
    top = lax.broadcasted_iota(jnp.int32, (8, LANES), 0) == 0
    block_ref[32:PART, :] = jnp.where(top, 2.0 * block_ref[32:PART, :] - 1.0, 0.0)
    spread = [pltpu.make_async_copy(block_ref, copies_ref.at[n], out_sems.at[n]) for n in range(copies_ref.shape[0])]
    for move in spread:
        move.start()
    for move in moves[3:] + spread:
        move.wait()


def turned(pos_ref, k, index):
    line = pos_ref[k : k + 1, lanes_at(index)]
    return jnp.broadcast_to(line, (LANES, LANES)).T


def fill_tiles(pos_ref, row_ref, high_ref, low_ref, quads, first, count):
    quad = lax.axis_index("zh") * 2 + lax.axis_index("c")
    place = lax.axis_index("yx")
    tiles = pos_ref.shape[1] // (4 * LANES)
    for n, other in enumerate(quads):
        for k in range(3):
            row_ref[k, n * LANES : (n + 1) * LANES, :] = turned(pos_ref, k, place * 4 + other)

    def tile(step, carry):
        at = lanes_at(step * 4 + quad)
        cols = [pos_ref[k : k + 1, at] for k in range(3)]
        for n in range(0, count, 32):
            size = min(32, count - n)
            dx, dy, dz = [row_ref[k, first + n : first + n + size, :] - cols[k] for k in range(3)]
            for part, value in enumerate(coupling(dx, dy, dz)):
                high, low = split(value)
                lanes = lanes_at(step + part * tiles)
                high_ref[n : n + size, lanes] = high
                low_ref[n : n + size, lanes] = low
        return carry

    lax.fori_loop(0, tiles, tile, 0)


def term_kernel(pos_ref, slab_ref, near_ref, pair_ref, det_ref, rest_ref, row_ref, full_ref):
    own = lax.axis_index("zl")
    start = pl.multiple_of(own * 16, 16)
    offsets = []
    for k in range(3):
        row_ref[k] = turned(pos_ref, k, 0)
        offsets.append(row_ref[k, pl.ds(start, 16), :] - pos_ref[k : k + 1, 0:LANES])
    w_real, w_imag = coupling(*offsets)
    eye = (lax.broadcasted_iota(jnp.int32, (16, LANES), 0) + start) == lax.broadcasted_iota(jnp.int32, (16, LANES), 1)
    w_real = jnp.where(eye, det_ref[1:2, :], w_real)[:, 0:64]
    w_imag = jnp.where(eye, -0.5, w_imag)[:, 0:64]
    for n, ref in enumerate((slab_ref, near_ref, pair_ref.at[0], pair_ref.at[1])):
        place = own + (n % 2) * (1 - 2 * (own % 2))
        place = place + (n // 2) * (2 - 4 * (own // 2))
        there = pl.ds(pl.multiple_of(place * 16, 16), 16)
        full_ref[0, there, :] = ref[0]
        full_ref[1, there, :] = ref[1]

    def mul(a, b):
        return jnp.dot(a, b, precision=lax.Precision.HIGHEST, preferred_element_type=jnp.float32)

    v_real = mul(w_real, full_ref[0]) + mul(w_imag, full_ref[1])
    v_imag = mul(w_real, full_ref[1]) - mul(w_imag, full_ref[0])
    y_real, y_imag = slab_ref[0], slab_ref[1]
    line = det_ref[0:1, :]
    rest_ref[0] = line * y_imag - 0.5 * y_real - v_imag
    rest_ref[1] = v_real - line * y_real - 0.5 * y_imag


def far_quads():
    half, core = lax.axis_index("zh"), lax.axis_index("c")
    return (1 - half) * 2 + 1 - core, (1 - half) * 2 + core


def early_blocks():
    lo = lax.axis_index("zl")
    return jnp.where(lo == 0, 2, jnp.where(lo == 3, 0, 1)) * (1 - lax.axis_index("zh"))


def fill_own(n, pos_ref, row_ref, high_ref, low_ref):
    place = lax.axis_index("yx")
    half, core = lax.axis_index("zh"), lax.axis_index("c")
    tiles = pos_ref.shape[1] // (4 * LANES)
    quad = half * 2 + (core if n else 1 - core)
    fill_tiles(pos_ref, row_ref, high_ref, low_ref, (quad,), 0, LANES)
    if n == 0:
        return
    eye = lax.broadcasted_iota(jnp.int32, (LANES, LANES), 0) == lax.broadcasted_iota(jnp.int32, (LANES, LANES), 1)
    for part in range(2):
        lanes = lanes_at(place + part * tiles)
        for ref in (high_ref, low_ref):
            ref[:, lanes] = jnp.where(eye, 0.0, ref[:, lanes].astype(jnp.float32)).astype(jnp.bfloat16)


def far_kernel(pos_ref, high_ref, low_ref, row_ref):
    fill_tiles(pos_ref, row_ref, high_ref, low_ref, far_quads(), 0, EARLY)


def fill_slab(block_ref, y_ref):
    zeros = jnp.zeros((16, LANES), jnp.float32)

    def fill(step, carry):
        block = block_ref[step]
        pops = jnp.concatenate([block[32:40], zeros[0:8]], axis=0)
        lanes = lanes_at(step)
        for n, value in enumerate((block[0:16], block[16:32], pops)):
            high, low = split(value)
            y_ref[n * 16 : n * 16 + 16, lanes] = high
            y_ref[WIDE + n * 16 : WIDE + n * 16 + 16, lanes] = low
        y_ref[2 * WIDE :, lanes] = jnp.zeros((LANES - 2 * WIDE, LANES), jnp.bfloat16)
        return carry

    lax.fori_loop(0, block_ref.shape[0], fill, 0, unroll=4)


def dot_slab(tiles, y):
    return lax.dot_general(tiles, y, (((1,), (1,)), ((), ())), preferred_element_type=jnp.float32)


def store_products(by_real, by_imag, out_ref, at):
    for n in range(by_real.shape[0] // LANES):
        rows = slice(n * LANES, (n + 1) * LANES)
        real, imag = by_real[rows, :].T, by_imag[rows, :].T
        real = real[0:PART] + real[WIDE : WIDE + PART]
        imag = imag[0:32] + imag[WIDE : WIDE + 32]
        out_ref[at + n, 0:16, :] = real[0:16] - imag[16:32]
        out_ref[at + n, 16:32, :] = real[16:32] + imag[0:16]
        out_ref[at + n, 32:PART, :] = real[32:PART]


def products(high_ref, low_ref, y):
    half = high_ref.shape[1] // 2
    by_real = dot_slab(high_ref[:, 0:half], y) + dot_slab(low_ref[:, 0:half], y)
    by_imag = dot_slab(high_ref[:, half:], y) + dot_slab(low_ref[:, half:], y)
    return by_real, by_imag


def send_kernel(pos_ref, high_ref, low_ref, block_ref, out_ref, y_ref, own_high, own_low, row_ref, more_high, more_low):
    fill_slab(block_ref, y_ref)
    fill_tiles(pos_ref, row_ref, more_high, more_low, far_quads()[1:], EARLY - LANES, 2 * LANES - EARLY)
    y = y_ref[...]
    pairs = zip(products(high_ref, low_ref, y), products(more_high, more_low, y))
    by_real, by_imag = [jnp.concatenate(pair, axis=0) for pair in pairs]
    store_products(by_real, by_imag, out_ref, 0)

    for n in range(2):

        @pl.when(early_blocks() > n)
        def _():
            fill_own(n, pos_ref, row_ref, own_high.at[n], own_low.at[n])


def keep_kernel(pos_ref, y_ref, done_high, done_low, slab_ref, near_ref, out_ref, pair_ref, row_ref, high_ref, low_ref):
    pair_ref[0] = slab_ref[...]
    pair_ref[1] = near_ref[...]

    def finish(n, high, low):
        by_real, by_imag = products(high, low, y_ref[...])
        store_products(by_real, by_imag, out_ref, n)

    for n in range(2):

        @pl.when(early_blocks() > n)
        def _():
            finish(n, done_high.at[n], done_low.at[n])

        @pl.when(early_blocks() <= n)
        def _():
            fill_own(n, pos_ref, row_ref, high_ref, low_ref)
            finish(n, high_ref, low_ref)


def finish_kernel(keep_ref, half_ref, core_ref, rest_ref, slab_ref, base_ref, accum_ref, next_ref, acc_ref):
    z = keep_ref[1] + half_ref[1] + core_ref[...]
    shift = z[32:33]
    rate_real = z[16:32] + shift * slab_ref[1] + rest_ref[0]
    rate_imag = rest_ref[1] - z[0:16] - shift * slab_ref[0]
    for n, rate in enumerate((rate_real, rate_imag)):
        next_ref[n] = base_ref[n] + (0.5 * TIME_STEP) * rate
        acc_ref[n] = accum_ref[n] + (TIME_STEP / 3.0) * rate


def params(mib):
    return pltpu.CompilerParams(vmem_limit_bytes=mib << 20)


def in_hbm(array):
    return pltpu.with_memory_space_constraint(array, pltpu.HBM)


def local(positions, detuning, populations, base, section, accum):
    bf16, f32 = jnp.bfloat16, jnp.float32
    count = positions.shape[1]
    tiles = count // (4 * LANES)
    deep = 2 * tiles * LANES
    hbm, vmem = pl.BlockSpec(memory_space=pltpu.HBM), pl.BlockSpec(memory_space=pltpu.VMEM)

    copies, pos, det = pl.pallas_call(
        pack_kernel,
        out_shape=(
            pltpu.HBM((tiles, PART, LANES), f32),
            pltpu.VMEM(positions.shape, f32),
            pltpu.VMEM((8, LANES), f32),
        ),
        in_specs=[hbm] * 4,
        out_specs=[hbm, vmem, vmem],
        scratch_shapes=[
            pltpu.VMEM((PART, LANES), f32),
            pltpu.SemaphoreType.DMA((6,)),
            pltpu.SemaphoreType.DMA((tiles,)),
        ],
        compiler_params=params(4),
        cost_estimate=pl.CostEstimate(flops=1 << 16, bytes_accessed=1 << 19, transcendentals=0),
        name="pack_block",
    )(in_hbm(section), in_hbm(populations.reshape(1, LANES)), in_hbm(positions), in_hbm(detuning.reshape(1, count)))
    blocks = lax.all_to_all(copies, "yx", 0, 0, tiled=True)
    near = lax.ppermute(section, "zl", [(i, i ^ 1) for i in range(4)])

    high, low = pl.pallas_call(
        far_kernel,
        out_shape=(pltpu.VMEM((EARLY, deep), bf16),) * 2,
        in_specs=[vmem],
        out_specs=[vmem] * 2,
        scratch_shapes=[pltpu.VMEM((3, 2 * LANES, LANES), f32)],
        compiler_params=params(4),
        cost_estimate=pl.CostEstimate(flops=45 << 20, bytes_accessed=6 << 20, transcendentals=1 << 20),
        name="far_tiles",
    )(pos)

    sent, y, own_high, own_low = pl.pallas_call(
        send_kernel,
        out_shape=(
            pltpu.VMEM((2, PART, LANES), f32),
            pltpu.VMEM((LANES, deep // 2), bf16),
            pltpu.VMEM((2, LANES, deep), bf16),
            pltpu.VMEM((2, LANES, deep), bf16),
        ),
        in_specs=[vmem] * 4,
        out_specs=[vmem] * 4,
        scratch_shapes=[
            pltpu.VMEM((3, 2 * LANES, LANES), f32),
            pltpu.VMEM((2 * LANES - EARLY, deep), bf16),
            pltpu.VMEM((2 * LANES - EARLY, deep), bf16),
        ],
        compiler_params=params(8),
        cost_estimate=pl.CostEstimate(flops=1 << 29, bytes_accessed=4 << 20, transcendentals=0),
        name="send_products",
    )(pos, high, low, blocks)
    half = lax.ppermute(sent, "zh", [(0, 1), (1, 0)])

    keep, pair = pl.pallas_call(
        keep_kernel,
        out_shape=(pltpu.VMEM((2, PART, LANES), f32), pltpu.VMEM((2, 2, 16, LANES), f32)),
        in_specs=[vmem] * 6,
        out_specs=[vmem] * 2,
        scratch_shapes=[
            pltpu.VMEM((3, LANES, LANES), f32),
            pltpu.VMEM((LANES, deep), bf16),
            pltpu.VMEM((LANES, deep), bf16),
        ],
        compiler_params=params(8),
        cost_estimate=pl.CostEstimate(flops=1 << 29, bytes_accessed=4 << 20, transcendentals=1 << 20),
        name="keep_products",
    )(pos, y, own_high, own_low, section, near)
    pair = lax.ppermute(pair, "zl", [(i, i ^ 2) for i in range(4)])
    core = lax.ppermute(keep[0] + half[0], "c", [(0, 1), (1, 0)])
    rest = pl.pallas_call(
        term_kernel,
        out_shape=pltpu.VMEM((2, 16, LANES), f32),
        in_specs=[vmem] * 5,
        out_specs=vmem,
        scratch_shapes=[pltpu.VMEM((3, LANES, LANES), f32), pltpu.VMEM((2, 64, LANES), f32)],
        compiler_params=params(4),
        cost_estimate=pl.CostEstimate(flops=1 << 22, bytes_accessed=1 << 18, transcendentals=1 << 11),
        name="slab_term",
    )(pos, section, near, pair, det)

    return pl.pallas_call(
        finish_kernel,
        out_shape=(jax.ShapeDtypeStruct(base.shape, f32),) * 2,
        compiler_params=params(4),
        cost_estimate=pl.CostEstimate(flops=1 << 16, bytes_accessed=1 << 18, transcendentals=0),
        name="finish_rate",
    )(keep, half, core, rest, section, base, accum)


def solution(mesh):
    fine = Mesh(mesh.devices.reshape(16, 2, 2, 4), ("yx", "zh", "c", "zl"))
    rows = ("yx", "zh", "c")
    slab = P(None, "zl", rows)
    return jax.shard_map(
        local,
        mesh=fine,
        in_specs=(P(), P(), P(rows), slab, slab, slab),
        out_specs=(slab, slab),
        check_vma=False,
    )
```

```python
import math

import jax
import jax.numpy as jnp
from jax import lax
from jax.experimental import pallas as pl
from jax.experimental.pallas import tpu as pltpu
from jax.sharding import Mesh
from jax.sharding import PartitionSpec as P

TIME_STEP = 0.2
LANES = 128
COS = (0.9999992211, -19.73898242, 64.92872338, -85.27236068, 58.79387231, -21.07651549)
SIN = (6.283182817, -41.3414213, 81.59618177, -76.58008122, 41.20531753, -12.27114973)
SCALE = -0.75 / (2.0 * math.pi)
INV_WAVE = 1.0 / (2.0 * math.pi)
ROUNDER = 12582912.0
PART = 40
WIDE = 48


def horner(coefs, scale, arg):
    total = jnp.float32(coefs[-1] * scale)
    for c in coefs[-2::-1]:
        total = total * arg + jnp.float32(c * scale)
    return total


def coupling(dx, dy, dz):
    dz_sq = dz * dz
    dist_sq = dx * dx + dy * dy + dz_sq
    inv = lax.rsqrt(dist_sq)
    dist = dist_sq * inv
    turn = dist - ((dist + ROUNDER) - ROUNDER)
    turn_sq = turn * turn
    cosine = horner(COS, SCALE, turn_sq)
    sine = horner(SIN, SCALE, turn_sq) * turn
    inv_sq = inv * inv
    aligned = dz_sq * inv_sq
    quad_imag = inv_sq * (INV_WAVE - (3.0 * INV_WAVE) * aligned)
    quad_real = inv * ((1.0 - aligned) - INV_WAVE * quad_imag)
    return cosine * quad_real - sine * quad_imag, sine * quad_real + cosine * quad_imag


def split(value):
    high = value.astype(jnp.bfloat16)
    low = (value - high.astype(jnp.float32)).astype(jnp.bfloat16)
    return high, low


def lanes_at(index):
    return pl.ds(pl.multiple_of(index * LANES, LANES), LANES)


def place_of(step):
    y = lax.rem(lax.axis_index("y") + 4 - lax.rem(step, 4), 4)
    x = lax.rem(lax.axis_index("x") + 4 - lax.div(step, 4), 4)
    return y * 4 + x


def own_place():
    return lax.axis_index("y") * 4 + lax.axis_index("x")


def pack_kernel(section_ref, pops_ref, pos_ref, det_ref, block_ref, pos_out, det_out, sems):
    own = own_place() * 4 + lax.axis_index("zh") * 2 + lax.axis_index("c")
    moves = [
        pltpu.make_async_copy(section_ref.at[0], block_ref.at[pl.ds(0, 16)], sems.at[0]),
        pltpu.make_async_copy(section_ref.at[1], block_ref.at[pl.ds(16, 16)], sems.at[1]),
        pltpu.make_async_copy(pops_ref, block_ref.at[pl.ds(32, 1)], sems.at[2]),
        pltpu.make_async_copy(pos_ref, pos_out, sems.at[3]),
        pltpu.make_async_copy(det_ref.at[:, lanes_at(own)], det_out.at[pl.ds(0, 1)], sems.at[4]),
        pltpu.make_async_copy(det_ref.at[:, pl.ds(0, LANES)], det_out.at[pl.ds(1, 1)], sems.at[5]),
    ]
    for move in moves:
        move.start()
    for move in moves:
        move.wait()
    top = lax.broadcasted_iota(jnp.int32, (8, LANES), 0) == 0
    block_ref[32:PART, :] = jnp.where(top, 2.0 * block_ref[32:PART, :] - 1.0, 0.0)


def merge_kernel(block_ref, one_ref, two_ref, three_ref, pos_ref, first_ref, all_ref, pos_out):
    for n, ref in enumerate((block_ref, one_ref, two_ref, three_ref)):
        all_ref[n] = ref[...]
    pos_out[...] = pos_ref[...]


def turned(pos_ref, k, index):
    line = pos_ref[k : k + 1, lanes_at(index)]
    return jnp.broadcast_to(line, (LANES, LANES)).T


def fill_tiles(pos_ref, row_ref, high_ref, low_ref, quads, first, count):
    quad = lax.axis_index("zh") * 2 + lax.axis_index("c")
    place = own_place()
    tiles = pos_ref.shape[1] // (4 * LANES)
    for n, other in enumerate(quads):
        for k in range(3):
            row_ref[k, n * LANES : (n + 1) * LANES, :] = turned(pos_ref, k, place * 4 + other)

    def tile(step, carry):
        at = lanes_at(place_of(step) * 4 + quad)
        cols = [pos_ref[k : k + 1, at] for k in range(3)]
        for n in range(0, count, 32):
            size = min(32, count - n)
            dx, dy, dz = [row_ref[k, first + n : first + n + size, :] - cols[k] for k in range(3)]
            for part, value in enumerate(coupling(dx, dy, dz)):
                high, low = split(value)
                lanes = lanes_at(step + part * tiles)
                high_ref[n : n + size, lanes] = high
                low_ref[n : n + size, lanes] = low
        return carry

    lax.fori_loop(0, tiles, tile, 0)


def term_kernel(pos_ref, slab_ref, near_ref, pair_ref, det_ref, rest_ref, row_ref, full_ref):
    own = lax.axis_index("zl")
    start = pl.multiple_of(own * 16, 16)
    offsets = []
    for k in range(3):
        row_ref[k] = turned(pos_ref, k, 0)
        offsets.append(row_ref[k, pl.ds(start, 16), :] - pos_ref[k : k + 1, 0:LANES])
    w_real, w_imag = coupling(*offsets)
    eye = (lax.broadcasted_iota(jnp.int32, (16, LANES), 0) + start) == lax.broadcasted_iota(jnp.int32, (16, LANES), 1)
    w_real = jnp.where(eye, det_ref[1:2, :], w_real)[:, 0:64]
    w_imag = jnp.where(eye, -0.5, w_imag)[:, 0:64]
    for n, ref in enumerate((slab_ref, near_ref, pair_ref.at[0], pair_ref.at[1])):
        place = own + (n % 2) * (1 - 2 * (own % 2))
        place = place + (n // 2) * (2 - 4 * (own // 2))
        there = pl.ds(pl.multiple_of(place * 16, 16), 16)
        full_ref[0, there, :] = ref[0]
        full_ref[1, there, :] = ref[1]

    def mul(a, b):
        return jnp.dot(a, b, precision=lax.Precision.HIGHEST, preferred_element_type=jnp.float32)

    v_real = mul(w_real, full_ref[0]) + mul(w_imag, full_ref[1])
    v_imag = mul(w_real, full_ref[1]) - mul(w_imag, full_ref[0])
    y_real, y_imag = slab_ref[0], slab_ref[1]
    line = det_ref[0:1, :]
    rest_ref[0] = line * y_imag - 0.5 * y_real - v_imag
    rest_ref[1] = v_real - line * y_real - 0.5 * y_imag


def early_own():
    return (1 - lax.axis_index("zh")) * (lax.axis_index("zl") < 2).astype(jnp.int32)


def fill_own(pos_ref, row_ref, high_ref, low_ref):
    tiles = pos_ref.shape[1] // (4 * LANES)
    quad = lax.axis_index("zh") * 2 + lax.axis_index("c")
    fill_tiles(pos_ref, row_ref, high_ref, low_ref, (quad,), 0, LANES)
    eye = lax.broadcasted_iota(jnp.int32, (LANES, LANES), 0) == lax.broadcasted_iota(jnp.int32, (LANES, LANES), 1)
    for part in range(2):
        lanes = pl.ds(part * tiles * LANES, LANES)
        for ref in (high_ref, low_ref):
            ref[:, lanes] = jnp.where(eye, 0.0, ref[:, lanes].astype(jnp.float32)).astype(jnp.bfloat16)


def first_kernel(pos_ref, high_ref, low_ref, row_ref):
    half, core = lax.axis_index("zh"), lax.axis_index("c")
    fill_tiles(pos_ref, row_ref, high_ref, low_ref, ((1 - half) * 2 + 1 - core,), 0, LANES)


def second_kernel(pos_ref, high_ref, low_ref, row_ref):
    half, core = lax.axis_index("zh"), lax.axis_index("c")
    quads = ((1 - half) * 2 + core, half * 2 + 1 - core)
    fill_tiles(pos_ref, row_ref, high_ref, low_ref, quads, 0, 2 * LANES)


def fill_slab(refs, y_ref):
    zeros = jnp.zeros((16, LANES), jnp.float32)
    for step in range(16):
        block = refs[step // 4][step % 4]
        pops = jnp.concatenate([block[32:40], zeros[0:8]], axis=0)
        lanes = slice(step * LANES, (step + 1) * LANES)
        for n, value in enumerate((block[0:16], block[16:32], pops)):
            high, low = split(value)
            y_ref[n * 16 : n * 16 + 16, lanes] = high
            y_ref[WIDE + n * 16 : WIDE + n * 16 + 16, lanes] = low
        y_ref[2 * WIDE :, lanes] = jnp.zeros((LANES - 2 * WIDE, LANES), jnp.bfloat16)


def dot_slab(tiles, y):
    return lax.dot_general(tiles, y, (((1,), (1,)), ((), ())), preferred_element_type=jnp.float32)


def store_products(by_real, by_imag, out_ref, at):
    for n in range(by_real.shape[0] // LANES):
        rows = slice(n * LANES, (n + 1) * LANES)
        real, imag = by_real[rows, :].T, by_imag[rows, :].T
        real = real[0:PART] + real[WIDE : WIDE + PART]
        imag = imag[0:32] + imag[WIDE : WIDE + 32]
        out_ref[at + n, 0:16, :] = real[0:16] - imag[16:32]
        out_ref[at + n, 16:32, :] = real[16:32] + imag[0:16]
        out_ref[at + n, 32:PART, :] = real[32:PART]


def products(high_ref, low_ref, y):
    half = high_ref.shape[1] // 2
    by_real = dot_slab(high_ref[:, 0:half], y) + dot_slab(low_ref[:, 0:half], y)
    by_imag = dot_slab(high_ref[:, half:], y) + dot_slab(low_ref[:, half:], y)
    return by_real, by_imag


def send_kernel(pos_ref, high0, low0, high1, low1, all0, all1, all2, all3, out_ref, y_ref, own_high, own_low, row_ref):
    fill_slab((all0, all1, all2, all3), y_ref)
    y = y_ref[...]
    store_products(*products(high0, low0, y), out_ref, 0)
    store_products(*products(high1.at[pl.ds(0, LANES)], low1.at[pl.ds(0, LANES)], y), out_ref, 1)

    @pl.when(early_own() == 1)
    def _():
        fill_own(pos_ref, row_ref, own_high, own_low)


def keep_kernel(pos_ref, y_ref, high1, low1, done_high, done_low, slab_ref, near_ref, out_ref, pair_ref, row_ref, high_ref, low_ref):
    pair_ref[0] = slab_ref[...]
    pair_ref[1] = near_ref[...]
    y = y_ref[...]
    store_products(*products(high1.at[pl.ds(LANES, LANES)], low1.at[pl.ds(LANES, LANES)], y), out_ref, 0)

    @pl.when(early_own() == 1)
    def _():
        store_products(*products(done_high, done_low, y), out_ref, 1)

    @pl.when(early_own() == 0)
    def _():
        fill_own(pos_ref, row_ref, high_ref, low_ref)
        store_products(*products(high_ref, low_ref, y), out_ref, 1)


def finish_kernel(keep_ref, half_ref, core_ref, rest_ref, slab_ref, base_ref, accum_ref, next_ref, acc_ref):
    z = keep_ref[1] + half_ref[1] + core_ref[...]
    shift = z[32:33]
    rate_real = z[16:32] + shift * slab_ref[1] + rest_ref[0]
    rate_imag = rest_ref[1] - z[0:16] - shift * slab_ref[0]
    for n, rate in enumerate((rate_real, rate_imag)):
        next_ref[n] = base_ref[n] + (0.5 * TIME_STEP) * rate
        acc_ref[n] = accum_ref[n] + (TIME_STEP / 3.0) * rate


def params(mib):
    return pltpu.CompilerParams(vmem_limit_bytes=mib << 20)


def in_hbm(array):
    return pltpu.with_memory_space_constraint(array, pltpu.HBM)


def local(positions, detuning, populations, base, section, accum):
    bf16, f32 = jnp.bfloat16, jnp.float32
    count = positions.shape[1]
    tiles = count // (4 * LANES)
    deep = 2 * tiles * LANES
    hbm, vmem = pl.BlockSpec(memory_space=pltpu.HBM), pl.BlockSpec(memory_space=pltpu.VMEM)

    block, pos, det = pl.pallas_call(
        pack_kernel,
        out_shape=(pltpu.VMEM((PART, LANES), f32), pltpu.VMEM(positions.shape, f32), pltpu.VMEM((8, LANES), f32)),
        in_specs=[hbm] * 4,
        out_specs=[vmem] * 3,
        scratch_shapes=[pltpu.SemaphoreType.DMA((6,))],
        compiler_params=params(4),
        cost_estimate=pl.CostEstimate(flops=1 << 16, bytes_accessed=1 << 19, transcendentals=0),
        name="pack_block",
    )(in_hbm(section), in_hbm(populations.reshape(1, LANES)), in_hbm(positions), in_hbm(detuning.reshape(1, count)))
    along_y = [lax.ppermute(block, "y", [(i, (i + d) % 4) for i in range(4)]) for d in (1, 2, 3)]

    high0, low0 = pl.pallas_call(
        first_kernel,
        out_shape=(pltpu.VMEM((LANES, deep), bf16),) * 2,
        in_specs=[vmem],
        out_specs=[vmem] * 2,
        scratch_shapes=[pltpu.VMEM((3, LANES, LANES), f32)],
        compiler_params=params(4),
        cost_estimate=pl.CostEstimate(flops=15 << 20, bytes_accessed=2 << 20, transcendentals=1 << 20),
        name="first_tiles",
    )(pos)

    merged, pos_again = pl.pallas_call(
        merge_kernel,
        out_shape=(pltpu.VMEM((4, PART, LANES), f32), pltpu.VMEM(positions.shape, f32)),
        in_specs=[vmem] * 5 + [pl.BlockSpec(memory_space=pl.ANY)],
        out_specs=[vmem] * 2,
        compiler_params=params(2),
        cost_estimate=pl.CostEstimate(flops=1, bytes_accessed=1 << 18, transcendentals=0),
        name="merge_blocks",
    )(block, *along_y, pos, high0)
    along_x = [lax.ppermute(merged, "x", [(i, (i + d) % 4) for i in range(4)]) for d in (1, 2, 3)]
    near = lax.ppermute(section, "zl", [(i, i ^ 1) for i in range(4)])

    high1, low1 = pl.pallas_call(
        second_kernel,
        out_shape=(pltpu.VMEM((2 * LANES, deep), bf16),) * 2,
        in_specs=[vmem],
        out_specs=[vmem] * 2,
        scratch_shapes=[pltpu.VMEM((3, 2 * LANES, LANES), f32)],
        compiler_params=params(4),
        cost_estimate=pl.CostEstimate(flops=30 << 20, bytes_accessed=4 << 20, transcendentals=1 << 20),
        name="second_tiles",
    )(pos_again)

    sent, y, own_high, own_low = pl.pallas_call(
        send_kernel,
        out_shape=(
            pltpu.VMEM((2, PART, LANES), f32),
            pltpu.VMEM((LANES, deep // 2), bf16),
            pltpu.VMEM((LANES, deep), bf16),
            pltpu.VMEM((LANES, deep), bf16),
        ),
        in_specs=[vmem] * 9,
        out_specs=[vmem] * 4,
        scratch_shapes=[pltpu.VMEM((3, LANES, LANES), f32)],
        compiler_params=params(8),
        cost_estimate=pl.CostEstimate(flops=1 << 29, bytes_accessed=4 << 20, transcendentals=0),
        name="send_products",
    )(pos, high0, low0, high1, low1, merged, *along_x)
    half = lax.ppermute(sent, "zh", [(0, 1), (1, 0)])

    keep, pair = pl.pallas_call(
        keep_kernel,
        out_shape=(pltpu.VMEM((2, PART, LANES), f32), pltpu.VMEM((2, 2, 16, LANES), f32)),
        in_specs=[vmem] * 8,
        out_specs=[vmem] * 2,
        scratch_shapes=[
            pltpu.VMEM((3, LANES, LANES), f32),
            pltpu.VMEM((LANES, deep), bf16),
            pltpu.VMEM((LANES, deep), bf16),
        ],
        compiler_params=params(8),
        cost_estimate=pl.CostEstimate(flops=1 << 29, bytes_accessed=4 << 20, transcendentals=1 << 20),
        name="keep_products",
    )(pos, y, high1, low1, own_high, own_low, section, near)
    pair = lax.ppermute(pair, "zl", [(i, i ^ 2) for i in range(4)])
    core = lax.ppermute(keep[0] + half[0], "c", [(0, 1), (1, 0)])
    rest = pl.pallas_call(
        term_kernel,
        out_shape=pltpu.VMEM((2, 16, LANES), f32),
        in_specs=[vmem] * 5,
        out_specs=vmem,
        scratch_shapes=[pltpu.VMEM((3, LANES, LANES), f32), pltpu.VMEM((2, 64, LANES), f32)],
        compiler_params=params(4),
        cost_estimate=pl.CostEstimate(flops=1 << 22, bytes_accessed=1 << 18, transcendentals=1 << 11),
        name="slab_term",
    )(pos, section, near, pair, det)

    return pl.pallas_call(
        finish_kernel,
        out_shape=(jax.ShapeDtypeStruct(base.shape, f32),) * 2,
        compiler_params=params(4),
        cost_estimate=pl.CostEstimate(flops=1 << 16, bytes_accessed=1 << 18, transcendentals=0),
        name="finish_rate",
    )(keep, half, core, rest, section, base, accum)


def solution(mesh):
    fine = Mesh(mesh.devices.reshape(4, 4, 2, 2, 4), ("y", "x", "zh", "c", "zl"))
    rows = ("y", "x", "zh", "c")
    slab = P(None, "zl", rows)
    return jax.shard_map(
        local,
        mesh=fine,
        in_specs=(P(), P(), P(rows), slab, slab, slab),
        out_specs=(slab, slab),
        check_vma=False,
    )
```

```python
import functools
import math

import jax
import jax.numpy as jnp
from jax import lax
from jax.experimental import pallas as pl
from jax.experimental.pallas import tpu as pltpu
from jax.sharding import Mesh
from jax.sharding import PartitionSpec as P

TIME_STEP = 0.2
LANES = 128
COS = (0.9999992211, -19.73898242, 64.92872338, -85.27236068, 58.79387231, -21.07651549)
SIN = (6.283182817, -41.3414213, 81.59618177, -76.58008122, 41.20531753, -12.27114973)
SCALE = -0.75 / (2.0 * math.pi)
INV_WAVE = 1.0 / (2.0 * math.pi)
ROUNDER = 12582912.0
PART = 40
WIDE = 48


def horner(coefs, scale, arg):
    total = jnp.float32(coefs[-1] * scale)
    for c in coefs[-2::-1]:
        total = total * arg + jnp.float32(c * scale)
    return total


def coupling(dx, dy, dz):
    dz_sq = dz * dz
    dist_sq = dx * dx + dy * dy + dz_sq
    inv = lax.rsqrt(dist_sq)
    dist = dist_sq * inv
    turn = dist - ((dist + ROUNDER) - ROUNDER)
    turn_sq = turn * turn
    cosine = horner(COS, SCALE, turn_sq)
    sine = horner(SIN, SCALE, turn_sq) * turn
    inv_sq = inv * inv
    aligned = dz_sq * inv_sq
    quad_imag = inv_sq * (INV_WAVE - (3.0 * INV_WAVE) * aligned)
    quad_real = inv * ((1.0 - aligned) - INV_WAVE * quad_imag)
    return cosine * quad_real - sine * quad_imag, sine * quad_real + cosine * quad_imag


def split(value):
    high = value.astype(jnp.bfloat16)
    low = (value - high.astype(jnp.float32)).astype(jnp.bfloat16)
    return high, low


def lanes_at(index):
    return pl.ds(pl.multiple_of(index * LANES, LANES), LANES)


def place_of(dx, dy):
    y = lax.rem(lax.axis_index("y") + 4 - dy, 4)
    x = lax.rem(lax.axis_index("x") + 4 - dx, 4)
    return y * 4 + x


def own_place():
    return lax.axis_index("y") * 4 + lax.axis_index("x")


def pack_kernel(section_ref, pops_ref, pos_ref, det_ref, block_ref, pos_out, det_out, high_ref, low_ref, row_ref, sems):
    own = own_place() * 4 + lax.axis_index("zh") * 2 + lax.axis_index("c")
    moves = [
        pltpu.make_async_copy(section_ref.at[0], block_ref.at[pl.ds(0, 16)], sems.at[0]),
        pltpu.make_async_copy(section_ref.at[1], block_ref.at[pl.ds(16, 16)], sems.at[1]),
        pltpu.make_async_copy(pops_ref, block_ref.at[pl.ds(32, 1)], sems.at[2]),
        pltpu.make_async_copy(pos_ref, pos_out, sems.at[3]),
        pltpu.make_async_copy(det_ref.at[:, lanes_at(own)], det_out.at[pl.ds(0, 1)], sems.at[4]),
        pltpu.make_async_copy(det_ref.at[:, pl.ds(0, LANES)], det_out.at[pl.ds(1, 1)], sems.at[5]),
    ]
    for move in moves:
        move.start()
    for move in moves:
        move.wait()
    top = lax.broadcasted_iota(jnp.int32, (8, LANES), 0) == 0
    block_ref[32:PART, :] = jnp.where(top, 2.0 * block_ref[32:PART, :] - 1.0, 0.0)


    @pl.when(ahead() == 1)
    def _():
        fill_rows(pos_out, row_ref)
        fill_unit(0, pos_out, row_ref, high_ref, low_ref)


def halves_kernel(own_ref, other_ref, after_ref, both_ref, token_ref):
    both_ref[0] = own_ref[...]
    both_ref[1] = other_ref[...]
    token_ref[...] = own_ref[0:8, :]


def lines_kernel(zero_ref, one_ref, two_ref, three_ref, slab_ref, near_ref, after_ref, all_ref, pair_ref, token_ref):
    for n, ref in enumerate((zero_ref, one_ref, two_ref, three_ref)):
        all_ref[n] = ref[...]
    pair_ref[0] = slab_ref[...]
    pair_ref[1] = near_ref[...]
    token_ref[...] = zero_ref[0, 0:8, :]


def turned(pos_ref, k, index):
    line = pos_ref[k : k + 1, lanes_at(index)]
    return jnp.broadcast_to(line, (LANES, LANES)).T


def ahead():
    return (1 - lax.axis_index("zh")) * (lax.axis_index("zl") < 2).astype(jnp.int32)


def fill_rows(pos_ref, row_ref):
    half, core = lax.axis_index("zh"), lax.axis_index("c")
    for n, quad in enumerate((half * 2 + 1 - core, half * 2 + core)):
        for k in range(3):
            row_ref[k, n * LANES : (n + 1) * LANES, :] = turned(pos_ref, k, own_place() * 4 + quad)


def fill_unit(unit, pos_ref, row_ref, high_ref, low_ref):
    half, core = lax.axis_index("zh"), lax.axis_index("c")
    quad = (half if unit < 2 else 1 - half) * 2 + core

    def tile(step, carry):
        at = lanes_at(place_of(2 * (unit % 2) + lax.div(step, 4), lax.rem(step, 4)) * 4 + quad)
        cols = [pos_ref[k : k + 1, at] for k in range(3)]
        for n in range(0, 2 * LANES, 32):
            dx, dy, dz = [row_ref[k, n : n + 32, :] - cols[k] for k in range(3)]
            for part, value in enumerate(coupling(dx, dy, dz)):
                high, low = split(value)
                lanes = lanes_at(step + part * 8)
                high_ref[n : n + 32, lanes] = high
                low_ref[n : n + 32, lanes] = low
        return carry

    lax.fori_loop(0, 8, tile, 0)
    if unit > 0:
        return
    eye = lax.broadcasted_iota(jnp.int32, (LANES, LANES), 0) == lax.broadcasted_iota(jnp.int32, (LANES, LANES), 1)
    for part in range(2):
        lanes = slice(part * 8 * LANES, (part * 8 + 1) * LANES)
        for ref in (high_ref, low_ref):
            own = ref[LANES:, lanes].astype(jnp.float32)
            ref[LANES:, lanes] = jnp.where(eye, 0.0, own).astype(jnp.bfloat16)


def near_kernel(pos_ref, high0_ref, low0_ref, high1_ref, low1_ref, row_ref):
    fill_rows(pos_ref, row_ref)
    fill_unit(1, pos_ref, row_ref, high1_ref, low1_ref)

    @pl.when(ahead() == 0)
    def _():
        fill_unit(0, pos_ref, row_ref, high0_ref, low0_ref)


def far_kernel(unit, pos_ref, row_ref, token_ref, high_ref, low_ref):
    fill_unit(unit, pos_ref, row_ref, high_ref, low_ref)


def term_kernel(pos_ref, slab_ref, near_ref, pair_ref, det_ref, rest_ref, row_ref, full_ref):
    own = lax.axis_index("zl")
    start = pl.multiple_of(own * 16, 16)
    offsets = []
    for k in range(3):
        row_ref[k] = turned(pos_ref, k, 0)
        offsets.append(row_ref[k, pl.ds(start, 16), :] - pos_ref[k : k + 1, 0:LANES])
    w_real, w_imag = coupling(*offsets)
    eye = (lax.broadcasted_iota(jnp.int32, (16, LANES), 0) + start) == lax.broadcasted_iota(jnp.int32, (16, LANES), 1)
    w_real = jnp.where(eye, det_ref[1:2, :], w_real)[:, 0:64]
    w_imag = jnp.where(eye, -0.5, w_imag)[:, 0:64]
    for n, ref in enumerate((slab_ref, near_ref, pair_ref.at[0], pair_ref.at[1])):
        place = own + (n % 2) * (1 - 2 * (own % 2))
        place = place + (n // 2) * (2 - 4 * (own // 2))
        there = pl.ds(pl.multiple_of(place * 16, 16), 16)
        full_ref[0, there, :] = ref[0]
        full_ref[1, there, :] = ref[1]

    def mul(a, b):
        return jnp.dot(a, b, precision=lax.Precision.HIGHEST, preferred_element_type=jnp.float32)

    v_real = mul(w_real, full_ref[0]) + mul(w_imag, full_ref[1])
    v_imag = mul(w_real, full_ref[1]) - mul(w_imag, full_ref[0])
    y_real, y_imag = slab_ref[0], slab_ref[1]
    line = det_ref[0:1, :]
    rest_ref[0] = line * y_imag - 0.5 * y_real - v_imag
    rest_ref[1] = v_real - line * y_real - 0.5 * y_imag


def early_own():
    return (1 - lax.axis_index("zh")) * (lax.axis_index("zl") < 2).astype(jnp.int32)


def fill_slab(unit, refs, y_ref):
    zeros = jnp.zeros((16, LANES), jnp.float32)
    for step in range(8):
        block = refs[2 * (unit % 2) + step // 4][step % 4, unit // 2]
        pops = jnp.concatenate([block[32:40], zeros[0:8]], axis=0)
        lanes = slice(step * LANES, (step + 1) * LANES)
        for n, value in enumerate((block[0:16], block[16:32], pops)):
            high, low = split(value)
            y_ref[n * 16 : n * 16 + 16, lanes] = high
            y_ref[WIDE + n * 16 : WIDE + n * 16 + 16, lanes] = low
        y_ref[2 * WIDE :, lanes] = jnp.zeros((LANES - 2 * WIDE, LANES), jnp.bfloat16)


def dot_slab(tiles, y):
    return lax.dot_general(tiles, y, (((1,), (1,)), ((), ())), preferred_element_type=jnp.float32)


def store_products(by_real, by_imag, out_ref, at):
    for n in range(by_real.shape[0] // LANES):
        rows = slice(n * LANES, (n + 1) * LANES)
        real, imag = by_real[rows, :].T, by_imag[rows, :].T
        real = real[0:PART] + real[WIDE : WIDE + PART]
        imag = imag[0:32] + imag[WIDE : WIDE + 32]
        out_ref[at + n, 0:16, :] = real[0:16] - imag[16:32]
        out_ref[at + n, 16:32, :] = real[16:32] + imag[0:16]
        out_ref[at + n, 32:PART, :] = real[32:PART]


def products(high_ref, low_ref, y):
    half = high_ref.shape[1] // 2
    by_real = dot_slab(high_ref[:, 0:half], y) + dot_slab(low_ref[:, 0:half], y)
    by_imag = dot_slab(high_ref[:, half:], y) + dot_slab(low_ref[:, half:], y)
    return by_real, by_imag


def product_kernel(early_high, early_low, high0, low0, high1, low1, high2, low2, high3, low3, all0, all1, all2, all3, out_ref, y_ref, real_ref, imag_ref):
    refs = (all0, all1, all2, all3)
    for unit in range(4):
        fill_slab(unit, refs, y_ref.at[unit])

    @pl.when(ahead() == 1)
    def _():
        real_ref[...], imag_ref[...] = products(early_high, early_low, y_ref[0])

    @pl.when(ahead() == 0)
    def _():
        real_ref[...], imag_ref[...] = products(high0, low0, y_ref[0])

    by_real, by_imag = real_ref[...], imag_ref[...]
    for unit, (high, low) in ((1, (high1, low1)), (2, (high2, low2)), (3, (high3, low3))):
        more_real, more_imag = products(high, low, y_ref[unit])
        by_real, by_imag = by_real + more_real, by_imag + more_imag
    store_products(by_real, by_imag, out_ref, 0)


def finish_kernel(keep_ref, core_ref, rest_ref, slab_ref, base_ref, accum_ref, next_ref, acc_ref):
    z = keep_ref[1] + core_ref[...]
    shift = z[32:33]
    rate_real = z[16:32] + shift * slab_ref[1] + rest_ref[0]
    rate_imag = rest_ref[1] - z[0:16] - shift * slab_ref[0]
    for n, rate in enumerate((rate_real, rate_imag)):
        next_ref[n] = base_ref[n] + (0.5 * TIME_STEP) * rate
        acc_ref[n] = accum_ref[n] + (TIME_STEP / 3.0) * rate


def params(mib):
    return pltpu.CompilerParams(vmem_limit_bytes=mib << 20)


def in_hbm(array):
    return pltpu.with_memory_space_constraint(array, pltpu.HBM)


def local(positions, detuning, populations, base, section, accum):
    bf16, f32 = jnp.bfloat16, jnp.float32
    count = positions.shape[1]
    hbm, vmem = pl.BlockSpec(memory_space=pltpu.HBM), pl.BlockSpec(memory_space=pltpu.VMEM)
    anywhere = pl.BlockSpec(memory_space=pl.ANY)
    unit = pltpu.VMEM((2 * LANES, 16 * LANES), bf16)
    token = pltpu.VMEM((8, LANES), f32)
    rows = pltpu.VMEM((3, 2 * LANES, LANES), f32)

    def call(kernel, name, out_shape, in_specs, flops, scratch=()):
        return pl.pallas_call(
            kernel,
            out_shape=out_shape,
            in_specs=in_specs,
            out_specs=[vmem] * len(out_shape),
            scratch_shapes=scratch,
            compiler_params=params(6),
            cost_estimate=pl.CostEstimate(flops=flops, bytes_accessed=1 << 20, transcendentals=0),
            name=name,
        )

    block, pos, det, early_high, early_low = call(
        pack_kernel,
        "pack_block",
        (pltpu.VMEM((PART, LANES), f32), pltpu.VMEM(positions.shape, f32), token, unit, unit),
        [hbm] * 4,
        1 << 16,
        [rows, pltpu.SemaphoreType.DMA((6,))],
    )(in_hbm(section), in_hbm(populations.reshape(1, LANES)), in_hbm(positions), in_hbm(detuning.reshape(1, count)))
    other = lax.ppermute(block, "zh", [(0, 1), (1, 0)])
    near = lax.ppermute(section, "zl", [(i, i ^ 1) for i in range(4)])
    high0, low0, high1, low1, row = call(
        near_kernel, "near_tiles", (unit, unit, unit, unit, rows), [vmem], 30 << 20
    )(pos)

    both, second = call(
        halves_kernel, "join_halves", (pltpu.VMEM((2, PART, LANES), f32), token), [vmem, vmem, anywhere], 1
    )(block, other, high1)
    along_y = [lax.ppermute(both, "y", [(i, (i + d) % 4) for i in range(4)]) for d in (2, 1, 3)]
    high2, low2 = call(
        functools.partial(far_kernel, 2), "far_tiles_a", (unit, unit), [vmem, vmem, anywhere], 15 << 20
    )(pos, row, second)

    lines, pair, third = call(
        lines_kernel,
        "join_lines",
        (pltpu.VMEM((4, 2, PART, LANES), f32), pltpu.VMEM((2, 2, 16, LANES), f32), token),
        [vmem] * 6 + [anywhere],
        1,
    )(both, along_y[1], along_y[0], along_y[2], section, near, high2)
    along_x = [lax.ppermute(lines, "x", [(i, (i + d) % 4) for i in range(4)]) for d in (2, 1, 3)]
    pair = lax.ppermute(pair, "zl", [(i, i ^ 2) for i in range(4)])
    high3, low3 = call(
        functools.partial(far_kernel, 3), "far_tiles_b", (unit, unit), [vmem, vmem, anywhere], 15 << 20
    )(pos, row, third)

    (keep,) = call(
        product_kernel,
        "tile_products",
        (pltpu.VMEM((2, PART, LANES), f32),),
        [vmem] * 14,
        1 << 30,
        [
            pltpu.VMEM((4, LANES, 8 * LANES), bf16),
            pltpu.VMEM((2 * LANES, LANES), f32),
            pltpu.VMEM((2 * LANES, LANES), f32),
        ],
    )(early_high, early_low, high0, low0, high1, low1, high2, low2, high3, low3, lines, along_x[1], along_x[0], along_x[2])
    core = lax.ppermute(keep[0], "c", [(0, 1), (1, 0)])
    rest = pl.pallas_call(
        term_kernel,
        out_shape=pltpu.VMEM((2, 16, LANES), f32),
        in_specs=[vmem] * 5,
        out_specs=vmem,
        scratch_shapes=[pltpu.VMEM((3, LANES, LANES), f32), pltpu.VMEM((2, 64, LANES), f32)],
        compiler_params=params(4),
        cost_estimate=pl.CostEstimate(flops=1 << 22, bytes_accessed=1 << 18, transcendentals=1 << 11),
        name="slab_term",
    )(pos, section, near, pair, det)

    return pl.pallas_call(
        finish_kernel,
        out_shape=(jax.ShapeDtypeStruct(base.shape, f32),) * 2,
        compiler_params=params(4),
        cost_estimate=pl.CostEstimate(flops=1 << 16, bytes_accessed=1 << 18, transcendentals=0),
        name="finish_rate",
    )(keep, core, rest, section, base, accum)


def solution(mesh):
    fine = Mesh(mesh.devices.reshape(4, 4, 2, 2, 4), ("y", "x", "zh", "c", "zl"))
    rows = ("y", "x", "zh", "c")
    slab = P(None, "zl", rows)
    return jax.shard_map(
        local,
        mesh=fine,
        in_specs=(P(), P(), P(rows), slab, slab, slab),
        out_specs=(slab, slab),
        check_vma=False,
    )
```

```python
import functools
import math

import jax
import jax.numpy as jnp
from jax import lax
from jax.experimental import pallas as pl
from jax.experimental.pallas import tpu as pltpu
from jax.sharding import Mesh
from jax.sharding import PartitionSpec as P

TIME_STEP = 0.2
LANES = 128
COS = (0.9999992211, -19.73898242, 64.92872338, -85.27236068, 58.79387231, -21.07651549)
SIN = (6.283182817, -41.3414213, 81.59618177, -76.58008122, 41.20531753, -12.27114973)
SCALE = -0.75 / (2.0 * math.pi)
INV_WAVE = 1.0 / (2.0 * math.pi)
ROUNDER = 12582912.0
PART = 40
WIDE = 48


def horner(coefs, scale, arg):
    total = jnp.float32(coefs[-1] * scale)
    for c in coefs[-2::-1]:
        total = total * arg + jnp.float32(c * scale)
    return total


def coupling(dx, dy, dz):
    dz_sq = dz * dz
    dist_sq = dx * dx + dy * dy + dz_sq
    inv = lax.rsqrt(dist_sq)
    dist = dist_sq * inv
    turn = dist - ((dist + ROUNDER) - ROUNDER)
    turn_sq = turn * turn
    cosine = horner(COS, SCALE, turn_sq)
    sine = horner(SIN, SCALE, turn_sq) * turn
    inv_sq = inv * inv
    aligned = dz_sq * inv_sq
    quad_imag = inv_sq * (INV_WAVE - (3.0 * INV_WAVE) * aligned)
    quad_real = inv * ((1.0 - aligned) - INV_WAVE * quad_imag)
    return cosine * quad_real - sine * quad_imag, sine * quad_real + cosine * quad_imag


def split(value):
    high = value.astype(jnp.bfloat16)
    low = (value - high.astype(jnp.float32)).astype(jnp.bfloat16)
    return high, low


def lanes_at(index):
    return pl.ds(pl.multiple_of(index * LANES, LANES), LANES)


def place_of(step):
    down, across = lax.rem(step, 4), lax.div(step, 4)
    y = lax.axis_index("y") ^ down ^ lax.div(down, 2)
    x = lax.axis_index("x") ^ across ^ lax.div(across, 2)
    return y * 4 + x


def own_place():
    return lax.axis_index("y") * 4 + lax.axis_index("x")


def pack_kernel(section_ref, pops_ref, pos_ref, det_ref, block_ref, pos_out, det_out, sems):
    own = own_place() * 4 + lax.axis_index("zh") * 2 + lax.axis_index("c")
    moves = [
        pltpu.make_async_copy(section_ref.at[0], block_ref.at[pl.ds(0, 16)], sems.at[0]),
        pltpu.make_async_copy(section_ref.at[1], block_ref.at[pl.ds(16, 16)], sems.at[1]),
        pltpu.make_async_copy(pops_ref, block_ref.at[pl.ds(32, 1)], sems.at[2]),
        pltpu.make_async_copy(pos_ref, pos_out, sems.at[3]),
        pltpu.make_async_copy(det_ref.at[:, lanes_at(own)], det_out.at[pl.ds(0, 1)], sems.at[4]),
        pltpu.make_async_copy(det_ref.at[:, pl.ds(0, LANES)], det_out.at[pl.ds(1, 1)], sems.at[5]),
    ]
    for move in moves:
        move.start()
    for move in moves:
        move.wait()
    top = lax.broadcasted_iota(jnp.int32, (8, LANES), 0) == 0
    block_ref[32:PART, :] = jnp.where(top, 2.0 * block_ref[32:PART, :] - 1.0, 0.0)


def pair_kernel(block_ref, one_ref, after_ref, both_ref, token_ref):
    both_ref[0] = block_ref[...]
    both_ref[1] = one_ref[...]
    token_ref[...] = block_ref[0:8, :]


def line_kernel(both_ref, two_ref, slab_ref, near_ref, after_ref, all_ref, pair_ref, token_ref):
    all_ref[0:2] = both_ref[...]
    all_ref[2:4] = two_ref[...]
    pair_ref[0] = slab_ref[...]
    pair_ref[1] = near_ref[...]
    token_ref[...] = both_ref[0, 0:8, :]


def turned(pos_ref, k, index):
    line = pos_ref[k : k + 1, lanes_at(index)]
    return jnp.broadcast_to(line, (LANES, LANES)).T


def fill_tiles(pos_ref, row_ref, high_ref, low_ref, quads, first, count):
    quad = lax.axis_index("zh") * 2 + lax.axis_index("c")
    place = own_place()
    tiles = pos_ref.shape[1] // (4 * LANES)
    for n, other in enumerate(quads):
        for k in range(3):
            row_ref[k, n * LANES : (n + 1) * LANES, :] = turned(pos_ref, k, place * 4 + other)

    def tile(step, carry):
        at = lanes_at(place_of(step) * 4 + quad)
        cols = [pos_ref[k : k + 1, at] for k in range(3)]
        for n in range(0, count, 32):
            size = min(32, count - n)
            dx, dy, dz = [row_ref[k, first + n : first + n + size, :] - cols[k] for k in range(3)]
            for part, value in enumerate(coupling(dx, dy, dz)):
                high, low = split(value)
                lanes = lanes_at(step + part * tiles)
                high_ref[n : n + size, lanes] = high
                low_ref[n : n + size, lanes] = low
        return carry

    lax.fori_loop(0, tiles, tile, 0)


def term_kernel(pos_ref, slab_ref, near_ref, pair_ref, det_ref, rest_ref, row_ref, full_ref):
    own = lax.axis_index("zl")
    start = pl.multiple_of(own * 16, 16)
    offsets = []
    for k in range(3):
        row_ref[k] = turned(pos_ref, k, 0)
        offsets.append(row_ref[k, pl.ds(start, 16), :] - pos_ref[k : k + 1, 0:LANES])
    w_real, w_imag = coupling(*offsets)
    eye = (lax.broadcasted_iota(jnp.int32, (16, LANES), 0) + start) == lax.broadcasted_iota(jnp.int32, (16, LANES), 1)
    w_real = jnp.where(eye, det_ref[1:2, :], w_real)[:, 0:64]
    w_imag = jnp.where(eye, -0.5, w_imag)[:, 0:64]
    for n, ref in enumerate((slab_ref, near_ref, pair_ref.at[0], pair_ref.at[1])):
        place = own + (n % 2) * (1 - 2 * (own % 2))
        place = place + (n // 2) * (2 - 4 * (own // 2))
        there = pl.ds(pl.multiple_of(place * 16, 16), 16)
        full_ref[0, there, :] = ref[0]
        full_ref[1, there, :] = ref[1]

    def mul(a, b):
        return jnp.dot(a, b, precision=lax.Precision.HIGHEST, preferred_element_type=jnp.float32)

    v_real = mul(w_real, full_ref[0]) + mul(w_imag, full_ref[1])
    v_imag = mul(w_real, full_ref[1]) - mul(w_imag, full_ref[0])
    y_real, y_imag = slab_ref[0], slab_ref[1]
    line = det_ref[0:1, :]
    rest_ref[0] = line * y_imag - 0.5 * y_real - v_imag
    rest_ref[1] = v_real - line * y_real - 0.5 * y_imag


def fill_own(pos_ref, row_ref, high_ref, low_ref):
    tiles = pos_ref.shape[1] // (4 * LANES)
    quad = lax.axis_index("zh") * 2 + lax.axis_index("c")
    fill_tiles(pos_ref, row_ref, high_ref, low_ref, (quad,), 0, LANES)
    eye = lax.broadcasted_iota(jnp.int32, (LANES, LANES), 0) == lax.broadcasted_iota(jnp.int32, (LANES, LANES), 1)
    for part in range(2):
        lanes = pl.ds(part * tiles * LANES, LANES)
        for ref in (high_ref, low_ref):
            ref[:, lanes] = jnp.where(eye, 0.0, ref[:, lanes].astype(jnp.float32)).astype(jnp.bfloat16)


def block_kernel(far, pos_ref, token_ref, high_ref, low_ref, row_ref):
    half, core = lax.axis_index("zh"), lax.axis_index("c")
    quad = ((1 - half) * 2 + 1 - core, (1 - half) * 2 + core, half * 2 + 1 - core)[far]
    fill_tiles(pos_ref, row_ref, high_ref, low_ref, (quad,), 0, LANES)


def fill_slab(refs, y_ref):
    zeros = jnp.zeros((16, LANES), jnp.float32)
    for step in range(16):
        block = refs[step // 4][step % 4]
        pops = jnp.concatenate([block[32:40], zeros[0:8]], axis=0)
        lanes = slice(step * LANES, (step + 1) * LANES)
        for n, value in enumerate((block[0:16], block[16:32], pops)):
            high, low = split(value)
            y_ref[n * 16 : n * 16 + 16, lanes] = high
            y_ref[WIDE + n * 16 : WIDE + n * 16 + 16, lanes] = low
        y_ref[2 * WIDE :, lanes] = jnp.zeros((LANES - 2 * WIDE, LANES), jnp.bfloat16)


def dot_slab(tiles, y):
    return lax.dot_general(tiles, y, (((1,), (1,)), ((), ())), preferred_element_type=jnp.float32)


def store_products(by_real, by_imag, out_ref, at):
    for n in range(by_real.shape[0] // LANES):
        rows = slice(n * LANES, (n + 1) * LANES)
        real, imag = by_real[rows, :].T, by_imag[rows, :].T
        real = real[0:PART] + real[WIDE : WIDE + PART]
        imag = imag[0:32] + imag[WIDE : WIDE + 32]
        out_ref[at + n, 0:16, :] = real[0:16] - imag[16:32]
        out_ref[at + n, 16:32, :] = real[16:32] + imag[0:16]
        out_ref[at + n, 32:PART, :] = real[32:PART]


def products(high_ref, low_ref, y):
    half = high_ref.shape[1] // 2
    by_real = dot_slab(high_ref[:, 0:half], y) + dot_slab(low_ref[:, 0:half], y)
    by_imag = dot_slab(high_ref[:, half:], y) + dot_slab(low_ref[:, half:], y)
    return by_real, by_imag


def send_kernel(high0, low0, high1, low1, all0, all1, all2, all3, out_ref, y_ref):
    fill_slab((all0, all1, all2, all3), y_ref)
    y = y_ref[...]
    store_products(*products(high0, low0, y), out_ref, 0)
    store_products(*products(high1, low1, y), out_ref, 1)


def keep_kernel(pos_ref, y_ref, high2, low2, out_ref, row_ref, high_ref, low_ref):
    fill_own(pos_ref, row_ref, high_ref, low_ref)
    y = y_ref[...]
    store_products(*products(high2, low2, y), out_ref, 0)
    store_products(*products(high_ref, low_ref, y), out_ref, 1)


def finish_kernel(keep_ref, half_ref, core_ref, rest_ref, slab_ref, base_ref, accum_ref, next_ref, acc_ref):
    z = keep_ref[1] + half_ref[1] + core_ref[...]
    shift = z[32:33]
    rate_real = z[16:32] + shift * slab_ref[1] + rest_ref[0]
    rate_imag = rest_ref[1] - z[0:16] - shift * slab_ref[0]
    for n, rate in enumerate((rate_real, rate_imag)):
        next_ref[n] = base_ref[n] + (0.5 * TIME_STEP) * rate
        acc_ref[n] = accum_ref[n] + (TIME_STEP / 3.0) * rate


def params(mib):
    return pltpu.CompilerParams(vmem_limit_bytes=mib << 20)


def in_hbm(array):
    return pltpu.with_memory_space_constraint(array, pltpu.HBM)


def local(positions, detuning, populations, base, section, accum):
    bf16, f32 = jnp.bfloat16, jnp.float32
    count = positions.shape[1]
    tiles = count // (4 * LANES)
    deep = 2 * tiles * LANES
    hbm, vmem = pl.BlockSpec(memory_space=pltpu.HBM), pl.BlockSpec(memory_space=pltpu.VMEM)
    anywhere = pl.BlockSpec(memory_space=pl.ANY)
    tile = pltpu.VMEM((LANES, deep), bf16)
    token = pltpu.VMEM((8, LANES), f32)
    rows = pltpu.VMEM((3, LANES, LANES), f32)

    def call(kernel, name, out_shape, in_specs, flops, scratch=()):
        return pl.pallas_call(
            kernel,
            out_shape=out_shape,
            in_specs=in_specs,
            out_specs=[vmem] * len(out_shape),
            scratch_shapes=scratch,
            compiler_params=params(6),
            cost_estimate=pl.CostEstimate(flops=flops, bytes_accessed=1 << 20, transcendentals=0),
            name=name,
        )

    def swap(array, axis, mask):
        size = lax.axis_size(axis)
        return lax.ppermute(array, axis, [(i, i ^ mask) for i in range(size)])

    def far_block(n, after):
        kernel = functools.partial(block_kernel, n)
        return call(kernel, "far_block_" + "abc"[n], (tile, tile), [vmem, anywhere], 1 << 24, [rows])(pos, after)

    block, pos, det = call(
        pack_kernel,
        "pack_block",
        (pltpu.VMEM((PART, LANES), f32), pltpu.VMEM(positions.shape, f32), token),
        [hbm] * 4,
        1 << 16,
        [pltpu.SemaphoreType.DMA((6,))],
    )(in_hbm(section), in_hbm(populations.reshape(1, LANES)), in_hbm(positions), in_hbm(detuning.reshape(1, count)))
    one = swap(block, "y", 1)
    near = swap(section, "zl", 1)
    high0, low0 = far_block(0, det)

    both, second = call(
        pair_kernel, "join_pair", (pltpu.VMEM((2, PART, LANES), f32), token), [vmem, vmem, anywhere], 1
    )(block, one, high0)
    two = swap(both, "y", 3)
    high1, low1 = far_block(1, second)

    line, pair, third = call(
        line_kernel,
        "join_line",
        (pltpu.VMEM((4, PART, LANES), f32), pltpu.VMEM((2, 2, 16, LANES), f32), token),
        [vmem] * 4 + [anywhere],
        1,
    )(both, two, section, near, high1)
    across = [swap(line, "x", mask) for mask in (1, 3, 2)]
    pair = swap(pair, "zl", 2)
    high2, low2 = far_block(2, third)

    sent, y = call(
        send_kernel,
        "send_products",
        (pltpu.VMEM((2, PART, LANES), f32), pltpu.VMEM((LANES, deep // 2), bf16)),
        [vmem] * 8,
        1 << 29,
    )(high0, low0, high1, low1, line, *across)
    half = swap(sent, "zh", 1)

    (keep,) = call(
        keep_kernel, "keep_products", (pltpu.VMEM((2, PART, LANES), f32),), [vmem] * 4, 1 << 29, [rows, tile, tile]
    )(pos, y, high2, low2)
    core = lax.ppermute(keep[0] + half[0], "c", [(0, 1), (1, 0)])
    rest = pl.pallas_call(
        term_kernel,
        out_shape=pltpu.VMEM((2, 16, LANES), f32),
        in_specs=[vmem] * 5,
        out_specs=vmem,
        scratch_shapes=[pltpu.VMEM((3, LANES, LANES), f32), pltpu.VMEM((2, 64, LANES), f32)],
        compiler_params=params(4),
        cost_estimate=pl.CostEstimate(flops=1 << 22, bytes_accessed=1 << 18, transcendentals=1 << 11),
        name="slab_term",
    )(pos, section, near, pair, det)

    return pl.pallas_call(
        finish_kernel,
        out_shape=(jax.ShapeDtypeStruct(base.shape, f32),) * 2,
        compiler_params=params(4),
        cost_estimate=pl.CostEstimate(flops=1 << 16, bytes_accessed=1 << 18, transcendentals=0),
        name="finish_rate",
    )(keep, half, core, rest, section, base, accum)


def solution(mesh):
    fine = Mesh(mesh.devices.reshape(4, 4, 2, 2, 4), ("y", "x", "zh", "c", "zl"))
    rows = ("y", "x", "zh", "c")
    slab = P(None, "zl", rows)
    return jax.shard_map(
        local,
        mesh=fine,
        in_specs=(P(), P(), P(rows), slab, slab, slab),
        out_specs=(slab, slab),
        check_vma=False,
    )
```

```python
import functools
import math

import jax
import jax.numpy as jnp
from jax import lax
from jax.experimental import pallas as pl
from jax.experimental.pallas import tpu as pltpu
from jax.sharding import Mesh
from jax.sharding import PartitionSpec as P

TIME_STEP = 0.2
LANES = 128
COS = (0.9999992211, -19.73898242, 64.92872338, -85.27236068, 58.79387231, -21.07651549)
SIN = (6.283182817, -41.3414213, 81.59618177, -76.58008122, 41.20531753, -12.27114973)
SCALE = -0.75 / (2.0 * math.pi)
INV_WAVE = 1.0 / (2.0 * math.pi)
ROUNDER = 12582912.0
PART = 40
WIDE = 48


def horner(coefs, scale, arg):
    total = jnp.float32(coefs[-1] * scale)
    for c in coefs[-2::-1]:
        total = total * arg + jnp.float32(c * scale)
    return total


def coupling(dx, dy, dz):
    dz_sq = dz * dz
    dist_sq = dx * dx + dy * dy + dz_sq
    inv = lax.rsqrt(dist_sq)
    dist = dist_sq * inv
    turn = dist - ((dist + ROUNDER) - ROUNDER)
    turn_sq = turn * turn
    cosine = horner(COS, SCALE, turn_sq)
    sine = horner(SIN, SCALE, turn_sq) * turn
    inv_sq = inv * inv
    aligned = dz_sq * inv_sq
    quad_imag = inv_sq * (INV_WAVE - (3.0 * INV_WAVE) * aligned)
    quad_real = inv * ((1.0 - aligned) - INV_WAVE * quad_imag)
    return cosine * quad_real - sine * quad_imag, sine * quad_real + cosine * quad_imag


def split(value):
    high = value.astype(jnp.bfloat16)
    low = (value - high.astype(jnp.float32)).astype(jnp.bfloat16)
    return high, low


def lanes_at(index):
    return pl.ds(pl.multiple_of(index * LANES, LANES), LANES)


def place_of(step):
    down, across = lax.rem(step, 4), lax.div(step, 4)
    y = lax.axis_index("y") ^ down ^ lax.div(down, 2)
    x = lax.axis_index("x") ^ across ^ lax.div(across, 2)
    return y * 4 + x


def own_place():
    return lax.axis_index("y") * 4 + lax.axis_index("x")


def pack_kernel(section_ref, pops_ref, pos_ref, det_ref, block_ref, pos_out, det_out, sems):
    own = own_place() * 4 + lax.axis_index("zh") * 2 + lax.axis_index("c")
    moves = [
        pltpu.make_async_copy(section_ref.at[0], block_ref.at[pl.ds(0, 16)], sems.at[0]),
        pltpu.make_async_copy(section_ref.at[1], block_ref.at[pl.ds(16, 16)], sems.at[1]),
        pltpu.make_async_copy(pops_ref, block_ref.at[pl.ds(32, 1)], sems.at[2]),
        pltpu.make_async_copy(pos_ref, pos_out, sems.at[3]),
        pltpu.make_async_copy(det_ref.at[:, lanes_at(own)], det_out.at[pl.ds(0, 1)], sems.at[4]),
        pltpu.make_async_copy(det_ref.at[:, pl.ds(0, LANES)], det_out.at[pl.ds(1, 1)], sems.at[5]),
    ]
    for move in moves:
        move.start()
    for move in moves:
        move.wait()
    top = lax.broadcasted_iota(jnp.int32, (8, LANES), 0) == 0
    block_ref[32:PART, :] = jnp.where(top, 2.0 * block_ref[32:PART, :] - 1.0, 0.0)


def pair_kernel(block_ref, one_ref, slab_ref, even_ref, after_ref, both_ref, cores_ref, token_ref):
    both_ref[0] = block_ref[...]
    both_ref[1] = one_ref[...]
    cores_ref[0] = even_ref[...]
    cores_ref[1] = slab_ref[...]
    token_ref[...] = block_ref[0:8, :]


def line_kernel(both_ref, two_ref, cores_ref, near_ref, after_ref, all_ref, pair_ref, token_ref):
    all_ref[0:2] = both_ref[...]
    all_ref[2:4] = two_ref[...]
    pair_ref[0] = cores_ref[...]
    pair_ref[1] = near_ref[...]
    token_ref[...] = both_ref[0, 0:8, :]


def turned(pos_ref, k, index):
    line = pos_ref[k : k + 1, lanes_at(index)]
    return jnp.broadcast_to(line, (LANES, LANES)).T


def fill_tiles(pos_ref, row_ref, high_ref, low_ref, quads, first, count):
    quad = lax.axis_index("zh") * 2 + lax.axis_index("c")
    place = own_place()
    tiles = pos_ref.shape[1] // (4 * LANES)
    for n, other in enumerate(quads):
        for k in range(3):
            row_ref[k, n * LANES : (n + 1) * LANES, :] = turned(pos_ref, k, place * 4 + other)

    def tile(step, carry):
        at = lanes_at(place_of(step) * 4 + quad)
        cols = [pos_ref[k : k + 1, at] for k in range(3)]
        for n in range(0, count, 32):
            size = min(32, count - n)
            dx, dy, dz = [row_ref[k, first + n : first + n + size, :] - cols[k] for k in range(3)]
            for part, value in enumerate(coupling(dx, dy, dz)):
                high, low = split(value)
                lanes = lanes_at(step + part * tiles)
                high_ref[n : n + size, lanes] = high
                low_ref[n : n + size, lanes] = low
        return carry

    lax.fori_loop(0, tiles, tile, 0)


def take_slab_term(pos_ref, pair_ref, far_ref, det_ref, out_ref, row_ref, full_ref):
    own = lax.axis_index("zl")
    start = pl.multiple_of(own * 16, 16)
    offsets = []
    for k in range(3):
        row_ref[k] = turned(pos_ref, k, 0)
        offsets.append(row_ref[k, pl.ds(start, 16), :] - pos_ref[k : k + 1, 0:LANES])
    w_real, w_imag = coupling(*offsets)
    eye = (lax.broadcasted_iota(jnp.int32, (16, LANES), 0) + start) == lax.broadcasted_iota(jnp.int32, (16, LANES), 1)
    w_real = jnp.where(eye, det_ref[1:2, :], w_real)[:, 0:64]
    w_imag = jnp.where(eye, -0.5, w_imag)[:, 0:64]
    for n in range(4):
        there = pl.ds(pl.multiple_of((own ^ n) * 16, 16), 16)
        source = (pair_ref, far_ref)[n // 2]
        for core in range(2):
            for part in range(2):
                full_ref[part, there, core * LANES : (core + 1) * LANES] = source[n % 2, core, part]

    def mul(a, b):
        return jnp.dot(a, b, precision=lax.Precision.HIGHEST, preferred_element_type=jnp.float32)

    v_real = mul(w_real, full_ref[0]) + mul(w_imag, full_ref[1])
    v_imag = mul(w_real, full_ref[1]) - mul(w_imag, full_ref[0])
    for core in range(2):
        lanes = slice(core * LANES, (core + 1) * LANES)
        out_ref[core, 0:16, :] -= v_real[:, lanes]
        out_ref[core, 16:32, :] -= v_imag[:, lanes]


def fill_own(pos_ref, row_ref, high_ref, low_ref):
    tiles = pos_ref.shape[1] // (4 * LANES)
    quad = lax.axis_index("zh") * 2 + lax.axis_index("c")
    fill_tiles(pos_ref, row_ref, high_ref, low_ref, (quad,), 0, LANES)
    eye = lax.broadcasted_iota(jnp.int32, (LANES, LANES), 0) == lax.broadcasted_iota(jnp.int32, (LANES, LANES), 1)
    for part in range(2):
        lanes = pl.ds(part * tiles * LANES, LANES)
        for ref in (high_ref, low_ref):
            ref[:, lanes] = jnp.where(eye, 0.0, ref[:, lanes].astype(jnp.float32)).astype(jnp.bfloat16)


def block_kernel(far, pos_ref, token_ref, high_ref, low_ref, row_ref):
    half, core = lax.axis_index("zh"), lax.axis_index("c")
    quad = ((1 - half) * 2 + 1 - core, (1 - half) * 2 + core, half * 2 + 1 - core)[far]
    fill_tiles(pos_ref, row_ref, high_ref, low_ref, (quad,), 0, LANES)


def fill_slab(refs, y_ref):
    zeros = jnp.zeros((16, LANES), jnp.float32)
    for step in range(16):
        block = refs[step // 4][step % 4]
        pops = jnp.concatenate([block[32:40], zeros[0:8]], axis=0)
        lanes = slice(step * LANES, (step + 1) * LANES)
        for n, value in enumerate((block[0:16], block[16:32], pops)):
            high, low = split(value)
            y_ref[n * 16 : n * 16 + 16, lanes] = high
            y_ref[WIDE + n * 16 : WIDE + n * 16 + 16, lanes] = low
        y_ref[2 * WIDE :, lanes] = jnp.zeros((LANES - 2 * WIDE, LANES), jnp.bfloat16)


def dot_slab(tiles, y):
    return lax.dot_general(tiles, y, (((1,), (1,)), ((), ())), preferred_element_type=jnp.float32)


def store_products(by_real, by_imag, out_ref, at):
    for n in range(by_real.shape[0] // LANES):
        rows = slice(n * LANES, (n + 1) * LANES)
        real, imag = by_real[rows, :].T, by_imag[rows, :].T
        real = real[0:PART] + real[WIDE : WIDE + PART]
        imag = imag[0:32] + imag[WIDE : WIDE + 32]
        out_ref[at + n, 0:16, :] = real[0:16] - imag[16:32]
        out_ref[at + n, 16:32, :] = real[16:32] + imag[0:16]
        out_ref[at + n, 32:PART, :] = real[32:PART]


def products(high_ref, low_ref, y):
    half = high_ref.shape[1] // 2
    by_real = dot_slab(high_ref[:, 0:half], y) + dot_slab(low_ref[:, 0:half], y)
    by_imag = dot_slab(high_ref[:, half:], y) + dot_slab(low_ref[:, half:], y)
    return by_real, by_imag


def send_kernel(high0, low0, high1, low1, all0, all1, all2, all3, out_ref, y_ref):
    fill_slab((all0, all1, all2, all3), y_ref)
    y = y_ref[...]
    store_products(*products(high0, low0, y), out_ref, 0)
    store_products(*products(high1, low1, y), out_ref, 1)


def keep_kernel(pos_ref, y_ref, high2, low2, pair_ref, far_ref, det_ref, out_ref, row_ref, high_ref, low_ref, full_ref):
    fill_own(pos_ref, row_ref, high_ref, low_ref)
    y = y_ref[...]
    store_products(*products(high2, low2, y), out_ref, 0)
    store_products(*products(high_ref, low_ref, y), out_ref, 1)

    @pl.when(lax.axis_index("c") == 1)
    def _():
        take_slab_term(pos_ref, pair_ref, far_ref, det_ref, out_ref, row_ref, full_ref)


def finish_kernel(keep_ref, half_ref, core_ref, det_ref, slab_ref, base_ref, accum_ref, next_ref, acc_ref):
    z = keep_ref[1] + half_ref[1] + core_ref[...]
    y_real, y_imag = slab_ref[0], slab_ref[1]
    level = det_ref[0:1, :] + z[32:33]
    rate_real = z[16:32] + level * y_imag - 0.5 * y_real
    rate_imag = -z[0:16] - level * y_real - 0.5 * y_imag
    for n, rate in enumerate((rate_real, rate_imag)):
        next_ref[n] = base_ref[n] + (0.5 * TIME_STEP) * rate
        acc_ref[n] = accum_ref[n] + (TIME_STEP / 3.0) * rate


def params(mib):
    return pltpu.CompilerParams(vmem_limit_bytes=mib << 20)


def in_hbm(array):
    return pltpu.with_memory_space_constraint(array, pltpu.HBM)


def local(positions, detuning, populations, base, section, accum):
    bf16, f32 = jnp.bfloat16, jnp.float32
    count = positions.shape[1]
    tiles = count // (4 * LANES)
    deep = 2 * tiles * LANES
    hbm, vmem = pl.BlockSpec(memory_space=pltpu.HBM), pl.BlockSpec(memory_space=pltpu.VMEM)
    anywhere = pl.BlockSpec(memory_space=pl.ANY)
    tile = pltpu.VMEM((LANES, deep), bf16)
    token = pltpu.VMEM((8, LANES), f32)
    rows = pltpu.VMEM((3, LANES, LANES), f32)

    def call(kernel, name, out_shape, in_specs, flops, scratch=()):
        return pl.pallas_call(
            kernel,
            out_shape=out_shape,
            in_specs=in_specs,
            out_specs=[vmem] * len(out_shape),
            scratch_shapes=scratch,
            compiler_params=params(6),
            cost_estimate=pl.CostEstimate(flops=flops, bytes_accessed=1 << 20, transcendentals=0),
            name=name,
        )

    def swap(array, axis, mask):
        size = lax.axis_size(axis)
        return lax.ppermute(array, axis, [(i, i ^ mask) for i in range(size)])

    def odd_swap(array, mask):
        return lax.ppermute(array, ("c", "zl"), [(4 + i, 4 + (i ^ mask)) for i in range(4)])

    def far_block(n, after):
        kernel = functools.partial(block_kernel, n)
        return call(kernel, "far_block_" + "abc"[n], (tile, tile), [vmem, anywhere], 1 << 24, [rows])(pos, after)

    block, pos, det = call(
        pack_kernel,
        "pack_block",
        (pltpu.VMEM((PART, LANES), f32), pltpu.VMEM(positions.shape, f32), token),
        [hbm] * 4,
        1 << 16,
        [pltpu.SemaphoreType.DMA((6,))],
    )(in_hbm(section), in_hbm(populations.reshape(1, LANES)), in_hbm(positions), in_hbm(detuning.reshape(1, count)))
    one = swap(block, "y", 1)
    even = lax.ppermute(section, "c", [(0, 1)])
    high0, low0 = far_block(0, det)

    both, cores, second = call(
        pair_kernel,
        "join_pair",
        (pltpu.VMEM((2, PART, LANES), f32), pltpu.VMEM((2, 2, 16, LANES), f32), token),
        [vmem] * 4 + [anywhere],
        1,
    )(block, one, section, even, high0)
    two = swap(both, "y", 3)
    near = odd_swap(cores, 1)
    high1, low1 = far_block(1, second)

    line, pair, third = call(
        line_kernel,
        "join_line",
        (pltpu.VMEM((4, PART, LANES), f32), pltpu.VMEM((2, 2, 2, 16, LANES), f32), token),
        [vmem] * 4 + [anywhere],
        1,
    )(both, two, cores, near, high1)
    across = [swap(line, "x", mask) for mask in (1, 3, 2)]
    distant = odd_swap(pair, 2)
    high2, low2 = far_block(2, third)

    sent, y = call(
        send_kernel,
        "send_products",
        (pltpu.VMEM((2, PART, LANES), f32), pltpu.VMEM((LANES, deep // 2), bf16)),
        [vmem] * 8,
        1 << 29,
    )(high0, low0, high1, low1, line, *across)
    half = swap(sent, "zh", 1)

    (keep,) = call(
        keep_kernel,
        "keep_products",
        (pltpu.VMEM((2, PART, LANES), f32),),
        [vmem] * 7,
        1 << 29,
        [rows, tile, tile, pltpu.VMEM((2, 64, 2 * LANES), f32)],
    )(pos, y, high2, low2, pair, distant, det)
    core = lax.ppermute(keep[0] + half[0], "c", [(0, 1), (1, 0)])
    return pl.pallas_call(
        finish_kernel,
        out_shape=(jax.ShapeDtypeStruct(base.shape, f32),) * 2,
        compiler_params=params(4),
        cost_estimate=pl.CostEstimate(flops=1 << 16, bytes_accessed=1 << 18, transcendentals=0),
        name="finish_rate",
    )(keep, half, core, det, section, base, accum)


def solution(mesh):
    fine = Mesh(mesh.devices.reshape(4, 4, 2, 2, 4), ("y", "x", "zh", "c", "zl"))
    rows = ("y", "x", "zh", "c")
    slab = P(None, "zl", rows)
    return jax.shard_map(
        local,
        mesh=fine,
        in_specs=(P(), P(), P(rows), slab, slab, slab),
        out_specs=(slab, slab),
        check_vma=False,
    )
```

```python
import functools
import math

import jax
import jax.numpy as jnp
from jax import lax
from jax.experimental import pallas as pl
from jax.experimental.pallas import tpu as pltpu
from jax.sharding import Mesh
from jax.sharding import PartitionSpec as P

TIME_STEP = 0.2
LANES = 128
COS = (0.9999992211, -19.73898242, 64.92872338, -85.27236068, 58.79387231, -21.07651549)
SIN = (6.283182817, -41.3414213, 81.59618177, -76.58008122, 41.20531753, -12.27114973)
SCALE = -0.75 / (2.0 * math.pi)
INV_WAVE = 1.0 / (2.0 * math.pi)
ROUNDER = 12582912.0
PART = 40
WIDE = 48


def horner(coefs, scale, arg):
    total = jnp.float32(coefs[-1] * scale)
    for c in coefs[-2::-1]:
        total = total * arg + jnp.float32(c * scale)
    return total


def coupling(dx, dy, dz):
    dz_sq = dz * dz
    dist_sq = dx * dx + dy * dy + dz_sq
    inv = lax.rsqrt(dist_sq)
    dist = dist_sq * inv
    turn = dist - ((dist + ROUNDER) - ROUNDER)
    turn_sq = turn * turn
    cosine = horner(COS, SCALE, turn_sq)
    sine = horner(SIN, SCALE, turn_sq) * turn
    inv_sq = inv * inv
    aligned = dz_sq * inv_sq
    quad_imag = inv_sq * (INV_WAVE - (3.0 * INV_WAVE) * aligned)
    quad_real = inv * ((1.0 - aligned) - INV_WAVE * quad_imag)
    return cosine * quad_real - sine * quad_imag, sine * quad_real + cosine * quad_imag


def split(value):
    high = value.astype(jnp.bfloat16)
    low = (value - high.astype(jnp.float32)).astype(jnp.bfloat16)
    return high, low


def lanes_at(index):
    return pl.ds(pl.multiple_of(index * LANES, LANES), LANES)


def place_of(step):
    down, across = lax.rem(step, 4), lax.div(step, 4)
    y = lax.axis_index("y") ^ down ^ lax.div(down, 2)
    x = lax.axis_index("x") ^ across ^ lax.div(across, 2)
    return y * 4 + x


def own_place():
    return lax.axis_index("y") * 4 + lax.axis_index("x")


def pack_kernel(section_ref, pops_ref, pos_ref, det_ref, block_ref, pos_out, det_out, sems):
    own = own_place() * 4 + lax.axis_index("zh") * 2 + lax.axis_index("c")
    moves = [
        pltpu.make_async_copy(section_ref.at[0], block_ref.at[pl.ds(0, 16)], sems.at[0]),
        pltpu.make_async_copy(section_ref.at[1], block_ref.at[pl.ds(16, 16)], sems.at[1]),
        pltpu.make_async_copy(pops_ref, block_ref.at[pl.ds(32, 1)], sems.at[2]),
        pltpu.make_async_copy(pos_ref, pos_out, sems.at[3]),
        pltpu.make_async_copy(det_ref.at[:, lanes_at(own)], det_out.at[pl.ds(0, 1)], sems.at[4]),
        pltpu.make_async_copy(det_ref.at[:, pl.ds(0, LANES)], det_out.at[pl.ds(1, 1)], sems.at[5]),
    ]
    for move in moves:
        move.start()
    for move in moves:
        move.wait()
    top = lax.broadcasted_iota(jnp.int32, (8, LANES), 0) == 0
    block_ref[32:PART, :] = jnp.where(top, 2.0 * block_ref[32:PART, :] - 1.0, 0.0)


def pair_kernel(block_ref, one_ref, after_ref, both_ref, token_ref):
    both_ref[0] = block_ref[...]
    both_ref[1] = one_ref[...]
    token_ref[...] = block_ref[0:8, :]


def line_kernel(both_ref, two_ref, slab_ref, near_ref, after_ref, all_ref, pair_ref, token_ref):
    all_ref[0:2] = both_ref[...]
    all_ref[2:4] = two_ref[...]
    pair_ref[0] = slab_ref[...]
    pair_ref[1] = near_ref[...]
    token_ref[...] = both_ref[0, 0:8, :]


def turned(pos_ref, k, index):
    line = pos_ref[k : k + 1, lanes_at(index)]
    return jnp.broadcast_to(line, (LANES, LANES)).T


def fill_tiles(pos_ref, row_ref, high_ref, low_ref, quads, first, count):
    quad = lax.axis_index("zh") * 2 + lax.axis_index("c")
    place = own_place()
    tiles = pos_ref.shape[1] // (4 * LANES)
    for n, other in enumerate(quads):
        for k in range(3):
            row_ref[k, n * LANES : (n + 1) * LANES, :] = turned(pos_ref, k, place * 4 + other)

    def tile(step, carry):
        at = lanes_at(place_of(step) * 4 + quad)
        cols = [pos_ref[k : k + 1, at] for k in range(3)]
        for n in range(0, count, 32):
            size = min(32, count - n)
            dx, dy, dz = [row_ref[k, first + n : first + n + size, :] - cols[k] for k in range(3)]
            for part, value in enumerate(coupling(dx, dy, dz)):
                high, low = split(value)
                lanes = lanes_at(step + part * tiles)
                high_ref[n : n + size, lanes] = high
                low_ref[n : n + size, lanes] = low
        return carry

    lax.fori_loop(0, tiles, tile, 0)


def term_kernel(pos_ref, slab_ref, near_ref, pair_ref, det_ref, rest_ref, row_ref, full_ref):
    own = lax.axis_index("zl")
    start = pl.multiple_of(own * 16, 16)
    offsets = []
    for k in range(3):
        row_ref[k] = turned(pos_ref, k, 0)
        offsets.append(row_ref[k, pl.ds(start, 16), :] - pos_ref[k : k + 1, 0:LANES])
    w_real, w_imag = coupling(*offsets)
    eye = (lax.broadcasted_iota(jnp.int32, (16, LANES), 0) + start) == lax.broadcasted_iota(jnp.int32, (16, LANES), 1)
    w_real = jnp.where(eye, det_ref[1:2, :], w_real)[:, 0:64]
    w_imag = jnp.where(eye, -0.5, w_imag)[:, 0:64]
    for n, ref in enumerate((slab_ref, near_ref, pair_ref.at[0], pair_ref.at[1])):
        place = own + (n % 2) * (1 - 2 * (own % 2))
        place = place + (n // 2) * (2 - 4 * (own // 2))
        there = pl.ds(pl.multiple_of(place * 16, 16), 16)
        full_ref[0, there, :] = ref[0]
        full_ref[1, there, :] = ref[1]

    def mul(a, b):
        return jnp.dot(a, b, precision=lax.Precision.HIGHEST, preferred_element_type=jnp.float32)

    v_real = mul(w_real, full_ref[0]) + mul(w_imag, full_ref[1])
    v_imag = mul(w_real, full_ref[1]) - mul(w_imag, full_ref[0])
    y_real, y_imag = slab_ref[0], slab_ref[1]
    line = det_ref[0:1, :]
    rest_ref[0] = line * y_imag - 0.5 * y_real - v_imag
    rest_ref[1] = v_real - line * y_real - 0.5 * y_imag


def clear_own(high_ref, low_ref, first):
    eye = lax.broadcasted_iota(jnp.int32, (LANES, LANES), 0) == lax.broadcasted_iota(jnp.int32, (LANES, LANES), 1)
    half = high_ref.shape[1] // 2
    for part in range(2):
        lanes = pl.ds(part * half, LANES)
        for ref in (high_ref, low_ref):
            own = ref[first : first + LANES, lanes].astype(jnp.float32)
            ref[first : first + LANES, lanes] = jnp.where(eye, 0.0, own).astype(jnp.bfloat16)


def own_quads():
    half, core = lax.axis_index("zh"), lax.axis_index("c")
    return half * 2 + 1 - core, half * 2 + core


def block_kernel(far, pos_ref, token_ref, high_ref, low_ref, row_ref):
    half, core = lax.axis_index("zh"), lax.axis_index("c")
    quad = (1 - half) * 2 + (core if far else 1 - core)
    fill_tiles(pos_ref, row_ref, high_ref, low_ref, (quad,), 0, LANES)


def early_kernel(pos_ref, token_ref, high_ref, low_ref, row_ref):
    @pl.when(lax.axis_index("zh") == 0)
    def _():
        fill_tiles(pos_ref, row_ref, high_ref, low_ref, own_quads()[:1], 0, LANES)


def fill_slab(refs, y_ref):
    zeros = jnp.zeros((16, LANES), jnp.float32)
    for step in range(16):
        block = refs[step // 4][step % 4]
        pops = jnp.concatenate([block[32:40], zeros[0:8]], axis=0)
        lanes = slice(step * LANES, (step + 1) * LANES)
        for n, value in enumerate((block[0:16], block[16:32], pops)):
            high, low = split(value)
            y_ref[n * 16 : n * 16 + 16, lanes] = high
            y_ref[WIDE + n * 16 : WIDE + n * 16 + 16, lanes] = low
        y_ref[2 * WIDE :, lanes] = jnp.zeros((LANES - 2 * WIDE, LANES), jnp.bfloat16)


def dot_slab(tiles, y):
    return lax.dot_general(tiles, y, (((1,), (1,)), ((), ())), preferred_element_type=jnp.float32)


def store_products(by_real, by_imag, out_ref, at):
    for n in range(by_real.shape[0] // LANES):
        rows = slice(n * LANES, (n + 1) * LANES)
        real, imag = by_real[rows, :].T, by_imag[rows, :].T
        real = real[0:PART] + real[WIDE : WIDE + PART]
        imag = imag[0:32] + imag[WIDE : WIDE + 32]
        out_ref[at + n, 0:16, :] = real[0:16] - imag[16:32]
        out_ref[at + n, 16:32, :] = real[16:32] + imag[0:16]
        out_ref[at + n, 32:PART, :] = real[32:PART]


def products(high_ref, low_ref, y):
    half = high_ref.shape[1] // 2
    by_real = dot_slab(high_ref[:, 0:half], y) + dot_slab(low_ref[:, 0:half], y)
    by_imag = dot_slab(high_ref[:, half:], y) + dot_slab(low_ref[:, half:], y)
    return by_real, by_imag


def send_kernel(pos_ref, high0, low0, high1, low1, all0, all1, all2, all3, out_ref, y_ref, own_high, own_low, row_ref):
    fill_slab((all0, all1, all2, all3), y_ref)
    y = y_ref[...]
    store_products(*products(high0, low0, y), out_ref, 0)
    store_products(*products(high1, low1, y), out_ref, 1)

    @pl.when(lax.axis_index("zh") == 0)
    def _():
        fill_tiles(pos_ref, row_ref, own_high, own_low, own_quads()[1:], 0, LANES)
        clear_own(own_high, own_low, 0)


def keep_kernel(pos_ref, y_ref, high2, low2, own_high, own_low, out_ref, row_ref, high_ref, low_ref):
    y = y_ref[...]

    @pl.when(lax.axis_index("zh") == 0)
    def _():
        store_products(*products(high2, low2, y), out_ref, 0)
        store_products(*products(own_high, own_low, y), out_ref, 1)

    @pl.when(lax.axis_index("zh") == 1)
    def _():
        fill_tiles(pos_ref, row_ref, high_ref, low_ref, own_quads(), 0, 2 * LANES)
        clear_own(high_ref, low_ref, LANES)
        store_products(*products(high_ref, low_ref, y), out_ref, 0)


def finish_kernel(keep_ref, half_ref, core_ref, rest_ref, slab_ref, base_ref, accum_ref, next_ref, acc_ref):
    z = keep_ref[1] + half_ref[1] + core_ref[...]
    shift = z[32:33]
    rate_real = z[16:32] + shift * slab_ref[1] + rest_ref[0]
    rate_imag = rest_ref[1] - z[0:16] - shift * slab_ref[0]
    for n, rate in enumerate((rate_real, rate_imag)):
        next_ref[n] = base_ref[n] + (0.5 * TIME_STEP) * rate
        acc_ref[n] = accum_ref[n] + (TIME_STEP / 3.0) * rate


def params(mib):
    return pltpu.CompilerParams(vmem_limit_bytes=mib << 20)


def in_hbm(array):
    return pltpu.with_memory_space_constraint(array, pltpu.HBM)


def local(positions, detuning, populations, base, section, accum):
    bf16, f32 = jnp.bfloat16, jnp.float32
    count = positions.shape[1]
    tiles = count // (4 * LANES)
    deep = 2 * tiles * LANES
    hbm, vmem = pl.BlockSpec(memory_space=pltpu.HBM), pl.BlockSpec(memory_space=pltpu.VMEM)
    anywhere = pl.BlockSpec(memory_space=pl.ANY)
    tile = pltpu.VMEM((LANES, deep), bf16)
    token = pltpu.VMEM((8, LANES), f32)
    rows = pltpu.VMEM((3, LANES, LANES), f32)

    def call(kernel, name, out_shape, in_specs, flops, scratch=()):
        return pl.pallas_call(
            kernel,
            out_shape=out_shape,
            in_specs=in_specs,
            out_specs=[vmem] * len(out_shape),
            scratch_shapes=scratch,
            compiler_params=params(6),
            cost_estimate=pl.CostEstimate(flops=flops, bytes_accessed=1 << 20, transcendentals=0),
            name=name,
        )

    def swap(array, axis, mask):
        size = lax.axis_size(axis)
        return lax.ppermute(array, axis, [(i, i ^ mask) for i in range(size)])

    def far_block(n, after):
        kernel = functools.partial(block_kernel, n)
        return call(kernel, "far_block_" + "ab"[n], (tile, tile), [vmem, anywhere], 1 << 24, [rows])(pos, after)

    block, pos, det = call(
        pack_kernel,
        "pack_block",
        (pltpu.VMEM((PART, LANES), f32), pltpu.VMEM(positions.shape, f32), token),
        [hbm] * 4,
        1 << 16,
        [pltpu.SemaphoreType.DMA((6,))],
    )(in_hbm(section), in_hbm(populations.reshape(1, LANES)), in_hbm(positions), in_hbm(detuning.reshape(1, count)))
    one = swap(block, "y", 1)
    near = swap(section, "zl", 1)
    high0, low0 = far_block(0, det)

    both, second = call(
        pair_kernel, "join_pair", (pltpu.VMEM((2, PART, LANES), f32), token), [vmem, vmem, anywhere], 1
    )(block, one, high0)
    two = swap(both, "y", 3)
    high1, low1 = far_block(1, second)

    line, pair, third = call(
        line_kernel,
        "join_line",
        (pltpu.VMEM((4, PART, LANES), f32), pltpu.VMEM((2, 2, 16, LANES), f32), token),
        [vmem] * 4 + [anywhere],
        1,
    )(both, two, section, near, high1)
    across = [swap(line, "x", mask) for mask in (1, 3, 2)]
    pair = swap(pair, "zl", 2)
    high2, low2 = call(
        early_kernel, "early_block", (tile, tile), [vmem, anywhere], 1 << 24, [rows]
    )(pos, third)

    sent, y, own_high, own_low = call(
        send_kernel,
        "send_products",
        (pltpu.VMEM((2, PART, LANES), f32), pltpu.VMEM((LANES, deep // 2), bf16), tile, tile),
        [vmem] * 9,
        1 << 29,
        [rows],
    )(pos, high0, low0, high1, low1, line, *across)
    half = swap(sent, "zh", 1)

    wide = pltpu.VMEM((2 * LANES, deep), bf16)
    (keep,) = call(
        keep_kernel,
        "keep_products",
        (pltpu.VMEM((2, PART, LANES), f32),),
        [vmem] * 6,
        1 << 29,
        [pltpu.VMEM((3, 2 * LANES, LANES), f32), wide, wide],
    )(pos, y, high2, low2, own_high, own_low)
    core = lax.ppermute(keep[0] + half[0], "c", [(0, 1), (1, 0)])
    rest = pl.pallas_call(
        term_kernel,
        out_shape=pltpu.VMEM((2, 16, LANES), f32),
        in_specs=[vmem] * 5,
        out_specs=vmem,
        scratch_shapes=[pltpu.VMEM((3, LANES, LANES), f32), pltpu.VMEM((2, 64, LANES), f32)],
        compiler_params=params(4),
        cost_estimate=pl.CostEstimate(flops=1 << 22, bytes_accessed=1 << 18, transcendentals=1 << 11),
        name="slab_term",
    )(pos, section, near, pair, det)

    return pl.pallas_call(
        finish_kernel,
        out_shape=(jax.ShapeDtypeStruct(base.shape, f32),) * 2,
        compiler_params=params(4),
        cost_estimate=pl.CostEstimate(flops=1 << 16, bytes_accessed=1 << 18, transcendentals=0),
        name="finish_rate",
    )(keep, half, core, rest, section, base, accum)


def solution(mesh):
    fine = Mesh(mesh.devices.reshape(4, 4, 2, 2, 4), ("y", "x", "zh", "c", "zl"))
    rows = ("y", "x", "zh", "c")
    slab = P(None, "zl", rows)
    return jax.shard_map(
        local,
        mesh=fine,
        in_specs=(P(), P(), P(rows), slab, slab, slab),
        out_specs=(slab, slab),
        check_vma=False,
    )
```

```python
import functools
import math

import jax
import jax.numpy as jnp
from jax import lax
from jax.experimental import pallas as pl
from jax.experimental.pallas import tpu as pltpu
from jax.sharding import Mesh
from jax.sharding import PartitionSpec as P

TIME_STEP = 0.2
LANES = 128
COS = (0.9999992211, -19.73898242, 64.92872338, -85.27236068, 58.79387231, -21.07651549)
SIN = (6.283182817, -41.3414213, 81.59618177, -76.58008122, 41.20531753, -12.27114973)
SCALE = -0.75 / (2.0 * math.pi)
INV_WAVE = 1.0 / (2.0 * math.pi)
ROUNDER = 12582912.0
PART = 40
WIDE = 48


def horner(coefs, scale, arg):
    total = jnp.float32(coefs[-1] * scale)
    for c in coefs[-2::-1]:
        total = total * arg + jnp.float32(c * scale)
    return total


def coupling(dx, dy, dz):
    dz_sq = dz * dz
    dist_sq = dx * dx + dy * dy + dz_sq
    inv = lax.rsqrt(dist_sq)
    dist = dist_sq * inv
    turn = dist - ((dist + ROUNDER) - ROUNDER)
    turn_sq = turn * turn
    cosine = horner(COS, SCALE, turn_sq)
    sine = horner(SIN, SCALE, turn_sq) * turn
    inv_sq = inv * inv
    aligned = dz_sq * inv_sq
    quad_imag = inv_sq * (INV_WAVE - (3.0 * INV_WAVE) * aligned)
    quad_real = inv * ((1.0 - aligned) - INV_WAVE * quad_imag)
    return cosine * quad_real - sine * quad_imag, sine * quad_real + cosine * quad_imag


def split(value):
    high = value.astype(jnp.bfloat16)
    low = (value - high.astype(jnp.float32)).astype(jnp.bfloat16)
    return high, low


def lanes_at(index):
    return pl.ds(pl.multiple_of(index * LANES, LANES), LANES)


def place_of(step):
    down, across = lax.rem(step, 4), lax.div(step, 4)
    y = lax.axis_index("y") ^ down ^ lax.div(down, 2)
    x = lax.axis_index("x") ^ across ^ lax.div(across, 2)
    return y * 4 + x


def own_place():
    return lax.axis_index("y") * 4 + lax.axis_index("x")


def pack_kernel(section_ref, pops_ref, pos_ref, det_ref, block_ref, pos_out, det_out, sems):
    own = own_place() * 4 + lax.axis_index("zh") * 2 + lax.axis_index("c")
    moves = [
        pltpu.make_async_copy(section_ref.at[0], block_ref.at[pl.ds(0, 16)], sems.at[0]),
        pltpu.make_async_copy(section_ref.at[1], block_ref.at[pl.ds(16, 16)], sems.at[1]),
        pltpu.make_async_copy(pops_ref, block_ref.at[pl.ds(32, 1)], sems.at[2]),
        pltpu.make_async_copy(pos_ref, pos_out, sems.at[3]),
        pltpu.make_async_copy(det_ref.at[:, lanes_at(own)], det_out.at[pl.ds(0, 1)], sems.at[4]),
        pltpu.make_async_copy(det_ref.at[:, pl.ds(0, LANES)], det_out.at[pl.ds(1, 1)], sems.at[5]),
    ]
    for move in moves:
        move.start()
    for move in moves:
        move.wait()
    top = lax.broadcasted_iota(jnp.int32, (8, LANES), 0) == 0
    block_ref[32:PART, :] = jnp.where(top, 2.0 * block_ref[32:PART, :] - 1.0, 0.0)


def pair_kernel(block_ref, one_ref, after_ref, both_ref, token_ref):
    both_ref[0] = block_ref[...]
    both_ref[1] = one_ref[...]
    token_ref[...] = block_ref[0:8, :]


def line_kernel(both_ref, two_ref, slab_ref, near_ref, after_ref, all_ref, pair_ref, token_ref):
    all_ref[0:2] = both_ref[...]
    all_ref[2:4] = two_ref[...]
    pair_ref[0] = slab_ref[...]
    pair_ref[1] = near_ref[...]
    token_ref[...] = both_ref[0, 0:8, :]


def turned(pos_ref, k, index):
    line = pos_ref[k : k + 1, lanes_at(index)]
    return jnp.broadcast_to(line, (LANES, LANES)).T


def fill_tiles(pos_ref, row_ref, high_ref, low_ref, quads, first, count):
    quad = lax.axis_index("zh") * 2 + lax.axis_index("c")
    place = own_place()
    tiles = pos_ref.shape[1] // (4 * LANES)
    for n, other in enumerate(quads):
        for k in range(3):
            row_ref[k, n * LANES : (n + 1) * LANES, :] = turned(pos_ref, k, place * 4 + other)

    def tile(step, carry):
        at = lanes_at(place_of(step) * 4 + quad)
        cols = [pos_ref[k : k + 1, at] for k in range(3)]
        for n in range(0, count, 32):
            size = min(32, count - n)
            dx, dy, dz = [row_ref[k, first + n : first + n + size, :] - cols[k] for k in range(3)]
            for part, value in enumerate(coupling(dx, dy, dz)):
                high, low = split(value)
                lanes = lanes_at(step + part * tiles)
                high_ref[n : n + size, lanes] = high
                low_ref[n : n + size, lanes] = low
        return carry

    lax.fori_loop(0, tiles, tile, 0)


def term_kernel(pos_ref, slab_ref, near_ref, pair_ref, det_ref, rest_ref, row_ref, full_ref):
    own = lax.axis_index("zl")
    start = pl.multiple_of(own * 16, 16)
    offsets = []
    for k in range(3):
        row_ref[k] = turned(pos_ref, k, 0)
        offsets.append(row_ref[k, pl.ds(start, 16), :] - pos_ref[k : k + 1, 0:LANES])
    w_real, w_imag = coupling(*offsets)
    eye = (lax.broadcasted_iota(jnp.int32, (16, LANES), 0) + start) == lax.broadcasted_iota(jnp.int32, (16, LANES), 1)
    w_real = jnp.where(eye, det_ref[1:2, :], w_real)[:, 0:64]
    w_imag = jnp.where(eye, -0.5, w_imag)[:, 0:64]
    for n, ref in enumerate((slab_ref, near_ref, pair_ref.at[0], pair_ref.at[1])):
        place = own + (n % 2) * (1 - 2 * (own % 2))
        place = place + (n // 2) * (2 - 4 * (own // 2))
        there = pl.ds(pl.multiple_of(place * 16, 16), 16)
        full_ref[0, there, :] = ref[0]
        full_ref[1, there, :] = ref[1]

    def mul(a, b):
        return jnp.dot(a, b, precision=lax.Precision.HIGHEST, preferred_element_type=jnp.float32)

    v_real = mul(w_real, full_ref[0]) + mul(w_imag, full_ref[1])
    v_imag = mul(w_real, full_ref[1]) - mul(w_imag, full_ref[0])
    y_real, y_imag = slab_ref[0], slab_ref[1]
    line = det_ref[0:1, :]
    rest_ref[0] = line * y_imag - 0.5 * y_real - v_imag
    rest_ref[1] = v_real - line * y_real - 0.5 * y_imag


def clear_own(high_ref, low_ref, first):
    eye = lax.broadcasted_iota(jnp.int32, (LANES, LANES), 0) == lax.broadcasted_iota(jnp.int32, (LANES, LANES), 1)
    half = high_ref.shape[1] // 2
    for part in range(2):
        lanes = pl.ds(part * half, LANES)
        for ref in (high_ref, low_ref):
            own = ref[first : first + LANES, lanes].astype(jnp.float32)
            ref[first : first + LANES, lanes] = jnp.where(eye, 0.0, own).astype(jnp.bfloat16)


def own_quads():
    half, core = lax.axis_index("zh"), lax.axis_index("c")
    return half * 2 + 1 - core, half * 2 + core


def block_kernel(far, pos_ref, token_ref, high_ref, low_ref, row_ref):
    half, core = lax.axis_index("zh"), lax.axis_index("c")
    quad = (1 - half) * 2 + (core if far else 1 - core)
    fill_tiles(pos_ref, row_ref, high_ref, low_ref, (quad,), 0, LANES)


def early_kernel(pos_ref, token_ref, high_ref, low_ref, row_ref):
    @pl.when(lax.axis_index("zh") == 0)
    def _():
        fill_tiles(pos_ref, row_ref, high_ref, low_ref, own_quads()[:1], 0, LANES)


def fill_slab(refs, y_ref):
    zeros = jnp.zeros((16, LANES), jnp.float32)
    for step in range(16):
        block = refs[step // 4][step % 4]
        pops = jnp.concatenate([block[32:40], zeros[0:8]], axis=0)
        lanes = slice(step * LANES, (step + 1) * LANES)
        for n, value in enumerate((block[0:16], block[16:32], pops)):
            high, low = split(value)
            y_ref[n * 16 : n * 16 + 16, lanes] = high
            y_ref[WIDE + n * 16 : WIDE + n * 16 + 16, lanes] = low
        y_ref[2 * WIDE :, lanes] = jnp.zeros((LANES - 2 * WIDE, LANES), jnp.bfloat16)


def dot_slab(tiles, y):
    return lax.dot_general(tiles, y, (((1,), (1,)), ((), ())), preferred_element_type=jnp.float32)


def store_products(by_real, by_imag, out_ref, at):
    for n in range(by_real.shape[0] // LANES):
        rows = slice(n * LANES, (n + 1) * LANES)
        real, imag = by_real[rows, :].T, by_imag[rows, :].T
        real = real[0:PART] + real[WIDE : WIDE + PART]
        imag = imag[0:32] + imag[WIDE : WIDE + 32]
        out_ref[at + n, 0:16, :] = real[0:16] - imag[16:32]
        out_ref[at + n, 16:32, :] = real[16:32] + imag[0:16]
        out_ref[at + n, 32:PART, :] = real[32:PART]


def products(high_ref, low_ref, y):
    half = high_ref.shape[1] // 2
    by_real = dot_slab(high_ref[:, 0:half], y) + dot_slab(low_ref[:, 0:half], y)
    by_imag = dot_slab(high_ref[:, half:], y) + dot_slab(low_ref[:, half:], y)
    return by_real, by_imag


def send_kernel(high0, low0, high1, low1, all0, all1, all2, all3, out_ref, y_ref):
    fill_slab((all0, all1, all2, all3), y_ref)
    y = y_ref[...]
    store_products(*products(high0, low0, y), out_ref, 0)
    store_products(*products(high1, low1, y), out_ref, 1)


def keep_kernel(pos_ref, y_ref, high2, low2, out_ref, row_ref, high_ref, low_ref):
    y = y_ref[...]

    @pl.when(lax.axis_index("zh") == 0)
    def _():
        high, low = high_ref.at[pl.ds(0, LANES)], low_ref.at[pl.ds(0, LANES)]
        fill_tiles(pos_ref, row_ref, high, low, own_quads()[1:], 0, LANES)
        clear_own(high, low, 0)
        store_products(*products(high2, low2, y), out_ref, 0)
        store_products(*products(high, low, y), out_ref, 1)

    @pl.when(lax.axis_index("zh") == 1)
    def _():
        fill_tiles(pos_ref, row_ref, high_ref, low_ref, own_quads(), 0, 2 * LANES)
        clear_own(high_ref, low_ref, LANES)
        store_products(*products(high_ref, low_ref, y), out_ref, 0)


def finish_kernel(keep_ref, half_ref, core_ref, rest_ref, slab_ref, base_ref, accum_ref, next_ref, acc_ref):
    z = keep_ref[1] + half_ref[1] + core_ref[...]
    shift = z[32:33]
    rate_real = z[16:32] + shift * slab_ref[1] + rest_ref[0]
    rate_imag = rest_ref[1] - z[0:16] - shift * slab_ref[0]
    for n, rate in enumerate((rate_real, rate_imag)):
        next_ref[n] = base_ref[n] + (0.5 * TIME_STEP) * rate
        acc_ref[n] = accum_ref[n] + (TIME_STEP / 3.0) * rate


def params(mib):
    return pltpu.CompilerParams(vmem_limit_bytes=mib << 20)


def in_hbm(array):
    return pltpu.with_memory_space_constraint(array, pltpu.HBM)


def local(positions, detuning, populations, base, section, accum):
    bf16, f32 = jnp.bfloat16, jnp.float32
    count = positions.shape[1]
    tiles = count // (4 * LANES)
    deep = 2 * tiles * LANES
    hbm, vmem = pl.BlockSpec(memory_space=pltpu.HBM), pl.BlockSpec(memory_space=pltpu.VMEM)
    anywhere = pl.BlockSpec(memory_space=pl.ANY)
    tile = pltpu.VMEM((LANES, deep), bf16)
    token = pltpu.VMEM((8, LANES), f32)
    rows = pltpu.VMEM((3, LANES, LANES), f32)

    def call(kernel, name, out_shape, in_specs, flops, scratch=()):
        return pl.pallas_call(
            kernel,
            out_shape=out_shape,
            in_specs=in_specs,
            out_specs=[vmem] * len(out_shape),
            scratch_shapes=scratch,
            compiler_params=params(6),
            cost_estimate=pl.CostEstimate(flops=flops, bytes_accessed=1 << 20, transcendentals=0),
            name=name,
        )

    def swap(array, axis, mask):
        size = lax.axis_size(axis)
        return lax.ppermute(array, axis, [(i, i ^ mask) for i in range(size)])

    def far_block(n, after):
        kernel = functools.partial(block_kernel, n)
        return call(kernel, "far_block_" + "ab"[n], (tile, tile), [vmem, anywhere], 1 << 24, [rows])(pos, after)

    block, pos, det = call(
        pack_kernel,
        "pack_block",
        (pltpu.VMEM((PART, LANES), f32), pltpu.VMEM(positions.shape, f32), token),
        [hbm] * 4,
        1 << 16,
        [pltpu.SemaphoreType.DMA((6,))],
    )(in_hbm(section), in_hbm(populations.reshape(1, LANES)), in_hbm(positions), in_hbm(detuning.reshape(1, count)))
    one = swap(block, "y", 1)
    near = swap(section, "zl", 1)
    high0, low0 = far_block(0, det)

    both, second = call(
        pair_kernel, "join_pair", (pltpu.VMEM((2, PART, LANES), f32), token), [vmem, vmem, anywhere], 1
    )(block, one, high0)
    two = swap(both, "y", 3)
    high1, low1 = far_block(1, second)

    line, pair, third = call(
        line_kernel,
        "join_line",
        (pltpu.VMEM((4, PART, LANES), f32), pltpu.VMEM((2, 2, 16, LANES), f32), token),
        [vmem] * 4 + [anywhere],
        1,
    )(both, two, section, near, high1)
    across = [swap(line, "x", mask) for mask in (1, 3, 2)]
    pair = swap(pair, "zl", 2)
    high2, low2 = call(
        early_kernel, "early_block", (tile, tile), [vmem, anywhere], 1 << 24, [rows]
    )(pos, third)

    sent, y = call(
        send_kernel,
        "send_products",
        (pltpu.VMEM((2, PART, LANES), f32), pltpu.VMEM((LANES, deep // 2), bf16)),
        [vmem] * 8,
        1 << 29,
    )(high0, low0, high1, low1, line, *across)
    half = swap(sent, "zh", 1)

    wide = pltpu.VMEM((2 * LANES, deep), bf16)
    (keep,) = call(
        keep_kernel,
        "keep_products",
        (pltpu.VMEM((2, PART, LANES), f32),),
        [vmem] * 4,
        1 << 29,
        [pltpu.VMEM((3, 2 * LANES, LANES), f32), wide, wide],
    )(pos, y, high2, low2)
    core = lax.ppermute(keep[0] + half[0], "c", [(0, 1), (1, 0)])
    rest = pl.pallas_call(
        term_kernel,
        out_shape=pltpu.VMEM((2, 16, LANES), f32),
        in_specs=[vmem] * 5,
        out_specs=vmem,
        scratch_shapes=[pltpu.VMEM((3, LANES, LANES), f32), pltpu.VMEM((2, 64, LANES), f32)],
        compiler_params=params(4),
        cost_estimate=pl.CostEstimate(flops=1 << 22, bytes_accessed=1 << 18, transcendentals=1 << 11),
        name="slab_term",
    )(pos, section, near, pair, det)

    return pl.pallas_call(
        finish_kernel,
        out_shape=(jax.ShapeDtypeStruct(base.shape, f32),) * 2,
        compiler_params=params(4),
        cost_estimate=pl.CostEstimate(flops=1 << 16, bytes_accessed=1 << 18, transcendentals=0),
        name="finish_rate",
    )(keep, half, core, rest, section, base, accum)


def solution(mesh):
    fine = Mesh(mesh.devices.reshape(4, 4, 2, 2, 4), ("y", "x", "zh", "c", "zl"))
    rows = ("y", "x", "zh", "c")
    slab = P(None, "zl", rows)
    return jax.shard_map(
        local,
        mesh=fine,
        in_specs=(P(), P(), P(rows), slab, slab, slab),
        out_specs=(slab, slab),
        check_vma=False,
    )
```

```python
import functools
import math

import jax
import jax.numpy as jnp
from jax import lax
from jax.experimental import pallas as pl
from jax.experimental.pallas import tpu as pltpu
from jax.sharding import Mesh
from jax.sharding import PartitionSpec as P

TIME_STEP = 0.2
LANES = 128
COS = (0.9999992211, -19.73898242, 64.92872338, -85.27236068, 58.79387231, -21.07651549)
SIN = (6.283182817, -41.3414213, 81.59618177, -76.58008122, 41.20531753, -12.27114973)
SCALE = -0.75 / (2.0 * math.pi)
INV_WAVE = 1.0 / (2.0 * math.pi)
ROUNDER = 12582912.0
PART = 40
WIDE = 48


def horner(coefs, scale, arg):
    total = jnp.float32(coefs[-1] * scale)
    for c in coefs[-2::-1]:
        total = total * arg + jnp.float32(c * scale)
    return total


def coupling(dx, dy, dz):
    dz_sq = dz * dz
    dist_sq = dx * dx + dy * dy + dz_sq
    inv = lax.rsqrt(dist_sq)
    dist = dist_sq * inv
    turn = dist - ((dist + ROUNDER) - ROUNDER)
    turn_sq = turn * turn
    cosine = horner(COS, SCALE, turn_sq)
    sine = horner(SIN, SCALE, turn_sq) * turn
    inv_sq = inv * inv
    aligned = dz_sq * inv_sq
    quad_imag = inv_sq * (INV_WAVE - (3.0 * INV_WAVE) * aligned)
    quad_real = inv * ((1.0 - aligned) - INV_WAVE * quad_imag)
    return cosine * quad_real - sine * quad_imag, sine * quad_real + cosine * quad_imag


def split(value):
    high = value.astype(jnp.bfloat16)
    low = (value - high.astype(jnp.float32)).astype(jnp.bfloat16)
    return high, low


def lanes_at(index):
    return pl.ds(pl.multiple_of(index * LANES, LANES), LANES)


def place_of(step):
    down, across = lax.rem(step, 4), lax.div(step, 4)
    y = lax.axis_index("y") ^ down ^ lax.div(down, 2)
    x = lax.axis_index("x") ^ across ^ lax.div(across, 2)
    return y * 4 + x


def own_place():
    return lax.axis_index("y") * 4 + lax.axis_index("x")


def pack_kernel(section_ref, pops_ref, pos_ref, det_ref, block_ref, pos_out, det_out, sems):
    own = own_place() * 4 + lax.axis_index("zh") * 2 + lax.axis_index("c")
    moves = [
        pltpu.make_async_copy(section_ref.at[0], block_ref.at[pl.ds(0, 16)], sems.at[0]),
        pltpu.make_async_copy(section_ref.at[1], block_ref.at[pl.ds(16, 16)], sems.at[1]),
        pltpu.make_async_copy(pops_ref, block_ref.at[pl.ds(32, 1)], sems.at[2]),
        pltpu.make_async_copy(pos_ref, pos_out, sems.at[3]),
        pltpu.make_async_copy(det_ref.at[:, lanes_at(own)], det_out.at[pl.ds(0, 1)], sems.at[4]),
        pltpu.make_async_copy(det_ref.at[:, pl.ds(0, LANES)], det_out.at[pl.ds(1, 1)], sems.at[5]),
    ]
    for move in moves:
        move.start()
    for move in moves:
        move.wait()
    top = lax.broadcasted_iota(jnp.int32, (8, LANES), 0) == 0
    block_ref[32:PART, :] = jnp.where(top, 2.0 * block_ref[32:PART, :] - 1.0, 0.0)


def pair_kernel(block_ref, one_ref, after_ref, both_ref, token_ref):
    both_ref[0] = block_ref[...]
    both_ref[1] = one_ref[...]
    token_ref[...] = block_ref[0:8, :]


def line_kernel(both_ref, two_ref, near_ref, after_ref, all_ref, token_ref):
    all_ref[0:2] = both_ref[...]
    all_ref[2:4] = two_ref[...]
    token_ref[...] = both_ref[0, 0:8, :]


def turned(pos_ref, k, index):
    line = pos_ref[k : k + 1, lanes_at(index)]
    return jnp.broadcast_to(line, (LANES, LANES)).T


def fill_tiles(pos_ref, row_ref, high_ref, low_ref, quads, first, count):
    quad = lax.axis_index("zh") * 2 + lax.axis_index("c")
    place = own_place()
    tiles = pos_ref.shape[1] // (4 * LANES)
    for n, other in enumerate(quads):
        for k in range(3):
            row_ref[k, n * LANES : (n + 1) * LANES, :] = turned(pos_ref, k, place * 4 + other)

    together = 4 * LANES // count

    def tile(group, carry):
        for step in [group * together + n for n in range(together)]:
            at = lanes_at(place_of(step) * 4 + quad)
            cols = [pos_ref[k : k + 1, at] for k in range(3)]
            for n in range(0, count, 32):
                dx, dy, dz = [row_ref[k, first + n : first + n + 32, :] - cols[k] for k in range(3)]
                for part, value in enumerate(coupling(dx, dy, dz)):
                    high, low = split(value)
                    lanes = lanes_at(step + part * tiles)
                    high_ref[n : n + 32, lanes] = high
                    low_ref[n : n + 32, lanes] = low
        return carry

    lax.fori_loop(0, tiles // together, tile, 0)


def term_kernel(pos_ref, slab_ref, near_ref, pair_ref, det_ref, rest_ref, row_ref, full_ref):
    own = lax.axis_index("zl")
    start = pl.multiple_of(own * 16, 16)
    offsets = []
    for k in range(3):
        row_ref[k] = turned(pos_ref, k, 0)
        offsets.append(row_ref[k, pl.ds(start, 16), :] - pos_ref[k : k + 1, 0:LANES])
    w_real, w_imag = coupling(*offsets)
    eye = (lax.broadcasted_iota(jnp.int32, (16, LANES), 0) + start) == lax.broadcasted_iota(jnp.int32, (16, LANES), 1)
    w_real = jnp.where(eye, det_ref[1:2, :], w_real)[:, 0:64]
    w_imag = jnp.where(eye, -0.5, w_imag)[:, 0:64]
    for n, ref in enumerate((slab_ref, near_ref, pair_ref.at[0], pair_ref.at[1])):
        place = own + (n % 2) * (1 - 2 * (own % 2))
        place = place + (n // 2) * (2 - 4 * (own // 2))
        there = pl.ds(pl.multiple_of(place * 16, 16), 16)
        full_ref[0, there, :] = ref[0:16]
        full_ref[1, there, :] = ref[16:32]

    def mul(a, b):
        return jnp.dot(a, b, precision=lax.Precision.HIGHEST, preferred_element_type=jnp.float32)

    v_real = mul(w_real, full_ref[0]) + mul(w_imag, full_ref[1])
    v_imag = mul(w_real, full_ref[1]) - mul(w_imag, full_ref[0])
    y_real, y_imag = slab_ref[0:16], slab_ref[16:32]
    line = det_ref[0:1, :]
    rest_ref[0] = line * y_imag - 0.5 * y_real - v_imag
    rest_ref[1] = v_real - line * y_real - 0.5 * y_imag


def clear_own(high_ref, low_ref, first):
    eye = lax.broadcasted_iota(jnp.int32, (LANES, LANES), 0) == lax.broadcasted_iota(jnp.int32, (LANES, LANES), 1)
    half = high_ref.shape[1] // 2
    for part in range(2):
        lanes = pl.ds(part * half, LANES)
        for ref in (high_ref, low_ref):
            own = ref[first : first + LANES, lanes].astype(jnp.float32)
            ref[first : first + LANES, lanes] = jnp.where(eye, 0.0, own).astype(jnp.bfloat16)


def own_quads():
    half, core = lax.axis_index("zh"), lax.axis_index("c")
    return half * 2 + 1 - core, half * 2 + core


def block_kernel(far, pos_ref, token_ref, high_ref, low_ref, row_ref):
    half, core = lax.axis_index("zh"), lax.axis_index("c")
    quad = (1 - half) * 2 + (core if far else 1 - core)
    fill_tiles(pos_ref, row_ref, high_ref, low_ref, (quad,), 0, LANES)


def ahead():
    return (1 - lax.axis_index("zh")) * (lax.axis_index("zl") < 2).astype(jnp.int32)


def ahead_kernel(pos_ref, slab_ref, near_ref, token_ref, high_ref, low_ref, pair_ref, row_ref):
    pair_ref[0] = slab_ref[...]
    pair_ref[1] = near_ref[...]

    @pl.when(ahead() == 1)
    def _():
        fill_tiles(pos_ref, row_ref, high_ref, low_ref, own_quads()[:1], 0, LANES)


def early_kernel(pos_ref, token_ref, high_ref, low_ref, row_ref):
    @pl.when((1 - lax.axis_index("zh")) - ahead() == 1)
    def _():
        fill_tiles(pos_ref, row_ref, high_ref, low_ref, own_quads()[:1], 0, LANES)


def fill_slab(refs, y_ref):
    zeros = jnp.zeros((16, LANES), jnp.float32)
    for step in range(16):
        block = refs[step // 4][step % 4]
        pops = jnp.concatenate([block[32:40], zeros[0:8]], axis=0)
        lanes = slice(step * LANES, (step + 1) * LANES)
        for n, value in enumerate((block[0:16], block[16:32], pops)):
            high, low = split(value)
            y_ref[n * 16 : n * 16 + 16, lanes] = high
            y_ref[WIDE + n * 16 : WIDE + n * 16 + 16, lanes] = low
        y_ref[2 * WIDE :, lanes] = jnp.zeros((LANES - 2 * WIDE, LANES), jnp.bfloat16)


def dot_slab(tiles, y):
    return lax.dot_general(tiles, y, (((1,), (1,)), ((), ())), preferred_element_type=jnp.float32)


def store_products(by_real, by_imag, out_ref, at):
    for n in range(by_real.shape[0] // LANES):
        rows = slice(n * LANES, (n + 1) * LANES)
        real, imag = by_real[rows, :].T, by_imag[rows, :].T
        real = real[0:PART] + real[WIDE : WIDE + PART]
        imag = imag[0:32] + imag[WIDE : WIDE + 32]
        out_ref[at + n, 0:16, :] = real[0:16] - imag[16:32]
        out_ref[at + n, 16:32, :] = real[16:32] + imag[0:16]
        out_ref[at + n, 32:PART, :] = real[32:PART]


def products(high_ref, low_ref, y):
    half = high_ref.shape[1] // 2
    by_real = dot_slab(high_ref[:, 0:half], y) + dot_slab(low_ref[:, 0:half], y)
    by_imag = dot_slab(high_ref[:, half:], y) + dot_slab(low_ref[:, half:], y)
    return by_real, by_imag


def send_kernel(high0, low0, high1, low1, high3, low3, all0, all1, all2, all3, out_ref, y_ref, first_ref):
    fill_slab((all0, all1, all2, all3), y_ref)
    y = y_ref[...]
    store_products(*products(high0, low0, y), out_ref, 0)
    store_products(*products(high1, low1, y), out_ref, 1)

    @pl.when(ahead() == 1)
    def _():
        store_products(*products(high3, low3, y), first_ref, 0)


def keep_kernel(pos_ref, y_ref, high2, low2, first_ref, out_ref, row_ref, high_ref, low_ref):
    y = y_ref[...]

    @pl.when(lax.axis_index("zh") == 0)
    def _():
        high, low = high_ref.at[pl.ds(0, LANES)], low_ref.at[pl.ds(0, LANES)]
        fill_tiles(pos_ref, row_ref, high, low, own_quads()[1:], 0, LANES)
        clear_own(high, low, 0)
        store_products(*products(high, low, y), out_ref, 1)

    @pl.when(ahead() == 1)
    def _():
        out_ref[0] = first_ref[0]

    @pl.when((1 - lax.axis_index("zh")) - ahead() == 1)
    def _():
        store_products(*products(high2, low2, y), out_ref, 0)

    @pl.when(lax.axis_index("zh") == 1)
    def _():
        fill_tiles(pos_ref, row_ref, high_ref, low_ref, own_quads(), 0, 2 * LANES)
        clear_own(high_ref, low_ref, LANES)
        store_products(*products(high_ref, low_ref, y), out_ref, 0)


def finish_kernel(keep_ref, half_ref, core_ref, rest_ref, slab_ref, base_ref, accum_ref, next_ref, acc_ref):
    z = keep_ref[1] + half_ref[1] + core_ref[...]
    shift = z[32:33]
    rate_real = z[16:32] + shift * slab_ref[16:32] + rest_ref[0]
    rate_imag = rest_ref[1] - z[0:16] - shift * slab_ref[0:16]
    for n, rate in enumerate((rate_real, rate_imag)):
        next_ref[n] = base_ref[n] + (0.5 * TIME_STEP) * rate
        acc_ref[n] = accum_ref[n] + (TIME_STEP / 3.0) * rate


def params(mib):
    return pltpu.CompilerParams(vmem_limit_bytes=mib << 20)


def in_hbm(array):
    return pltpu.with_memory_space_constraint(array, pltpu.HBM)


def local(positions, detuning, populations, base, section, accum):
    bf16, f32 = jnp.bfloat16, jnp.float32
    count = positions.shape[1]
    tiles = count // (4 * LANES)
    deep = 2 * tiles * LANES
    hbm, vmem = pl.BlockSpec(memory_space=pltpu.HBM), pl.BlockSpec(memory_space=pltpu.VMEM)
    anywhere = pl.BlockSpec(memory_space=pl.ANY)
    tile = pltpu.VMEM((LANES, deep), bf16)
    token = pltpu.VMEM((8, LANES), f32)
    rows = pltpu.VMEM((3, LANES, LANES), f32)

    def call(kernel, name, out_shape, in_specs, flops, scratch=()):
        return pl.pallas_call(
            kernel,
            out_shape=out_shape,
            in_specs=in_specs,
            out_specs=[vmem] * len(out_shape),
            scratch_shapes=scratch,
            compiler_params=params(6),
            cost_estimate=pl.CostEstimate(flops=flops, bytes_accessed=1 << 20, transcendentals=0),
            name=name,
        )

    def swap(array, axis, mask):
        size = lax.axis_size(axis)
        return lax.ppermute(array, axis, [(i, i ^ mask) for i in range(size)])

    def far_block(n, after):
        kernel = functools.partial(block_kernel, n)
        return call(kernel, "far_block_" + "ab"[n], (tile, tile), [vmem, anywhere], 1 << 24, [rows])(pos, after)

    block, pos, det = call(
        pack_kernel,
        "pack_block",
        (pltpu.VMEM((PART, LANES), f32), pltpu.VMEM(positions.shape, f32), token),
        [hbm] * 4,
        1 << 16,
        [pltpu.SemaphoreType.DMA((6,))],
    )(in_hbm(section), in_hbm(populations.reshape(1, LANES)), in_hbm(positions), in_hbm(detuning.reshape(1, count)))
    one = swap(block, "y", 1)
    near = swap(block, "zl", 1)
    high0, low0 = far_block(0, det)

    both, second = call(
        pair_kernel, "join_pair", (pltpu.VMEM((2, PART, LANES), f32), token), [vmem, vmem, anywhere], 1
    )(block, one, high0)
    two = swap(both, "y", 3)
    high1, low1 = far_block(1, second)

    line, third = call(
        line_kernel, "join_line", (pltpu.VMEM((4, PART, LANES), f32), token), [vmem] * 3 + [anywhere], 1
    )(both, two, near, high1)
    across = [swap(line, "x", mask) for mask in (1, 3, 2)]
    high3, low3, pair = call(
        ahead_kernel,
        "ahead_block",
        (tile, tile, pltpu.VMEM((2, PART, LANES), f32)),
        [vmem] * 3 + [anywhere],
        1 << 24,
        [rows],
    )(pos, block, near, third)
    pair = swap(pair, "zl", 2)
    high2, low2 = call(
        early_kernel, "early_block", (tile, tile), [vmem, anywhere], 1 << 24, [rows]
    )(pos, high3)

    sent, y, first = call(
        send_kernel,
        "send_products",
        (
            pltpu.VMEM((2, PART, LANES), f32),
            pltpu.VMEM((LANES, deep // 2), bf16),
            pltpu.VMEM((1, PART, LANES), f32),
        ),
        [vmem] * 10,
        1 << 29,
    )(high0, low0, high1, low1, high3, low3, line, *across)
    half = swap(sent, "zh", 1)

    wide = pltpu.VMEM((2 * LANES, deep), bf16)
    (keep,) = call(
        keep_kernel,
        "keep_products",
        (pltpu.VMEM((2, PART, LANES), f32),),
        [vmem] * 5,
        1 << 29,
        [pltpu.VMEM((3, 2 * LANES, LANES), f32), wide, wide],
    )(pos, y, high2, low2, first)
    core = lax.ppermute(keep[0] + half[0], "c", [(0, 1), (1, 0)])
    rest = pl.pallas_call(
        term_kernel,
        out_shape=pltpu.VMEM((2, 16, LANES), f32),
        in_specs=[vmem] * 5,
        out_specs=vmem,
        scratch_shapes=[pltpu.VMEM((3, LANES, LANES), f32), pltpu.VMEM((2, 64, LANES), f32)],
        compiler_params=params(4),
        cost_estimate=pl.CostEstimate(flops=1 << 22, bytes_accessed=1 << 18, transcendentals=1 << 11),
        name="slab_term",
    )(pos, block, near, pair, det)

    return pl.pallas_call(
        finish_kernel,
        out_shape=(jax.ShapeDtypeStruct(base.shape, f32),) * 2,
        compiler_params=params(4),
        cost_estimate=pl.CostEstimate(flops=1 << 16, bytes_accessed=1 << 18, transcendentals=0),
        name="finish_rate",
    )(keep, half, core, rest, block, base, accum)


def solution(mesh):
    fine = Mesh(mesh.devices.reshape(4, 4, 2, 2, 4), ("y", "x", "zh", "c", "zl"))
    rows = ("y", "x", "zh", "c")
    slab = P(None, "zl", rows)
    return jax.shard_map(
        local,
        mesh=fine,
        in_specs=(P(), P(), P(rows), slab, slab, slab),
        out_specs=(slab, slab),
        check_vma=False,
    )
```

```python
import functools
import math

import jax
import jax.numpy as jnp
from jax import lax
from jax.experimental import pallas as pl
from jax.experimental.pallas import tpu as pltpu
from jax.sharding import Mesh
from jax.sharding import PartitionSpec as P

TIME_STEP = 0.2
LANES = 128
COS = (0.9999992211, -19.73898242, 64.92872338, -85.27236068, 58.79387231, -21.07651549)
SIN = (6.283182817, -41.3414213, 81.59618177, -76.58008122, 41.20531753, -12.27114973)
SCALE = -0.75 / (2.0 * math.pi)
INV_WAVE = 1.0 / (2.0 * math.pi)
ROUNDER = 12582912.0
PART = 40
WIDE = 48


def horner(coefs, scale, arg):
    total = jnp.float32(coefs[-1] * scale)
    for c in coefs[-2::-1]:
        total = total * arg + jnp.float32(c * scale)
    return total


def coupling(dx, dy, dz):
    dz_sq = dz * dz
    dist_sq = dx * dx + dy * dy + dz_sq
    inv = lax.rsqrt(dist_sq)
    dist = dist_sq * inv
    turn = dist - ((dist + ROUNDER) - ROUNDER)
    turn_sq = turn * turn
    cosine = horner(COS, SCALE, turn_sq)
    sine = horner(SIN, SCALE, turn_sq) * turn
    inv_sq = inv * inv
    aligned = dz_sq * inv_sq
    quad_imag = inv_sq * (INV_WAVE - (3.0 * INV_WAVE) * aligned)
    quad_real = inv * ((1.0 - aligned) - INV_WAVE * quad_imag)
    return cosine * quad_real - sine * quad_imag, sine * quad_real + cosine * quad_imag


def split(value):
    high = value.astype(jnp.bfloat16)
    low = (value - high.astype(jnp.float32)).astype(jnp.bfloat16)
    return high, low


def lanes_at(index):
    return pl.ds(pl.multiple_of(index * LANES, LANES), LANES)


def place_of(step):
    down, across = lax.rem(step, 4), lax.div(step, 4)
    y = lax.axis_index("y") ^ down ^ lax.div(down, 2)
    x = lax.axis_index("x") ^ across ^ lax.div(across, 2)
    return y * 4 + x


def own_place():
    return lax.axis_index("y") * 4 + lax.axis_index("x")


def pack_kernel(section_ref, pops_ref, pos_ref, det_ref, block_ref, pos_out, det_out, sems):
    own = own_place() * 4 + lax.axis_index("zh") * 2 + lax.axis_index("c")
    moves = [
        pltpu.make_async_copy(section_ref.at[0], block_ref.at[pl.ds(0, 16)], sems.at[0]),
        pltpu.make_async_copy(section_ref.at[1], block_ref.at[pl.ds(16, 16)], sems.at[1]),
        pltpu.make_async_copy(pops_ref, block_ref.at[pl.ds(32, 1)], sems.at[2]),
        pltpu.make_async_copy(pos_ref, pos_out, sems.at[3]),
        pltpu.make_async_copy(det_ref.at[:, lanes_at(own)], det_out.at[pl.ds(0, 1)], sems.at[4]),
        pltpu.make_async_copy(det_ref.at[:, pl.ds(0, LANES)], det_out.at[pl.ds(1, 1)], sems.at[5]),
    ]
    for move in moves:
        move.start()
    for move in moves:
        move.wait()
    top = lax.broadcasted_iota(jnp.int32, (8, LANES), 0) == 0
    block_ref[32:PART, :] = jnp.where(top, 2.0 * block_ref[32:PART, :] - 1.0, 0.0)


def pair_kernel(block_ref, one_ref, after_ref, both_ref, token_ref):
    both_ref[0] = block_ref[...]
    both_ref[1] = one_ref[...]
    token_ref[...] = block_ref[0:8, :]


def line_kernel(both_ref, two_ref, near_ref, after_ref, all_ref, token_ref):
    all_ref[0:2] = both_ref[...]
    all_ref[2:4] = two_ref[...]
    token_ref[...] = both_ref[0, 0:8, :]


def turned(pos_ref, k, index):
    line = pos_ref[k : k + 1, lanes_at(index)]
    return jnp.broadcast_to(line, (LANES, LANES)).T


def fill_tiles(pos_ref, row_ref, high_ref, low_ref, quads, first, count, begin=0, end=16):
    quad = lax.axis_index("zh") * 2 + lax.axis_index("c")
    place = own_place()
    for n, other in enumerate(quads):
        for k in range(3):
            row_ref[k, n * LANES : (n + 1) * LANES, :] = turned(pos_ref, k, place * 4 + other)

    together = 4 * LANES // count

    def tile(group, carry):
        for step in [group * together + n for n in range(together)]:
            at = lanes_at(place_of(step) * 4 + quad)
            cols = [pos_ref[k : k + 1, at] for k in range(3)]
            for n in range(0, count, 32):
                dx, dy, dz = [row_ref[k, first + n : first + n + 32, :] - cols[k] for k in range(3)]
                for part, value in enumerate(coupling(dx, dy, dz)):
                    high, low = split(value)
                    lanes = lanes_at(step - begin + part * (end - begin))
                    high_ref[n : n + 32, lanes] = high
                    low_ref[n : n + 32, lanes] = low
        return carry

    lax.fori_loop(begin // together, end // together, tile, 0)


def term_kernel(pos_ref, slab_ref, near_ref, pair_ref, det_ref, rest_ref, row_ref, full_ref):
    own = lax.axis_index("zl")
    start = pl.multiple_of(own * 16, 16)
    offsets = []
    for k in range(3):
        row_ref[k] = turned(pos_ref, k, 0)
        offsets.append(row_ref[k, pl.ds(start, 16), :] - pos_ref[k : k + 1, 0:LANES])
    w_real, w_imag = coupling(*offsets)
    eye = (lax.broadcasted_iota(jnp.int32, (16, LANES), 0) + start) == lax.broadcasted_iota(jnp.int32, (16, LANES), 1)
    w_real = jnp.where(eye, det_ref[1:2, :], w_real)[:, 0:64]
    w_imag = jnp.where(eye, -0.5, w_imag)[:, 0:64]
    for n, ref in enumerate((slab_ref, near_ref, pair_ref.at[0], pair_ref.at[1])):
        place = own + (n % 2) * (1 - 2 * (own % 2))
        place = place + (n // 2) * (2 - 4 * (own // 2))
        there = pl.ds(pl.multiple_of(place * 16, 16), 16)
        full_ref[0, there, :] = ref[0:16]
        full_ref[1, there, :] = ref[16:32]

    def mul(a, b):
        return jnp.dot(a, b, precision=lax.Precision.HIGHEST, preferred_element_type=jnp.float32)

    v_real = mul(w_real, full_ref[0]) + mul(w_imag, full_ref[1])
    v_imag = mul(w_real, full_ref[1]) - mul(w_imag, full_ref[0])
    y_real, y_imag = slab_ref[0:16], slab_ref[16:32]
    line = det_ref[0:1, :]
    rest_ref[0] = line * y_imag - 0.5 * y_real - v_imag
    rest_ref[1] = v_real - line * y_real - 0.5 * y_imag


def clear_own(high_ref, low_ref, first):
    eye = lax.broadcasted_iota(jnp.int32, (LANES, LANES), 0) == lax.broadcasted_iota(jnp.int32, (LANES, LANES), 1)
    half = high_ref.shape[1] // 2
    for part in range(2):
        lanes = pl.ds(part * half, LANES)
        for ref in (high_ref, low_ref):
            own = ref[first : first + LANES, lanes].astype(jnp.float32)
            ref[first : first + LANES, lanes] = jnp.where(eye, 0.0, own).astype(jnp.bfloat16)


def own_quads():
    half, core = lax.axis_index("zh"), lax.axis_index("c")
    return half * 2 + 1 - core, half * 2 + core


def block_kernel(far, pos_ref, token_ref, high_ref, low_ref, row_ref):
    half, core = lax.axis_index("zh"), lax.axis_index("c")
    quad = (1 - half) * 2 + (core if far else 1 - core)
    fill_tiles(pos_ref, row_ref, high_ref, low_ref, (quad,), 0, LANES)


def ahead():
    return (1 - lax.axis_index("zh")) * (lax.axis_index("zl") < 2).astype(jnp.int32)


def ahead_kernel(pos_ref, slab_ref, near_ref, token_ref, high_ref, low_ref, pair_ref, row_ref):
    pair_ref[0] = slab_ref[...]
    pair_ref[1] = near_ref[...]

    @pl.when(ahead() == 1)
    def _():
        fill_tiles(pos_ref, row_ref, high_ref, low_ref, own_quads()[:1], 0, LANES)


def early_kernel(pos_ref, token_ref, high_ref, low_ref, row_ref):
    @pl.when((1 - lax.axis_index("zh")) - ahead() == 1)
    def _():
        fill_tiles(pos_ref, row_ref, high_ref, low_ref, own_quads()[:1], 0, LANES)


def fill_slab(refs, y_ref):
    zeros = jnp.zeros((16, LANES), jnp.float32)
    for step in range(16):
        block = refs[step // 4][step % 4]
        pops = jnp.concatenate([block[32:40], zeros[0:8]], axis=0)
        lanes = slice(step * LANES, (step + 1) * LANES)
        for n, value in enumerate((block[0:16], block[16:32], pops)):
            high, low = split(value)
            y_ref[n * 16 : n * 16 + 16, lanes] = high
            y_ref[WIDE + n * 16 : WIDE + n * 16 + 16, lanes] = low
        y_ref[2 * WIDE :, lanes] = jnp.zeros((LANES - 2 * WIDE, LANES), jnp.bfloat16)


def dot_slab(tiles, y):
    return lax.dot_general(tiles, y, (((1,), (1,)), ((), ())), preferred_element_type=jnp.float32)


def store_products(by_real, by_imag, out_ref, at):
    for n in range(by_real.shape[0] // LANES):
        rows = slice(n * LANES, (n + 1) * LANES)
        real, imag = by_real[rows, :].T, by_imag[rows, :].T
        real = real[0:PART] + real[WIDE : WIDE + PART]
        imag = imag[0:32] + imag[WIDE : WIDE + 32]
        out_ref[at + n, 0:16, :] = real[0:16] - imag[16:32]
        out_ref[at + n, 16:32, :] = real[16:32] + imag[0:16]
        out_ref[at + n, 32:PART, :] = real[32:PART]


def products(high_ref, low_ref, y):
    half = high_ref.shape[1] // 2
    by_real = dot_slab(high_ref[:, 0:half], y) + dot_slab(low_ref[:, 0:half], y)
    by_imag = dot_slab(high_ref[:, half:], y) + dot_slab(low_ref[:, half:], y)
    return by_real, by_imag


def send_kernel(high0, low0, high1, low1, high3, low3, pos_ref, all0, all1, all2, all3, out_ref, y_ref, first_ref, row_ref, part_high, part_low):
    fill_slab((all0, all1, all2, all3), y_ref)
    y = y_ref[...]
    store_products(*products(high0, low0, y), out_ref, 0)
    store_products(*products(high1, low1, y), out_ref, 1)

    @pl.when(ahead() == 1)
    def _():
        fill_tiles(pos_ref, row_ref, part_high, part_low, own_quads()[1:], 0, LANES, 0, 4)
        clear_own(part_high, part_low, 0)
        store_products(*products(high3, low3, y), first_ref, 0)
        store_products(*products(part_high, part_low, y[:, 0 : 4 * LANES]), first_ref, 1)


def keep_kernel(pos_ref, y_ref, high2, low2, first_ref, out_ref, row_ref, high_ref, low_ref):
    y = y_ref[...]
    rows = pl.ds(0, LANES)

    @pl.when(ahead() == 1)
    def _():
        high, low = high_ref.at[rows, pl.ds(0, 24 * LANES)], low_ref.at[rows, pl.ds(0, 24 * LANES)]
        fill_tiles(pos_ref, row_ref, high, low, own_quads()[1:], 0, LANES, 4, 16)
        store_products(*products(high, low, y[:, 4 * LANES :]), out_ref, 1)
        out_ref[0] = first_ref[0]
        out_ref[1] += first_ref[1]

    @pl.when((1 - lax.axis_index("zh")) - ahead() == 1)
    def _():
        high, low = high_ref.at[rows], low_ref.at[rows]
        fill_tiles(pos_ref, row_ref, high, low, own_quads()[1:], 0, LANES)
        clear_own(high, low, 0)
        store_products(*products(high, low, y), out_ref, 1)
        store_products(*products(high2, low2, y), out_ref, 0)

    @pl.when(lax.axis_index("zh") == 1)
    def _():
        fill_tiles(pos_ref, row_ref, high_ref, low_ref, own_quads(), 0, 2 * LANES)
        clear_own(high_ref, low_ref, LANES)
        store_products(*products(high_ref, low_ref, y), out_ref, 0)


def finish_kernel(keep_ref, half_ref, core_ref, rest_ref, slab_ref, base_ref, accum_ref, next_ref, acc_ref):
    z = keep_ref[1] + half_ref[1] + core_ref[...]
    shift = z[32:33]
    rate_real = z[16:32] + shift * slab_ref[16:32] + rest_ref[0]
    rate_imag = rest_ref[1] - z[0:16] - shift * slab_ref[0:16]
    for n, rate in enumerate((rate_real, rate_imag)):
        next_ref[n] = base_ref[n] + (0.5 * TIME_STEP) * rate
        acc_ref[n] = accum_ref[n] + (TIME_STEP / 3.0) * rate


def params(mib):
    return pltpu.CompilerParams(vmem_limit_bytes=mib << 20)


def in_hbm(array):
    return pltpu.with_memory_space_constraint(array, pltpu.HBM)


def local(positions, detuning, populations, base, section, accum):
    bf16, f32 = jnp.bfloat16, jnp.float32
    count = positions.shape[1]
    tiles = count // (4 * LANES)
    deep = 2 * tiles * LANES
    hbm, vmem = pl.BlockSpec(memory_space=pltpu.HBM), pl.BlockSpec(memory_space=pltpu.VMEM)
    anywhere = pl.BlockSpec(memory_space=pl.ANY)
    tile = pltpu.VMEM((LANES, deep), bf16)
    token = pltpu.VMEM((8, LANES), f32)
    rows = pltpu.VMEM((3, LANES, LANES), f32)

    def call(kernel, name, out_shape, in_specs, flops, scratch=()):
        return pl.pallas_call(
            kernel,
            out_shape=out_shape,
            in_specs=in_specs,
            out_specs=[vmem] * len(out_shape),
            scratch_shapes=scratch,
            compiler_params=params(6),
            cost_estimate=pl.CostEstimate(flops=flops, bytes_accessed=1 << 20, transcendentals=0),
            name=name,
        )

    def swap(array, axis, mask):
        size = lax.axis_size(axis)
        return lax.ppermute(array, axis, [(i, i ^ mask) for i in range(size)])

    def far_block(n, after):
        kernel = functools.partial(block_kernel, n)
        return call(kernel, "far_block_" + "ab"[n], (tile, tile), [vmem, anywhere], 1 << 24, [rows])(pos, after)

    block, pos, det = call(
        pack_kernel,
        "pack_block",
        (pltpu.VMEM((PART, LANES), f32), pltpu.VMEM(positions.shape, f32), token),
        [hbm] * 4,
        1 << 16,
        [pltpu.SemaphoreType.DMA((6,))],
    )(in_hbm(section), in_hbm(populations.reshape(1, LANES)), in_hbm(positions), in_hbm(detuning.reshape(1, count)))
    one = swap(block, "y", 1)
    near = swap(block, "zl", 1)
    high0, low0 = far_block(0, det)

    both, second = call(
        pair_kernel, "join_pair", (pltpu.VMEM((2, PART, LANES), f32), token), [vmem, vmem, anywhere], 1
    )(block, one, high0)
    two = swap(both, "y", 3)
    high1, low1 = far_block(1, second)

    line, third = call(
        line_kernel, "join_line", (pltpu.VMEM((4, PART, LANES), f32), token), [vmem] * 3 + [anywhere], 1
    )(both, two, near, high1)
    across = [swap(line, "x", mask) for mask in (1, 3, 2)]
    high3, low3, pair = call(
        ahead_kernel,
        "ahead_block",
        (tile, tile, pltpu.VMEM((2, PART, LANES), f32)),
        [vmem] * 3 + [anywhere],
        1 << 24,
        [rows],
    )(pos, block, near, third)
    pair = swap(pair, "zl", 2)
    high2, low2 = call(
        early_kernel, "early_block", (tile, tile), [vmem, anywhere], 1 << 24, [rows]
    )(pos, high3)

    sent, y, first = call(
        send_kernel,
        "send_products",
        (
            pltpu.VMEM((2, PART, LANES), f32),
            pltpu.VMEM((LANES, deep // 2), bf16),
            pltpu.VMEM((2, PART, LANES), f32),
        ),
        [vmem] * 11,
        1 << 29,
        [rows, pltpu.VMEM((LANES, 8 * LANES), bf16), pltpu.VMEM((LANES, 8 * LANES), bf16)],
    )(high0, low0, high1, low1, high3, low3, pos, line, *across)
    half = swap(sent, "zh", 1)

    wide = pltpu.VMEM((2 * LANES, deep), bf16)
    (keep,) = call(
        keep_kernel,
        "keep_products",
        (pltpu.VMEM((2, PART, LANES), f32),),
        [vmem] * 5,
        1 << 29,
        [pltpu.VMEM((3, 2 * LANES, LANES), f32), wide, wide],
    )(pos, y, high2, low2, first)
    core = lax.ppermute(keep[0] + half[0], "c", [(0, 1), (1, 0)])
    rest = pl.pallas_call(
        term_kernel,
        out_shape=pltpu.VMEM((2, 16, LANES), f32),
        in_specs=[vmem] * 5,
        out_specs=vmem,
        scratch_shapes=[pltpu.VMEM((3, LANES, LANES), f32), pltpu.VMEM((2, 64, LANES), f32)],
        compiler_params=params(4),
        cost_estimate=pl.CostEstimate(flops=1 << 22, bytes_accessed=1 << 18, transcendentals=1 << 11),
        name="slab_term",
    )(pos, block, near, pair, det)

    return pl.pallas_call(
        finish_kernel,
        out_shape=(jax.ShapeDtypeStruct(base.shape, f32),) * 2,
        compiler_params=params(4),
        cost_estimate=pl.CostEstimate(flops=1 << 16, bytes_accessed=1 << 18, transcendentals=0),
        name="finish_rate",
    )(keep, half, core, rest, block, base, accum)


def solution(mesh):
    fine = Mesh(mesh.devices.reshape(4, 4, 2, 2, 4), ("y", "x", "zh", "c", "zl"))
    rows = ("y", "x", "zh", "c")
    slab = P(None, "zl", rows)
    return jax.shard_map(
        local,
        mesh=fine,
        in_specs=(P(), P(), P(rows), slab, slab, slab),
        out_specs=(slab, slab),
        check_vma=False,
    )
```

```python
import functools
import math

import jax
import jax.numpy as jnp
from jax import lax
from jax.experimental import pallas as pl
from jax.experimental.pallas import tpu as pltpu
from jax.sharding import Mesh
from jax.sharding import PartitionSpec as P

TIME_STEP = 0.2
LANES = 128
COS = (0.9999992211, -19.73898242, 64.92872338, -85.27236068, 58.79387231, -21.07651549)
SIN = (6.283182817, -41.3414213, 81.59618177, -76.58008122, 41.20531753, -12.27114973)
SCALE = -0.75 / (2.0 * math.pi)
INV_WAVE = 1.0 / (2.0 * math.pi)
ROUNDER = 12582912.0
PART = 40
WIDE = 48


def horner(coefs, scale, arg):
    total = jnp.float32(coefs[-1] * scale)
    for c in coefs[-2::-1]:
        total = total * arg + jnp.float32(c * scale)
    return total


def coupling(dx, dy, dz):
    dz_sq = dz * dz
    dist_sq = dx * dx + dy * dy + dz_sq
    inv = lax.rsqrt(dist_sq)
    dist = dist_sq * inv
    turn = dist - ((dist + ROUNDER) - ROUNDER)
    turn_sq = turn * turn
    cosine = horner(COS, SCALE, turn_sq)
    sine = horner(SIN, SCALE, turn_sq) * turn
    inv_sq = inv * inv
    aligned = dz_sq * inv_sq
    quad_imag = inv_sq * (INV_WAVE - (3.0 * INV_WAVE) * aligned)
    quad_real = inv * ((1.0 - aligned) - INV_WAVE * quad_imag)
    return cosine * quad_real - sine * quad_imag, sine * quad_real + cosine * quad_imag


def split(value):
    high = value.astype(jnp.bfloat16)
    low = (value - high.astype(jnp.float32)).astype(jnp.bfloat16)
    return high, low


def lanes_at(index):
    return pl.ds(pl.multiple_of(index * LANES, LANES), LANES)


def place_of(step):
    down, across = lax.rem(step, 4), lax.div(step, 4)
    y = lax.axis_index("y") ^ down ^ lax.div(down, 2)
    x = lax.axis_index("x") ^ across ^ lax.div(across, 2)
    return y * 4 + x


def own_place():
    return lax.axis_index("y") * 4 + lax.axis_index("x")


def pack_kernel(section_ref, pops_ref, pos_ref, det_ref, block_ref, pos_out, det_out, sems):
    own = own_place() * 4 + lax.axis_index("zh") * 2 + lax.axis_index("c")
    moves = [
        pltpu.make_async_copy(section_ref.at[0], block_ref.at[pl.ds(0, 16)], sems.at[0]),
        pltpu.make_async_copy(section_ref.at[1], block_ref.at[pl.ds(16, 16)], sems.at[1]),
        pltpu.make_async_copy(pops_ref, block_ref.at[pl.ds(32, 1)], sems.at[2]),
        pltpu.make_async_copy(pos_ref, pos_out, sems.at[3]),
        pltpu.make_async_copy(det_ref.at[:, lanes_at(own)], det_out.at[pl.ds(0, 1)], sems.at[4]),
        pltpu.make_async_copy(det_ref.at[:, pl.ds(0, LANES)], det_out.at[pl.ds(1, 1)], sems.at[5]),
    ]
    for move in moves:
        move.start()
    for move in moves:
        move.wait()
    top = lax.broadcasted_iota(jnp.int32, (8, LANES), 0) == 0
    block_ref[32:PART, :] = jnp.where(top, 2.0 * block_ref[32:PART, :] - 1.0, 0.0)


def pair_kernel(block_ref, one_ref, after_ref, both_ref, token_ref):
    both_ref[0] = block_ref[...]
    both_ref[1] = one_ref[...]
    token_ref[...] = block_ref[0:8, :]


def line_kernel(both_ref, two_ref, near_ref, after_ref, all_ref, token_ref):
    all_ref[0:2] = both_ref[...]
    all_ref[2:4] = two_ref[...]
    token_ref[...] = both_ref[0, 0:8, :]


def turned(pos_ref, k, index):
    line = pos_ref[k : k + 1, lanes_at(index)]
    return jnp.broadcast_to(line, (LANES, LANES)).T


def fill_tiles(pos_ref, row_ref, high_ref, low_ref, quads, first, count, begin=0, end=16):
    quad = lax.axis_index("zh") * 2 + lax.axis_index("c")
    place = own_place()
    for n, other in enumerate(quads):
        for k in range(3):
            row_ref[k, n * LANES : (n + 1) * LANES, :] = turned(pos_ref, k, place * 4 + other)

    together = 4 * LANES // count

    def tile(group, carry):
        for step in [group * together + n for n in range(together)]:
            at = lanes_at(place_of(step) * 4 + quad)
            cols = [pos_ref[k : k + 1, at] for k in range(3)]
            for n in range(0, count, 32):
                dx, dy, dz = [row_ref[k, first + n : first + n + 32, :] - cols[k] for k in range(3)]
                for part, value in enumerate(coupling(dx, dy, dz)):
                    high, low = split(value)
                    lanes = lanes_at(step - begin + part * (end - begin))
                    high_ref[n : n + 32, lanes] = high
                    low_ref[n : n + 32, lanes] = low
        return carry

    lax.fori_loop(begin // together, end // together, tile, 0)


def term_kernel(pos_ref, slab_ref, near_ref, pair_ref, det_ref, rest_ref, row_ref, full_ref):
    own = lax.axis_index("zl")
    start = pl.multiple_of(own * 16, 16)
    offsets = []
    for k in range(3):
        row_ref[k] = turned(pos_ref, k, 0)
        offsets.append(row_ref[k, pl.ds(start, 16), :] - pos_ref[k : k + 1, 0:LANES])
    w_real, w_imag = coupling(*offsets)
    eye = (lax.broadcasted_iota(jnp.int32, (16, LANES), 0) + start) == lax.broadcasted_iota(jnp.int32, (16, LANES), 1)
    w_real = jnp.where(eye, det_ref[1:2, :], w_real)[:, 0:64]
    w_imag = jnp.where(eye, -0.5, w_imag)[:, 0:64]
    for n, ref in enumerate((slab_ref, near_ref, pair_ref.at[0], pair_ref.at[1])):
        place = own + (n % 2) * (1 - 2 * (own % 2))
        place = place + (n // 2) * (2 - 4 * (own // 2))
        there = pl.ds(pl.multiple_of(place * 16, 16), 16)
        full_ref[0, there, :] = ref[0:16]
        full_ref[1, there, :] = ref[16:32]

    def mul(a, b):
        return jnp.dot(a, b, precision=lax.Precision.HIGHEST, preferred_element_type=jnp.float32)

    v_real = mul(w_real, full_ref[0]) + mul(w_imag, full_ref[1])
    v_imag = mul(w_real, full_ref[1]) - mul(w_imag, full_ref[0])
    y_real, y_imag = slab_ref[0:16], slab_ref[16:32]
    line = det_ref[0:1, :]
    rest_ref[0] = line * y_imag - 0.5 * y_real - v_imag
    rest_ref[1] = v_real - line * y_real - 0.5 * y_imag


def clear_own(high_ref, low_ref, first):
    eye = lax.broadcasted_iota(jnp.int32, (LANES, LANES), 0) == lax.broadcasted_iota(jnp.int32, (LANES, LANES), 1)
    half = high_ref.shape[1] // 2
    for part in range(2):
        lanes = pl.ds(part * half, LANES)
        for ref in (high_ref, low_ref):
            own = ref[first : first + LANES, lanes].astype(jnp.float32)
            ref[first : first + LANES, lanes] = jnp.where(eye, 0.0, own).astype(jnp.bfloat16)


def own_quads():
    half, core = lax.axis_index("zh"), lax.axis_index("c")
    return half * 2 + 1 - core, half * 2 + core


def block_kernel(far, pos_ref, token_ref, high_ref, low_ref, row_ref):
    half, core = lax.axis_index("zh"), lax.axis_index("c")
    quad = (1 - half) * 2 + (core if far else 1 - core)
    fill_tiles(pos_ref, row_ref, high_ref, low_ref, (quad,), 0, LANES)


def ahead():
    return (1 - lax.axis_index("zh")) * (lax.axis_index("zl") < 2).astype(jnp.int32)


def ahead_kernel(pos_ref, slab_ref, near_ref, token_ref, high_ref, low_ref, pair_ref, row_ref):
    pair_ref[0] = slab_ref[...]
    pair_ref[1] = near_ref[...]

    @pl.when(ahead() == 1)
    def _():
        fill_tiles(pos_ref, row_ref, high_ref, low_ref, own_quads()[:1], 0, LANES)


def early_kernel(pos_ref, token_ref, high_ref, low_ref, row_ref):
    @pl.when((1 - lax.axis_index("zh")) - ahead() == 1)
    def _():
        fill_tiles(pos_ref, row_ref, high_ref, low_ref, own_quads()[:1], 0, LANES, 0, 12)


def fill_slab(refs, y_ref):
    zeros = jnp.zeros((16, LANES), jnp.float32)
    for step in range(16):
        block = refs[step // 4][step % 4]
        pops = jnp.concatenate([block[32:40], zeros[0:8]], axis=0)
        lanes = slice(step * LANES, (step + 1) * LANES)
        for n, value in enumerate((block[0:16], block[16:32], pops)):
            high, low = split(value)
            y_ref[n * 16 : n * 16 + 16, lanes] = high
            y_ref[WIDE + n * 16 : WIDE + n * 16 + 16, lanes] = low
        y_ref[2 * WIDE :, lanes] = jnp.zeros((LANES - 2 * WIDE, LANES), jnp.bfloat16)


def dot_slab(tiles, y):
    return lax.dot_general(tiles, y, (((1,), (1,)), ((), ())), preferred_element_type=jnp.float32)


def store_products(by_real, by_imag, out_ref, at):
    for n in range(by_real.shape[0] // LANES):
        rows = slice(n * LANES, (n + 1) * LANES)
        real, imag = by_real[rows, :].T, by_imag[rows, :].T
        real = real[0:PART] + real[WIDE : WIDE + PART]
        imag = imag[0:32] + imag[WIDE : WIDE + 32]
        out_ref[at + n, 0:16, :] = real[0:16] - imag[16:32]
        out_ref[at + n, 16:32, :] = real[16:32] + imag[0:16]
        out_ref[at + n, 32:PART, :] = real[32:PART]


def products(high_ref, low_ref, y):
    half = high_ref.shape[1] // 2
    by_real = dot_slab(high_ref[:, 0:half], y) + dot_slab(low_ref[:, 0:half], y)
    by_imag = dot_slab(high_ref[:, half:], y) + dot_slab(low_ref[:, half:], y)
    return by_real, by_imag


def send_kernel(high0, low0, high1, low1, pos_ref, all0, all1, all2, all3, out_ref, y_ref, first_ref, row_ref, part_high, part_low):
    fill_slab((all0, all1, all2, all3), y_ref)
    y = y_ref[...]
    store_products(*products(high0, low0, y), out_ref, 0)
    store_products(*products(high1, low1, y), out_ref, 1)

    @pl.when(ahead() == 1)
    def _():
        fill_tiles(pos_ref, row_ref, part_high, part_low, own_quads()[1:], 0, LANES, 0, 4)
        clear_own(part_high, part_low, 0)
        store_products(*products(part_high, part_low, y[:, 0 : 4 * LANES]), first_ref, 0)


def keep_kernel(pos_ref, y_ref, high2, low2, high3, low3, first_ref, out_ref, row_ref, high_ref, low_ref):
    y = y_ref[...]
    rows = pl.ds(0, LANES)

    @pl.when(ahead() == 1)
    def _():
        high, low = high_ref.at[rows, pl.ds(0, 24 * LANES)], low_ref.at[rows, pl.ds(0, 24 * LANES)]
        fill_tiles(pos_ref, row_ref, high, low, own_quads()[1:], 0, LANES, 4, 16)
        store_products(*products(high, low, y[:, 4 * LANES :]), out_ref, 1)
        store_products(*products(high3, low3, y), out_ref, 0)
        out_ref[1] += first_ref[0]

    @pl.when((1 - lax.axis_index("zh")) - ahead() == 1)
    def _():
        high, low = high_ref.at[rows], low_ref.at[rows]
        fill_tiles(pos_ref, row_ref, high, low, own_quads()[1:], 0, LANES)
        clear_own(high, low, 0)
        store_products(*products(high, low, y), out_ref, 1)
        late_high = high_ref.at[pl.ds(LANES, LANES), pl.ds(0, 8 * LANES)]
        late_low = low_ref.at[pl.ds(LANES, LANES), pl.ds(0, 8 * LANES)]
        fill_tiles(pos_ref, row_ref, late_high, late_low, own_quads()[:1], 0, LANES, 12, 16)
        most = products(high2, low2, y[:, 0 : 12 * LANES])
        more = products(late_high, late_low, y[:, 12 * LANES :])
        store_products(most[0] + more[0], most[1] + more[1], out_ref, 0)

    @pl.when(lax.axis_index("zh") == 1)
    def _():
        fill_tiles(pos_ref, row_ref, high_ref, low_ref, own_quads(), 0, 2 * LANES)
        clear_own(high_ref, low_ref, LANES)
        store_products(*products(high_ref, low_ref, y), out_ref, 0)


def finish_kernel(keep_ref, half_ref, core_ref, rest_ref, slab_ref, base_ref, accum_ref, next_ref, acc_ref):
    z = keep_ref[1] + half_ref[1] + core_ref[...]
    shift = z[32:33]
    rate_real = z[16:32] + shift * slab_ref[16:32] + rest_ref[0]
    rate_imag = rest_ref[1] - z[0:16] - shift * slab_ref[0:16]
    for n, rate in enumerate((rate_real, rate_imag)):
        next_ref[n] = base_ref[n] + (0.5 * TIME_STEP) * rate
        acc_ref[n] = accum_ref[n] + (TIME_STEP / 3.0) * rate


def params(mib):
    return pltpu.CompilerParams(vmem_limit_bytes=mib << 20)


def in_hbm(array):
    return pltpu.with_memory_space_constraint(array, pltpu.HBM)


def local(positions, detuning, populations, base, section, accum):
    bf16, f32 = jnp.bfloat16, jnp.float32
    count = positions.shape[1]
    tiles = count // (4 * LANES)
    deep = 2 * tiles * LANES
    hbm, vmem = pl.BlockSpec(memory_space=pltpu.HBM), pl.BlockSpec(memory_space=pltpu.VMEM)
    anywhere = pl.BlockSpec(memory_space=pl.ANY)
    tile = pltpu.VMEM((LANES, deep), bf16)
    token = pltpu.VMEM((8, LANES), f32)
    rows = pltpu.VMEM((3, LANES, LANES), f32)

    def call(kernel, name, out_shape, in_specs, flops, scratch=()):
        return pl.pallas_call(
            kernel,
            out_shape=out_shape,
            in_specs=in_specs,
            out_specs=[vmem] * len(out_shape),
            scratch_shapes=scratch,
            compiler_params=params(12),
            cost_estimate=pl.CostEstimate(flops=flops, bytes_accessed=1 << 20, transcendentals=0),
            name=name,
        )

    def swap(array, axis, mask):
        size = lax.axis_size(axis)
        return lax.ppermute(array, axis, [(i, i ^ mask) for i in range(size)])

    def far_block(n, after):
        kernel = functools.partial(block_kernel, n)
        return call(kernel, "far_block_" + "ab"[n], (tile, tile), [vmem, anywhere], 1 << 24, [rows])(pos, after)

    block, pos, det = call(
        pack_kernel,
        "pack_block",
        (pltpu.VMEM((PART, LANES), f32), pltpu.VMEM(positions.shape, f32), token),
        [hbm] * 4,
        1 << 16,
        [pltpu.SemaphoreType.DMA((6,))],
    )(in_hbm(section), in_hbm(populations.reshape(1, LANES)), in_hbm(positions), in_hbm(detuning.reshape(1, count)))
    one = swap(block, "y", 1)
    near = swap(block, "zl", 1)
    high0, low0 = far_block(0, det)

    both, second = call(
        pair_kernel, "join_pair", (pltpu.VMEM((2, PART, LANES), f32), token), [vmem, vmem, anywhere], 1
    )(block, one, high0)
    two = swap(both, "y", 3)
    high1, low1 = far_block(1, second)

    line, third = call(
        line_kernel, "join_line", (pltpu.VMEM((4, PART, LANES), f32), token), [vmem] * 3 + [anywhere], 1
    )(both, two, near, high1)
    across = [swap(line, "x", mask) for mask in (1, 3, 2)]
    high3, low3, pair = call(
        ahead_kernel,
        "ahead_block",
        (tile, tile, pltpu.VMEM((2, PART, LANES), f32)),
        [vmem] * 3 + [anywhere],
        1 << 24,
        [rows],
    )(pos, block, near, third)
    pair = swap(pair, "zl", 2)
    most = pltpu.VMEM((LANES, 24 * LANES), bf16)
    high2, low2 = call(
        early_kernel, "early_block", (most, most), [vmem, anywhere], 1 << 24, [rows]
    )(pos, high3)

    sent, y, first = call(
        send_kernel,
        "send_products",
        (
            pltpu.VMEM((2, PART, LANES), f32),
            pltpu.VMEM((LANES, deep // 2), bf16),
            pltpu.VMEM((1, PART, LANES), f32),
        ),
        [vmem] * 9,
        1 << 29,
        [rows, pltpu.VMEM((LANES, 8 * LANES), bf16), pltpu.VMEM((LANES, 8 * LANES), bf16)],
    )(high0, low0, high1, low1, pos, line, *across)
    half = swap(sent, "zh", 1)

    wide = pltpu.VMEM((2 * LANES, deep), bf16)
    (keep,) = call(
        keep_kernel,
        "keep_products",
        (pltpu.VMEM((2, PART, LANES), f32),),
        [vmem] * 7,
        1 << 29,
        [pltpu.VMEM((3, 2 * LANES, LANES), f32), wide, wide],
    )(pos, y, high2, low2, high3, low3, first)
    core = lax.ppermute(keep[0] + half[0], "c", [(0, 1), (1, 0)])
    rest = pl.pallas_call(
        term_kernel,
        out_shape=pltpu.VMEM((2, 16, LANES), f32),
        in_specs=[vmem] * 5,
        out_specs=vmem,
        scratch_shapes=[pltpu.VMEM((3, LANES, LANES), f32), pltpu.VMEM((2, 64, LANES), f32)],
        compiler_params=params(4),
        cost_estimate=pl.CostEstimate(flops=1 << 22, bytes_accessed=1 << 18, transcendentals=1 << 11),
        name="slab_term",
    )(pos, block, near, pair, det)

    return pl.pallas_call(
        finish_kernel,
        out_shape=(jax.ShapeDtypeStruct(base.shape, f32),) * 2,
        compiler_params=params(4),
        cost_estimate=pl.CostEstimate(flops=1 << 16, bytes_accessed=1 << 18, transcendentals=0),
        name="finish_rate",
    )(keep, half, core, rest, block, base, accum)


def solution(mesh):
    fine = Mesh(mesh.devices.reshape(4, 4, 2, 2, 4), ("y", "x", "zh", "c", "zl"))
    rows = ("y", "x", "zh", "c")
    slab = P(None, "zl", rows)
    return jax.shard_map(
        local,
        mesh=fine,
        in_specs=(P(), P(), P(rows), slab, slab, slab),
        out_specs=(slab, slab),
        check_vma=False,
    )
```

```python
import functools
import math

import jax
import jax.numpy as jnp
from jax import lax
from jax.experimental import pallas as pl
from jax.experimental.pallas import tpu as pltpu
from jax.sharding import Mesh
from jax.sharding import PartitionSpec as P

TIME_STEP = 0.2
LANES = 128
COS = (0.9999992211, -19.73898242, 64.92872338, -85.27236068, 58.79387231, -21.07651549)
SIN = (6.283182817, -41.3414213, 81.59618177, -76.58008122, 41.20531753, -12.27114973)
SCALE = -0.75 / (2.0 * math.pi)
INV_WAVE = 1.0 / (2.0 * math.pi)
ROUNDER = 12582912.0
PART = 40
WIDE = 48


def horner(coefs, scale, arg):
    total = jnp.float32(coefs[-1] * scale)
    for c in coefs[-2::-1]:
        total = total * arg + jnp.float32(c * scale)
    return total


def coupling(dx, dy, dz):
    dz_sq = dz * dz
    dist_sq = dx * dx + dy * dy + dz_sq
    inv = lax.rsqrt(dist_sq)
    dist = dist_sq * inv
    turn = dist - ((dist + ROUNDER) - ROUNDER)
    turn_sq = turn * turn
    cosine = horner(COS, SCALE, turn_sq)
    sine = horner(SIN, SCALE, turn_sq) * turn
    inv_sq = inv * inv
    aligned = dz_sq * inv_sq
    quad_imag = inv_sq * (INV_WAVE - (3.0 * INV_WAVE) * aligned)
    quad_real = inv * ((1.0 - aligned) - INV_WAVE * quad_imag)
    return cosine * quad_real - sine * quad_imag, sine * quad_real + cosine * quad_imag


def split(value):
    high = value.astype(jnp.bfloat16)
    low = (value - high.astype(jnp.float32)).astype(jnp.bfloat16)
    return high, low


def lanes_at(index):
    return pl.ds(pl.multiple_of(index * LANES, LANES), LANES)


def place_of(step):
    down, across = lax.rem(step, 4), lax.div(step, 4)
    y = lax.axis_index("y") ^ down ^ lax.div(down, 2)
    x = lax.axis_index("x") ^ across ^ lax.div(across, 2)
    return y * 4 + x


def own_place():
    return lax.axis_index("y") * 4 + lax.axis_index("x")


def pack_kernel(section_ref, pops_ref, pos_ref, det_ref, block_ref, pos_out, det_out, sems):
    own = own_place() * 4 + lax.axis_index("zh") * 2 + lax.axis_index("c")
    moves = [
        pltpu.make_async_copy(section_ref.at[0], block_ref.at[pl.ds(0, 16)], sems.at[0]),
        pltpu.make_async_copy(section_ref.at[1], block_ref.at[pl.ds(16, 16)], sems.at[1]),
        pltpu.make_async_copy(pops_ref, block_ref.at[pl.ds(32, 1)], sems.at[2]),
        pltpu.make_async_copy(pos_ref, pos_out, sems.at[3]),
        pltpu.make_async_copy(det_ref.at[:, lanes_at(own)], det_out.at[pl.ds(0, 1)], sems.at[4]),
        pltpu.make_async_copy(det_ref.at[:, pl.ds(0, LANES)], det_out.at[pl.ds(1, 1)], sems.at[5]),
    ]
    for move in moves:
        move.start()
    for move in moves:
        move.wait()
    top = lax.broadcasted_iota(jnp.int32, (8, LANES), 0) == 0
    block_ref[32:PART, :] = jnp.where(top, 2.0 * block_ref[32:PART, :] - 1.0, 0.0)


def pair_kernel(block_ref, one_ref, after_ref, both_ref, token_ref):
    both_ref[0] = block_ref[...]
    both_ref[1] = one_ref[...]
    token_ref[...] = block_ref[0:8, :]


def line_kernel(both_ref, two_ref, near_ref, after_ref, all_ref, token_ref):
    all_ref[0:2] = both_ref[...]
    all_ref[2:4] = two_ref[...]
    token_ref[...] = both_ref[0, 0:8, :]


def turned(pos_ref, k, index):
    line = pos_ref[k : k + 1, lanes_at(index)]
    return jnp.broadcast_to(line, (LANES, LANES)).T


def fill_tiles(pos_ref, row_ref, high_ref, low_ref, quads, first, count, begin=0, end=16):
    quad = lax.axis_index("zh") * 2 + lax.axis_index("c")
    place = own_place()
    for n, other in enumerate(quads):
        for k in range(3):
            row_ref[k, n * LANES : (n + 1) * LANES, :] = turned(pos_ref, k, place * 4 + other)

    together = 4 * LANES // count

    def tile(group, carry):
        for step in [group * together + n for n in range(together)]:
            at = lanes_at(place_of(step) * 4 + quad)
            cols = [pos_ref[k : k + 1, at] for k in range(3)]
            for n in range(0, count, 32):
                dx, dy, dz = [row_ref[k, first + n : first + n + 32, :] - cols[k] for k in range(3)]
                for part, value in enumerate(coupling(dx, dy, dz)):
                    high, low = split(value)
                    lanes = lanes_at(step - begin + part * (end - begin))
                    high_ref[n : n + 32, lanes] = high
                    low_ref[n : n + 32, lanes] = low
        return carry

    lax.fori_loop(begin // together, end // together, tile, 0)


def term_kernel(pos_ref, slab_ref, near_ref, pair_ref, det_ref, rest_ref, row_ref, full_ref):
    own = lax.axis_index("zl")
    start = pl.multiple_of(own * 16, 16)
    offsets = []
    for k in range(3):
        row_ref[k] = turned(pos_ref, k, 0)
        offsets.append(row_ref[k, pl.ds(start, 16), :] - pos_ref[k : k + 1, 0:LANES])
    w_real, w_imag = coupling(*offsets)
    eye = (lax.broadcasted_iota(jnp.int32, (16, LANES), 0) + start) == lax.broadcasted_iota(jnp.int32, (16, LANES), 1)
    w_real = jnp.where(eye, det_ref[1:2, :], w_real)[:, 0:64]
    w_imag = jnp.where(eye, -0.5, w_imag)[:, 0:64]
    for n, ref in enumerate((slab_ref, near_ref, pair_ref.at[0], pair_ref.at[1])):
        place = own + (n % 2) * (1 - 2 * (own % 2))
        place = place + (n // 2) * (2 - 4 * (own // 2))
        there = pl.ds(pl.multiple_of(place * 16, 16), 16)
        full_ref[0, there, :] = ref[0:16]
        full_ref[1, there, :] = ref[16:32]

    def mul(a, b):
        return jnp.dot(a, b, precision=lax.Precision.HIGHEST, preferred_element_type=jnp.float32)

    v_real = mul(w_real, full_ref[0]) + mul(w_imag, full_ref[1])
    v_imag = mul(w_real, full_ref[1]) - mul(w_imag, full_ref[0])
    y_real, y_imag = slab_ref[0:16], slab_ref[16:32]
    line = det_ref[0:1, :]
    rest_ref[0] = line * y_imag - 0.5 * y_real - v_imag
    rest_ref[1] = v_real - line * y_real - 0.5 * y_imag


def clear_own(high_ref, low_ref, first):
    eye = lax.broadcasted_iota(jnp.int32, (LANES, LANES), 0) == lax.broadcasted_iota(jnp.int32, (LANES, LANES), 1)
    half = high_ref.shape[1] // 2
    for part in range(2):
        lanes = pl.ds(part * half, LANES)
        for ref in (high_ref, low_ref):
            own = ref[first : first + LANES, lanes].astype(jnp.float32)
            ref[first : first + LANES, lanes] = jnp.where(eye, 0.0, own).astype(jnp.bfloat16)


def own_quads():
    half, core = lax.axis_index("zh"), lax.axis_index("c")
    return half * 2 + 1 - core, half * 2 + core


def block_kernel(far, pos_ref, token_ref, high_ref, low_ref, row_ref):
    half, core = lax.axis_index("zh"), lax.axis_index("c")
    quad = (1 - half) * 2 + (core if far else 1 - core)
    fill_tiles(pos_ref, row_ref, high_ref, low_ref, (quad,), 0, LANES)


def ahead():
    return (1 - lax.axis_index("zh")) * (lax.axis_index("zl") < 2).astype(jnp.int32)


def ahead_kernel(pos_ref, slab_ref, near_ref, token_ref, high_ref, low_ref, pair_ref, row_ref):
    pair_ref[0] = slab_ref[...]
    pair_ref[1] = near_ref[...]

    @pl.when(ahead() == 1)
    def _():
        fill_tiles(pos_ref, row_ref, high_ref, low_ref, own_quads()[:1], 0, LANES)


def early_kernel(pos_ref, token_ref, high_ref, low_ref, row_ref):
    @pl.when((1 - lax.axis_index("zh")) - ahead() == 1)
    def _():
        fill_tiles(pos_ref, row_ref, high_ref, low_ref, own_quads()[:1], 0, LANES)


def fill_slab(refs, y_ref):
    zeros = jnp.zeros((16, LANES), jnp.float32)
    for step in range(16):
        block = refs[step // 4][step % 4]
        pops = jnp.concatenate([block[32:40], zeros[0:8]], axis=0)
        lanes = slice(step * LANES, (step + 1) * LANES)
        for n, value in enumerate((block[0:16], block[16:32], pops)):
            high, low = split(value)
            y_ref[n * 16 : n * 16 + 16, lanes] = high
            y_ref[WIDE + n * 16 : WIDE + n * 16 + 16, lanes] = low
        y_ref[2 * WIDE :, lanes] = jnp.zeros((LANES - 2 * WIDE, LANES), jnp.bfloat16)


def dot_slab(tiles, y):
    return lax.dot_general(tiles, y, (((1,), (1,)), ((), ())), preferred_element_type=jnp.float32)


def store_products(by_real, by_imag, out_ref, at):
    for n in range(by_real.shape[0] // LANES):
        rows = slice(n * LANES, (n + 1) * LANES)
        real, imag = by_real[rows, :].T, by_imag[rows, :].T
        real = real[0:PART] + real[WIDE : WIDE + PART]
        imag = imag[0:32] + imag[WIDE : WIDE + 32]
        out_ref[at + n, 0:16, :] = real[0:16] - imag[16:32]
        out_ref[at + n, 16:32, :] = real[16:32] + imag[0:16]
        out_ref[at + n, 32:PART, :] = real[32:PART]


def products(high_ref, low_ref, y):
    half = high_ref.shape[1] // 2
    by_real = dot_slab(high_ref[:, 0:half], y) + dot_slab(low_ref[:, 0:half], y)
    by_imag = dot_slab(high_ref[:, half:], y) + dot_slab(low_ref[:, half:], y)
    return by_real, by_imag


def send_kernel(high0, low0, high1, low1, high3, low3, pos_ref, all0, all1, all2, all3, out_ref, y_ref, first_ref, row_ref, part_high, part_low):
    fill_slab((all0, all1, all2, all3), y_ref)
    y = y_ref[...]
    store_products(*products(high0, low0, y), out_ref, 0)
    store_products(*products(high1, low1, y), out_ref, 1)

    @pl.when(ahead() == 1)
    def _():
        fill_tiles(pos_ref, row_ref, part_high, part_low, own_quads()[1:], 0, LANES, 0, 4)
        clear_own(part_high, part_low, 0)
        store_products(*products(high3, low3, y), first_ref, 0)
        store_products(*products(part_high, part_low, y[:, 0 : 4 * LANES]), first_ref, 1)


def keep_kernel(pos_ref, y_ref, high2, low2, first_ref, out_ref, row_ref, high_ref, low_ref):
    y = y_ref[...]
    rows = pl.ds(0, LANES)

    @pl.when(ahead() == 1)
    def _():
        high, low = high_ref.at[rows, pl.ds(0, 24 * LANES)], low_ref.at[rows, pl.ds(0, 24 * LANES)]
        fill_tiles(pos_ref, row_ref, high, low, own_quads()[1:], 0, LANES, 4, 16)
        store_products(*products(high, low, y[:, 4 * LANES :]), out_ref, 1)
        out_ref[0] = first_ref[0]
        out_ref[1] += first_ref[1]

    @pl.when((1 - lax.axis_index("zh")) - ahead() == 1)
    def _():
        high, low = high_ref.at[rows], low_ref.at[rows]
        fill_tiles(pos_ref, row_ref, high, low, own_quads()[1:], 0, LANES)
        clear_own(high, low, 0)
        store_products(*products(high, low, y), out_ref, 1)
        store_products(*products(high2, low2, y), out_ref, 0)

    @pl.when(lax.axis_index("zh") == 1)
    def _():
        fill_tiles(pos_ref, row_ref, high_ref, low_ref, own_quads(), 0, 2 * LANES)
        clear_own(high_ref, low_ref, LANES)
        store_products(*products(high_ref, low_ref, y), out_ref, 0)


def finish_kernel(keep_ref, half_ref, core_ref, rest_ref, slab_ref, base_ref, accum_ref, next_ref, acc_ref):
    z = keep_ref[1] + half_ref[1] + core_ref[...]
    shift = z[32:33]
    rate_real = z[16:32] + shift * slab_ref[16:32] + rest_ref[0]
    rate_imag = rest_ref[1] - z[0:16] - shift * slab_ref[0:16]
    for n, rate in enumerate((rate_real, rate_imag)):
        next_ref[n] = base_ref[n] + (0.5 * TIME_STEP) * rate
        acc_ref[n] = accum_ref[n] + (TIME_STEP / 3.0) * rate


def params(mib):
    return pltpu.CompilerParams(vmem_limit_bytes=mib << 20)


def in_hbm(array):
    return pltpu.with_memory_space_constraint(array, pltpu.HBM)


def local(positions, detuning, populations, base, section, accum):
    bf16, f32 = jnp.bfloat16, jnp.float32
    count = positions.shape[1]
    tiles = count // (4 * LANES)
    deep = 2 * tiles * LANES
    hbm, vmem = pl.BlockSpec(memory_space=pltpu.HBM), pl.BlockSpec(memory_space=pltpu.VMEM)
    anywhere = pl.BlockSpec(memory_space=pl.ANY)
    tile = pltpu.VMEM((LANES, deep), bf16)
    token = pltpu.VMEM((8, LANES), f32)
    rows = pltpu.VMEM((3, LANES, LANES), f32)

    def call(kernel, name, out_shape, in_specs, flops, scratch=()):
        return pl.pallas_call(
            kernel,
            out_shape=out_shape,
            in_specs=in_specs,
            out_specs=[vmem] * len(out_shape),
            scratch_shapes=scratch,
            compiler_params=params(6),
            cost_estimate=pl.CostEstimate(flops=flops, bytes_accessed=1 << 20, transcendentals=0),
            name=name,
        )

    def swap(array, axis, mask):
        size = lax.axis_size(axis)
        return lax.ppermute(array, axis, [(i, i ^ mask) for i in range(size)])

    def far_block(n, after):
        kernel = functools.partial(block_kernel, n)
        return call(kernel, "far_block_" + "ab"[n], (tile, tile), [vmem, anywhere], 1 << 24, [rows])(pos, after)

    block, pos, det = call(
        pack_kernel,
        "pack_block",
        (pltpu.VMEM((PART, LANES), f32), pltpu.VMEM(positions.shape, f32), token),
        [hbm] * 4,
        1 << 16,
        [pltpu.SemaphoreType.DMA((6,))],
    )(in_hbm(section), in_hbm(populations.reshape(1, LANES)), in_hbm(positions), in_hbm(detuning.reshape(1, count)))
    one = swap(block, "y", 1)
    near = swap(block, "zl", 1)
    high0, low0 = far_block(0, det)

    both, second = call(
        pair_kernel, "join_pair", (pltpu.VMEM((2, PART, LANES), f32), token), [vmem, vmem, anywhere], 1
    )(block, one, high0)
    two = swap(both, "y", 3)
    high1, low1 = far_block(1, second)

    line, third = call(
        line_kernel, "join_line", (pltpu.VMEM((4, PART, LANES), f32), token), [vmem] * 3 + [anywhere], 1
    )(both, two, near, high1)
    two_hops, three, next_to = [swap(line, "x", mask) for mask in (2, 3, 1)]
    across = [next_to, three, two_hops]
    high3, low3, pair = call(
        ahead_kernel,
        "ahead_block",
        (tile, tile, pltpu.VMEM((2, PART, LANES), f32)),
        [vmem] * 3 + [anywhere],
        1 << 24,
        [rows],
    )(pos, block, near, third)
    pair = swap(pair, "zl", 2)
    high2, low2 = call(
        early_kernel, "early_block", (tile, tile), [vmem, anywhere], 1 << 24, [rows]
    )(pos, high3)

    sent, y, first = call(
        send_kernel,
        "send_products",
        (
            pltpu.VMEM((2, PART, LANES), f32),
            pltpu.VMEM((LANES, deep // 2), bf16),
            pltpu.VMEM((2, PART, LANES), f32),
        ),
        [vmem] * 11,
        1 << 29,
        [rows, pltpu.VMEM((LANES, 8 * LANES), bf16), pltpu.VMEM((LANES, 8 * LANES), bf16)],
    )(high0, low0, high1, low1, high3, low3, pos, line, *across)
    half = swap(sent, "zh", 1)

    wide = pltpu.VMEM((2 * LANES, deep), bf16)
    (keep,) = call(
        keep_kernel,
        "keep_products",
        (pltpu.VMEM((2, PART, LANES), f32),),
        [vmem] * 5,
        1 << 29,
        [pltpu.VMEM((3, 2 * LANES, LANES), f32), wide, wide],
    )(pos, y, high2, low2, first)
    core = lax.ppermute(keep[0] + half[0], "c", [(0, 1), (1, 0)])
    rest = pl.pallas_call(
        term_kernel,
        out_shape=pltpu.VMEM((2, 16, LANES), f32),
        in_specs=[vmem] * 5,
        out_specs=vmem,
        scratch_shapes=[pltpu.VMEM((3, LANES, LANES), f32), pltpu.VMEM((2, 64, LANES), f32)],
        compiler_params=params(4),
        cost_estimate=pl.CostEstimate(flops=1 << 22, bytes_accessed=1 << 18, transcendentals=1 << 11),
        name="slab_term",
    )(pos, block, near, pair, det)

    return pl.pallas_call(
        finish_kernel,
        out_shape=(jax.ShapeDtypeStruct(base.shape, f32),) * 2,
        compiler_params=params(4),
        cost_estimate=pl.CostEstimate(flops=1 << 16, bytes_accessed=1 << 18, transcendentals=0),
        name="finish_rate",
    )(keep, half, core, rest, block, base, accum)


def solution(mesh):
    fine = Mesh(mesh.devices.reshape(4, 4, 2, 2, 4), ("y", "x", "zh", "c", "zl"))
    rows = ("y", "x", "zh", "c")
    slab = P(None, "zl", rows)
    return jax.shard_map(
        local,
        mesh=fine,
        in_specs=(P(), P(), P(rows), slab, slab, slab),
        out_specs=(slab, slab),
        check_vma=False,
    )
```

```python
import functools
import math

import jax
import jax.numpy as jnp
from jax import lax
from jax.experimental import pallas as pl
from jax.experimental.pallas import tpu as pltpu
from jax.sharding import Mesh
from jax.sharding import PartitionSpec as P

TIME_STEP = 0.2
LANES = 128
COS = (0.9999992211, -19.73898242, 64.92872338, -85.27236068, 58.79387231, -21.07651549)
SIN = (6.283182817, -41.3414213, 81.59618177, -76.58008122, 41.20531753, -12.27114973)
SCALE = -0.75 / (2.0 * math.pi)
INV_WAVE = 1.0 / (2.0 * math.pi)
ROUNDER = 12582912.0
PART = 40
WIDE = 48


def horner(coefs, scale, arg):
    total = jnp.float32(coefs[-1] * scale)
    for c in coefs[-2::-1]:
        total = total * arg + jnp.float32(c * scale)
    return total


def coupling(dx, dy, dz):
    dz_sq = dz * dz
    dist_sq = dx * dx + dy * dy + dz_sq
    inv = lax.rsqrt(dist_sq)
    dist = dist_sq * inv
    turn = dist - ((dist + ROUNDER) - ROUNDER)
    turn_sq = turn * turn
    cosine = horner(COS, SCALE, turn_sq)
    sine = horner(SIN, SCALE, turn_sq) * turn
    inv_sq = inv * inv
    aligned = dz_sq * inv_sq
    quad_imag = inv_sq * (INV_WAVE - (3.0 * INV_WAVE) * aligned)
    quad_real = inv * ((1.0 - aligned) - INV_WAVE * quad_imag)
    return cosine * quad_real - sine * quad_imag, sine * quad_real + cosine * quad_imag


def split(value):
    high = value.astype(jnp.bfloat16)
    low = (value - high.astype(jnp.float32)).astype(jnp.bfloat16)
    return high, low


def lanes_at(index):
    return pl.ds(pl.multiple_of(index * LANES, LANES), LANES)


def place_of(step):
    down, across = lax.rem(step, 4), lax.div(step, 4)
    y = lax.axis_index("y") ^ down ^ lax.div(down, 2)
    x = lax.axis_index("x") ^ across ^ lax.div(across, 2)
    return y * 4 + x


def own_place():
    return lax.axis_index("y") * 4 + lax.axis_index("x")


def pack_kernel(section_ref, pops_ref, pos_ref, det_ref, block_ref, pos_out, det_out, sems):
    own = own_place() * 4 + lax.axis_index("zh") * 2 + lax.axis_index("c")
    moves = [
        pltpu.make_async_copy(section_ref.at[0], block_ref.at[pl.ds(0, 16)], sems.at[0]),
        pltpu.make_async_copy(section_ref.at[1], block_ref.at[pl.ds(16, 16)], sems.at[1]),
        pltpu.make_async_copy(pops_ref, block_ref.at[pl.ds(32, 1)], sems.at[2]),
        pltpu.make_async_copy(pos_ref, pos_out, sems.at[3]),
        pltpu.make_async_copy(det_ref.at[:, lanes_at(own)], det_out.at[pl.ds(0, 1)], sems.at[4]),
        pltpu.make_async_copy(det_ref.at[:, pl.ds(0, LANES)], det_out.at[pl.ds(1, 1)], sems.at[5]),
    ]
    for move in moves:
        move.start()
    for move in moves:
        move.wait()
    top = lax.broadcasted_iota(jnp.int32, (8, LANES), 0) == 0
    block_ref[32:PART, :] = jnp.where(top, 2.0 * block_ref[32:PART, :] - 1.0, 0.0)


def pair_kernel(block_ref, one_ref, after_ref, both_ref, token_ref):
    both_ref[0] = block_ref[...]
    both_ref[1] = one_ref[...]
    token_ref[...] = block_ref[0:8, :]


def line_kernel(both_ref, two_ref, near_ref, after_ref, all_ref, token_ref):
    all_ref[0:2] = both_ref[...]
    all_ref[2:4] = two_ref[...]
    token_ref[...] = both_ref[0, 0:8, :]


def turned(pos_ref, k, index):
    line = pos_ref[k : k + 1, lanes_at(index)]
    return jnp.broadcast_to(line, (LANES, LANES)).T


def fill_tiles(pos_ref, row_ref, high_ref, low_ref, quads, first, count, begin=0, end=16):
    quad = lax.axis_index("zh") * 2 + lax.axis_index("c")
    place = own_place()
    for n, other in enumerate(quads):
        for k in range(3):
            row_ref[k, n * LANES : (n + 1) * LANES, :] = turned(pos_ref, k, place * 4 + other)

    together = 4 * LANES // count

    def tile(group, carry):
        for step in [group * together + n for n in range(together)]:
            at = lanes_at(place_of(step) * 4 + quad)
            cols = [pos_ref[k : k + 1, at] for k in range(3)]
            for n in range(0, count, 32):
                dx, dy, dz = [row_ref[k, first + n : first + n + 32, :] - cols[k] for k in range(3)]
                for part, value in enumerate(coupling(dx, dy, dz)):
                    high, low = split(value)
                    lanes = lanes_at(step - begin + part * (end - begin))
                    high_ref[n : n + 32, lanes] = high
                    low_ref[n : n + 32, lanes] = low
        return carry

    lax.fori_loop(begin // together, end // together, tile, 0)


def term_kernel(pos_ref, slab_ref, near_ref, pair_ref, det_ref, rest_ref, row_ref, full_ref):
    own = lax.axis_index("zl")
    start = pl.multiple_of(own * 16, 16)
    offsets = []
    for k in range(3):
        row_ref[k] = turned(pos_ref, k, 0)
        offsets.append(row_ref[k, pl.ds(start, 16), :] - pos_ref[k : k + 1, 0:LANES])
    w_real, w_imag = coupling(*offsets)
    eye = (lax.broadcasted_iota(jnp.int32, (16, LANES), 0) + start) == lax.broadcasted_iota(jnp.int32, (16, LANES), 1)
    w_real = jnp.where(eye, det_ref[1:2, :], w_real)[:, 0:64]
    w_imag = jnp.where(eye, -0.5, w_imag)[:, 0:64]
    for n, ref in enumerate((slab_ref, near_ref, pair_ref.at[0], pair_ref.at[1])):
        place = own + (n % 2) * (1 - 2 * (own % 2))
        place = place + (n // 2) * (2 - 4 * (own // 2))
        there = pl.ds(pl.multiple_of(place * 16, 16), 16)
        full_ref[0, there, :] = ref[0:16]
        full_ref[1, there, :] = ref[16:32]

    def mul(a, b):
        return jnp.dot(a, b, precision=lax.Precision.HIGHEST, preferred_element_type=jnp.float32)

    v_real = mul(w_real, full_ref[0]) + mul(w_imag, full_ref[1])
    v_imag = mul(w_real, full_ref[1]) - mul(w_imag, full_ref[0])
    y_real, y_imag = slab_ref[0:16], slab_ref[16:32]
    line = det_ref[0:1, :]
    rest_ref[0] = line * y_imag - 0.5 * y_real - v_imag
    rest_ref[1] = v_real - line * y_real - 0.5 * y_imag


def clear_own(high_ref, low_ref, first):
    eye = lax.broadcasted_iota(jnp.int32, (LANES, LANES), 0) == lax.broadcasted_iota(jnp.int32, (LANES, LANES), 1)
    half = high_ref.shape[1] // 2
    for part in range(2):
        lanes = pl.ds(part * half, LANES)
        for ref in (high_ref, low_ref):
            own = ref[first : first + LANES, lanes].astype(jnp.float32)
            ref[first : first + LANES, lanes] = jnp.where(eye, 0.0, own).astype(jnp.bfloat16)


def own_quads():
    half, core = lax.axis_index("zh"), lax.axis_index("c")
    return half * 2 + 1 - core, half * 2 + core


def block_kernel(far, pos_ref, token_ref, high_ref, low_ref, row_ref):
    half, core = lax.axis_index("zh"), lax.axis_index("c")
    quad = (1 - half) * 2 + (core if far else 1 - core)
    fill_tiles(pos_ref, row_ref, high_ref, low_ref, (quad,), 0, LANES)


def ahead():
    return (1 - lax.axis_index("zh")) * (lax.axis_index("zl") < 2).astype(jnp.int32)


def ahead_kernel(pos_ref, slab_ref, near_ref, token_ref, high_ref, low_ref, pair_ref, row_ref):
    pair_ref[0] = slab_ref[...]
    pair_ref[1] = near_ref[...]

    @pl.when(ahead() == 1)
    def _():
        fill_tiles(pos_ref, row_ref, high_ref, low_ref, own_quads()[:1], 0, LANES)


def early_kernel(pos_ref, token_ref, high_ref, low_ref, row_ref):
    @pl.when((1 - lax.axis_index("zh")) - ahead() == 1)
    def _():
        fill_tiles(pos_ref, row_ref, high_ref, low_ref, own_quads()[:1], 0, LANES)


def fill_slab(refs, y_ref):
    zeros = jnp.zeros((16, LANES), jnp.float32)
    for step in range(16):
        block = refs[step // 4][step % 4]
        pops = jnp.concatenate([block[32:40], zeros[0:8]], axis=0)
        lanes = slice(step * LANES, (step + 1) * LANES)
        for n, value in enumerate((block[0:16], block[16:32], pops)):
            high, low = split(value)
            y_ref[n * 16 : n * 16 + 16, lanes] = high
            y_ref[WIDE + n * 16 : WIDE + n * 16 + 16, lanes] = low
        y_ref[2 * WIDE :, lanes] = jnp.zeros((LANES - 2 * WIDE, LANES), jnp.bfloat16)


def dot_slab(tiles, y):
    return lax.dot_general(tiles, y, (((1,), (1,)), ((), ())), preferred_element_type=jnp.float32)


def store_products(by_real, by_imag, out_ref, at):
    for n in range(by_real.shape[0] // LANES):
        rows = slice(n * LANES, (n + 1) * LANES)
        real, imag = by_real[rows, :].T, by_imag[rows, :].T
        real = real[0:PART] + real[WIDE : WIDE + PART]
        imag = imag[0:32] + imag[WIDE : WIDE + 32]
        out_ref[at + n, 0:16, :] = real[0:16] - imag[16:32]
        out_ref[at + n, 16:32, :] = real[16:32] + imag[0:16]
        out_ref[at + n, 32:PART, :] = real[32:PART]


def products(high_ref, low_ref, y):
    half = high_ref.shape[1] // 2
    by_real = dot_slab(high_ref[:, 0:half], y) + dot_slab(low_ref[:, 0:half], y)
    by_imag = dot_slab(high_ref[:, half:], y) + dot_slab(low_ref[:, half:], y)
    return by_real, by_imag


def send_kernel(high0, low0, high1, low1, high3, low3, pos_ref, all0, all3, all2, all1, out_ref, y_ref, first_ref, row_ref, part_high, part_low):
    fill_slab((all0, all1, all2, all3), y_ref)
    y = y_ref[...]
    store_products(*products(high0, low0, y), out_ref, 0)
    store_products(*products(high1, low1, y), out_ref, 1)

    @pl.when(ahead() == 1)
    def _():
        fill_tiles(pos_ref, row_ref, part_high, part_low, own_quads()[1:], 0, LANES, 0, 4)
        clear_own(part_high, part_low, 0)
        store_products(*products(high3, low3, y), first_ref, 0)
        store_products(*products(part_high, part_low, y[:, 0 : 4 * LANES]), first_ref, 1)


def keep_kernel(pos_ref, y_ref, high2, low2, first_ref, out_ref, row_ref, high_ref, low_ref):
    y = y_ref[...]
    rows = pl.ds(0, LANES)

    @pl.when(ahead() == 1)
    def _():
        high, low = high_ref.at[rows, pl.ds(0, 24 * LANES)], low_ref.at[rows, pl.ds(0, 24 * LANES)]
        fill_tiles(pos_ref, row_ref, high, low, own_quads()[1:], 0, LANES, 4, 16)
        store_products(*products(high, low, y[:, 4 * LANES :]), out_ref, 1)
        out_ref[0] = first_ref[0]
        out_ref[1] += first_ref[1]

    @pl.when((1 - lax.axis_index("zh")) - ahead() == 1)
    def _():
        high, low = high_ref.at[rows], low_ref.at[rows]
        fill_tiles(pos_ref, row_ref, high, low, own_quads()[1:], 0, LANES)
        clear_own(high, low, 0)
        store_products(*products(high, low, y), out_ref, 1)
        store_products(*products(high2, low2, y), out_ref, 0)

    @pl.when(lax.axis_index("zh") == 1)
    def _():
        fill_tiles(pos_ref, row_ref, high_ref, low_ref, own_quads(), 0, 2 * LANES)
        clear_own(high_ref, low_ref, LANES)
        store_products(*products(high_ref, low_ref, y), out_ref, 0)


def finish_kernel(keep_ref, half_ref, core_ref, rest_ref, slab_ref, base_ref, accum_ref, next_ref, acc_ref):
    z = keep_ref[1] + half_ref[1] + core_ref[...]
    shift = z[32:33]
    rate_real = z[16:32] + shift * slab_ref[16:32] + rest_ref[0]
    rate_imag = rest_ref[1] - z[0:16] - shift * slab_ref[0:16]
    for n, rate in enumerate((rate_real, rate_imag)):
        next_ref[n] = base_ref[n] + (0.5 * TIME_STEP) * rate
        acc_ref[n] = accum_ref[n] + (TIME_STEP / 3.0) * rate


def params(mib):
    return pltpu.CompilerParams(vmem_limit_bytes=mib << 20)


def in_hbm(array):
    return pltpu.with_memory_space_constraint(array, pltpu.HBM)


def local(positions, detuning, populations, base, section, accum):
    bf16, f32 = jnp.bfloat16, jnp.float32
    count = positions.shape[1]
    tiles = count // (4 * LANES)
    deep = 2 * tiles * LANES
    hbm, vmem = pl.BlockSpec(memory_space=pltpu.HBM), pl.BlockSpec(memory_space=pltpu.VMEM)
    anywhere = pl.BlockSpec(memory_space=pl.ANY)
    tile = pltpu.VMEM((LANES, deep), bf16)
    token = pltpu.VMEM((8, LANES), f32)
    rows = pltpu.VMEM((3, LANES, LANES), f32)

    def call(kernel, name, out_shape, in_specs, flops, scratch=()):
        return pl.pallas_call(
            kernel,
            out_shape=out_shape,
            in_specs=in_specs,
            out_specs=[vmem] * len(out_shape),
            scratch_shapes=scratch,
            compiler_params=params(6),
            cost_estimate=pl.CostEstimate(flops=flops, bytes_accessed=1 << 20, transcendentals=0),
            name=name,
        )

    def swap(array, axis, mask):
        size = lax.axis_size(axis)
        return lax.ppermute(array, axis, [(i, i ^ mask) for i in range(size)])

    def far_block(n, after):
        kernel = functools.partial(block_kernel, n)
        return call(kernel, "far_block_" + "ab"[n], (tile, tile), [vmem, anywhere], 1 << 24, [rows])(pos, after)

    block, pos, det = call(
        pack_kernel,
        "pack_block",
        (pltpu.VMEM((PART, LANES), f32), pltpu.VMEM(positions.shape, f32), token),
        [hbm] * 4,
        1 << 16,
        [pltpu.SemaphoreType.DMA((6,))],
    )(in_hbm(section), in_hbm(populations.reshape(1, LANES)), in_hbm(positions), in_hbm(detuning.reshape(1, count)))
    one = swap(block, "y", 1)
    near = swap(block, "zl", 1)
    high0, low0 = far_block(0, det)

    both, second = call(
        pair_kernel, "join_pair", (pltpu.VMEM((2, PART, LANES), f32), token), [vmem, vmem, anywhere], 1
    )(block, one, high0)
    two = swap(both, "y", 3)
    high1, low1 = far_block(1, second)

    line, third = call(
        line_kernel, "join_line", (pltpu.VMEM((4, PART, LANES), f32), token), [vmem] * 3 + [anywhere], 1
    )(both, two, near, high1)
    two_hops, three, next_to = [swap(line, "x", mask) for mask in (2, 3, 1)]
    across = [two_hops, three, next_to]
    high3, low3, pair = call(
        ahead_kernel,
        "ahead_block",
        (tile, tile, pltpu.VMEM((2, PART, LANES), f32)),
        [vmem] * 3 + [anywhere],
        1 << 24,
        [rows],
    )(pos, block, near, third)
    pair = swap(pair, "zl", 2)
    high2, low2 = call(
        early_kernel, "early_block", (tile, tile), [vmem, anywhere], 1 << 24, [rows]
    )(pos, high3)

    sent, y, first = call(
        send_kernel,
        "send_products",
        (
            pltpu.VMEM((2, PART, LANES), f32),
            pltpu.VMEM((LANES, deep // 2), bf16),
            pltpu.VMEM((2, PART, LANES), f32),
        ),
        [vmem] * 11,
        1 << 29,
        [rows, pltpu.VMEM((LANES, 8 * LANES), bf16), pltpu.VMEM((LANES, 8 * LANES), bf16)],
    )(high0, low0, high1, low1, high3, low3, pos, line, *across)
    half = swap(sent, "zh", 1)

    wide = pltpu.VMEM((2 * LANES, deep), bf16)
    (keep,) = call(
        keep_kernel,
        "keep_products",
        (pltpu.VMEM((2, PART, LANES), f32),),
        [vmem] * 5,
        1 << 29,
        [pltpu.VMEM((3, 2 * LANES, LANES), f32), wide, wide],
    )(pos, y, high2, low2, first)
    core = lax.ppermute(keep[0] + half[0], "c", [(0, 1), (1, 0)])
    rest = pl.pallas_call(
        term_kernel,
        out_shape=pltpu.VMEM((2, 16, LANES), f32),
        in_specs=[vmem] * 5,
        out_specs=vmem,
        scratch_shapes=[pltpu.VMEM((3, LANES, LANES), f32), pltpu.VMEM((2, 64, LANES), f32)],
        compiler_params=params(4),
        cost_estimate=pl.CostEstimate(flops=1 << 22, bytes_accessed=1 << 18, transcendentals=1 << 11),
        name="slab_term",
    )(pos, block, near, pair, det)

    return pl.pallas_call(
        finish_kernel,
        out_shape=(jax.ShapeDtypeStruct(base.shape, f32),) * 2,
        compiler_params=params(4),
        cost_estimate=pl.CostEstimate(flops=1 << 16, bytes_accessed=1 << 18, transcendentals=0),
        name="finish_rate",
    )(keep, half, core, rest, block, base, accum)


def solution(mesh):
    fine = Mesh(mesh.devices.reshape(4, 4, 2, 2, 4), ("y", "x", "zh", "c", "zl"))
    rows = ("y", "x", "zh", "c")
    slab = P(None, "zl", rows)
    return jax.shard_map(
        local,
        mesh=fine,
        in_specs=(P(), P(), P(rows), slab, slab, slab),
        out_specs=(slab, slab),
        check_vma=False,
    )
```
